32 devices in a mesh: groups: 2 (over y), seq: 8 (over z, x), head: 1, sub: 2 (over core).
Axes of the slice: x: 2, y: 2, z: 4, core: 2. Of those that a mesh axis runs over, the one named last changes fastest.
Arguments:
- queries: bfloat16 [8, 32768, 512], P('head', ('groups', 'seq', 'sub')), parts along dimension 1, may hold values from -6 to 6
- keys: bfloat16 [8, 32768, 512], P('head', ('groups', 'seq', 'sub')), parts along dimension 1, may hold values from -6 to 6
- values: bfloat16 [8, 32768, 512], P('head', ('groups', 'seq', 'sub')), parts along dimension 1, may hold values from -6 to 6
- lr_codes: int32 [8, 32768], P('head', ('groups', 'seq', 'sub')), parts along dimension 1, may hold values from 0 to 15
- fast_gate: float32 [8, 512, 512], P('head', ('seq', 'sub')), may hold values from -0.25 to 0.25
- fast_up: float32 [8, 512, 512], P('head', ('seq', 'sub')), may hold values from -0.25 to 0.25
- fast_down: float32 [8, 512, 512], P('head', ('seq', 'sub')), may hold values from -0.25 to 0.25
Outputs:
- fast_out: bfloat16 [8, 32768, 512], P('head', ('groups', 'seq', 'sub')), parts along dimension 1
The draws below stay inside these ranges and needn't reach their ends.
There are 2 independent parts, one for each index of `groups`. The reference program is written for one: setup_inputs(seed, part) draws one part's arguments, and reference() takes and returns one part's arrays. A program takes and returns all parts, laid end to end along the dimension named above; an argument that names none is the same for every part. Nothing has to cross between parts.
All inputs are finite; a program needn't handle non-finite values.
Results may differ from the reference program's by a relative error of at most 0.0085.
Values may be sent and summed in bfloat16 or wider, within the bound.
No kernel may reach another device: no remote copies, remote signals or barrier semaphores. Data moves between devices by JAX's collectives and lax.ppermute only.
A program may use at most 192 MiB of HBM per device.

```python
import jax
import jax.numpy as jnp
from jax import lax

HEADS = 8
FD = 512
FH = 512
BLOCK = 16384


def plant(entries, key, smallest, largest):
    longest = entries.shape.index(max(entries.shape))
    spots = []
    for shift in (0, 1):
        where = [jax.random.randint(jax.random.fold_in(key, axis), (), 0, length) for axis, length in enumerate(entries.shape)]
        where[longest] = (where[longest] + shift) % entries.shape[longest]
        spots.append(tuple(where))
    return entries.at[spots[0]].set(smallest).at[spots[1]].set(largest)


def raised(drawn, key, source, target, blocks, factor):
    owner, partner = [(jnp.arange(drawn.shape[dim]) // (drawn.shape[dim] // blocks)).reshape([-1 if axis == dim else 1 for axis in range(drawn.ndim)]) for dim in (source, target)]
    chosen = jax.random.permutation(key, blocks)[partner]
    strong = (owner == chosen) | (owner == (partner + blocks // 2) % blocks)
    return jnp.where(strong, factor * drawn, drawn)


def block_levels(stream_key, dims, cuts, smallest, top_value):
    def one(position, blocks):
        draws = jax.random.uniform(jax.random.fold_in(jax.random.fold_in(stream_key, 6), position), (blocks,), jnp.float32, smallest / len(cuts), top_value / len(cuts))
        return jnp.repeat(jnp.exp(draws), dims[position] // blocks).reshape((-1,) + (1,) * (len(dims) - position - 1))

    loudness = one(*cuts[0])
    for cut in cuts[1:]:
        loudness = loudness * one(*cut)
    return loudness


def scatter_about(stream_key, extent, scale, limit, pieces=(), kind=jnp.bfloat16):
    result = scale * jax.random.normal(stream_key, extent, jnp.float32)
    if pieces:
        result = result * block_levels(stream_key, extent, pieces, -0.22, 0.18)
    return jnp.clip(result, -limit, limit).astype(kind)


def bell_draw_with(rng, shape, width, limit, pieces, heavy, held_as=jnp.bfloat16):
    array = width * jax.random.normal(rng, shape, jnp.float32)
    if pieces:
        array = array * block_levels(rng, shape, pieces, -0.22, 0.18)
    return jnp.clip(raised(array, jax.random.fold_in(rng, 3), *heavy), -limit, limit).astype(held_as)


def setup_inputs(seed: int = 0, part: int = 0) -> dict:
    arg_keys = jax.random.split(jax.random.key(seed), 8)
    part_keys = jax.random.split(jax.random.fold_in(arg_keys[7], part), 8)
    return {
        "queries": scatter_about(part_keys[0], (HEADS, BLOCK, FD), 1.0, 6.0, ((1, 16),)),
        "keys": bell_draw_with(part_keys[1], (HEADS, BLOCK, FD), 1.0, 6.0, ((1, 16),), (1, 2, 16, 2.0)),
        "values": scatter_about(part_keys[2], (HEADS, BLOCK, FD), 1.0, 6.0, ((1, 16),)),
        "lr_codes": plant(jax.random.randint(part_keys[3], (HEADS, BLOCK), 0, 16), jax.random.fold_in(part_keys[3], 1), 0, 15).astype(jnp.int32),
        "fast_gate": scatter_about(arg_keys[4], (HEADS, FD, FH), FD ** -0.5, 0.25, ((1, 16),), jnp.float32),
        "fast_up": scatter_about(arg_keys[5], (HEADS, FD, FH), FD ** -0.5, 0.25, ((1, 16),), jnp.float32),
        "fast_down": scatter_about(arg_keys[6], (HEADS, FH, FD), FH ** -0.5, 0.25, ((1, 16),), jnp.float32),
    }


EPSILON = 1e-06
STEP_SIZE = 0.5

def renew(weight, grad):
    scale = STEP_SIZE * jnp.sqrt(jnp.sum(weight * weight) + EPSILON) / jnp.sqrt(jnp.sum(grad * grad) + EPSILON)
    moved = weight - scale * grad
    ratio = jnp.sqrt((lax.optimization_barrier(jnp.sum(weight * weight, axis=0)) + EPSILON) / (lax.optimization_barrier(jnp.sum(moved * moved, axis=0)) + EPSILON))
    return moved * ratio[None, :]

def one_head(operands):
    queries, keys, values, codes, gate_w, up_w, down_w = operands
    gate_b = gate_w.astype(jnp.bfloat16)
    up_b = up_w.astype(jnp.bfloat16)
    down_b = down_w.astype(jnp.bfloat16)
    gate_pre = jnp.dot(keys, gate_b, preferred_element_type=jnp.float32)
    up_pre = jnp.dot(keys, up_b, preferred_element_type=jnp.float32)
    sigmoid_gate = jax.nn.sigmoid(gate_pre)
    hidden = (gate_pre * sigmoid_gate * up_pre).astype(jnp.bfloat16)
    token_rates = (codes.astype(jnp.float32) + 1.0) / 16.0
    target = (-token_rates[:, None] * values.astype(jnp.float32)).astype(jnp.bfloat16)
    back = jnp.dot(target, down_b.T, preferred_element_type=jnp.float32)
    grad_gate_pre = (back * up_pre * sigmoid_gate * (1.0 + gate_pre * (1.0 - sigmoid_gate))).astype(jnp.bfloat16)
    grad_up_pre = (back * gate_pre * sigmoid_gate).astype(jnp.bfloat16)
    grad_gate = jnp.dot(keys.T, grad_gate_pre, preferred_element_type=jnp.float32)
    grad_up = jnp.dot(keys.T, grad_up_pre, preferred_element_type=jnp.float32)
    grad_down = jnp.dot(hidden.T, target, preferred_element_type=jnp.float32)
    new_gate = renew(gate_w, grad_gate).astype(jnp.bfloat16)
    new_up = renew(up_w, grad_up).astype(jnp.bfloat16)
    new_down = renew(down_w, grad_down).astype(jnp.bfloat16)
    query_gate = jnp.dot(queries, new_gate, preferred_element_type=jnp.float32)
    query_up = jnp.dot(queries, new_up, preferred_element_type=jnp.float32)
    query_hidden = (jax.nn.silu(query_gate) * query_up).astype(jnp.bfloat16)
    return jnp.dot(query_hidden, new_down, preferred_element_type=jnp.float32).astype(jnp.bfloat16)

def reference(queries, keys, values, lr_codes, fast_gate, fast_up, fast_down):
    return lax.map(one_head, (queries, keys, values, lr_codes, fast_gate, fast_up, fast_down))
```

```python
import functools

import jax
import jax.numpy as jnp
from jax import lax
from jax.experimental import pallas as pl
from jax.experimental.pallas import tpu as pltpu
from jax.sharding import PartitionSpec as P

EPSILON = 1e-06
STEP_SIZE = 0.5
BF16 = jnp.bfloat16
F32 = jnp.float32
VMEM_LIMIT = 56 * 1024 * 1024


def column_squares(matrix):
    return jnp.sum(matrix * matrix, axis=1)


def rescale(moved, col_weight, col_moved):
    return moved * jnp.sqrt((col_weight + EPSILON) / (col_moved + EPSILON))[:, None, :]


def step_scale(col_weight, grad_total):
    return (
        STEP_SIZE * jnp.sqrt(jnp.sum(col_weight, axis=1) + EPSILON) / jnp.sqrt(grad_total + EPSILON)
    )


def apply_fast(queries, gate_b, up_b, down_b):
    query_gate = jnp.einsum("htd,hdf->htf", queries, gate_b, preferred_element_type=jnp.float32)
    query_up = jnp.einsum("htd,hdf->htf", queries, up_b, preferred_element_type=jnp.float32)
    query_hidden = (jax.nn.silu(query_gate) * query_up).astype(jnp.bfloat16)
    return jnp.einsum(
        "htf,hfd->htd", query_hidden, down_b, preferred_element_type=jnp.float32
    ).astype(jnp.bfloat16)


def local_grads(keys, target, gate_b, up_b, down_b):
    gate_pre = jnp.einsum("htd,hdf->htf", keys, gate_b, preferred_element_type=jnp.float32)
    up_pre = jnp.einsum("htd,hdf->htf", keys, up_b, preferred_element_type=jnp.float32)
    sigmoid_gate = jax.nn.sigmoid(gate_pre)
    hidden = (gate_pre * sigmoid_gate * up_pre).astype(jnp.bfloat16)
    back = jnp.einsum("htd,hfd->htf", target, down_b, preferred_element_type=jnp.float32)
    grad_gate_pre = (back * up_pre * sigmoid_gate * (1.0 + gate_pre * (1.0 - sigmoid_gate))).astype(
        jnp.bfloat16
    )
    grad_up_pre = (back * gate_pre * sigmoid_gate).astype(jnp.bfloat16)
    grad_gate = jnp.einsum("htd,htf->hdf", keys, grad_gate_pre, preferred_element_type=jnp.float32)
    grad_up = jnp.einsum("htd,htf->hdf", keys, grad_up_pre, preferred_element_type=jnp.float32)
    grad_down = jnp.einsum("htf,htd->hfd", hidden, target, preferred_element_type=jnp.float32)
    return (grad_gate, grad_up, grad_down)


def on_device_generic(queries, keys, values, lr_codes, fast_gate, fast_up, fast_down):
    token_rates = (lr_codes.astype(jnp.float32) + 1.0) / 16.0
    target = (-token_rates[:, :, None] * values.astype(jnp.float32)).astype(jnp.bfloat16)
    gate_b, up_b, down_b = (
        lax.all_gather(fast_gate.astype(jnp.bfloat16), ("seq", "sub"), axis=1, tiled=True),
        lax.all_gather(fast_up.astype(jnp.bfloat16), ("seq", "sub"), axis=1, tiled=True),
        lax.all_gather(fast_down.astype(jnp.bfloat16), ("seq", "sub"), axis=1, tiled=True),
    )
    grad_gate, grad_up, grad_down = local_grads(keys, target, gate_b, up_b, down_b)
    owned = (
        lax.psum_scatter(grad_gate, ("seq", "sub"), scatter_dimension=1, tiled=True),
        lax.psum_scatter(grad_up, ("seq", "sub"), scatter_dimension=1, tiled=True),
        lax.psum_scatter(grad_down, ("seq", "sub"), scatter_dimension=1, tiled=True),
    )
    weights = (fast_gate, fast_up, fast_down)
    grad_local = jnp.stack(
        [
            jnp.sum(owned[0] * owned[0], axis=(1, 2)),
            jnp.sum(owned[1] * owned[1], axis=(1, 2)),
            jnp.sum(owned[2] * owned[2], axis=(1, 2)),
        ],
        axis=1,
    )
    col_gate, col_up, col_down, grad_totals = lax.psum(
        (column_squares(fast_gate), column_squares(fast_up), column_squares(fast_down), grad_local),
        ("seq", "sub"),
    )
    col_weights = (col_gate, col_up, col_down)
    moved_all = []
    for index in range(3):
        scale = step_scale(col_weights[index], grad_totals[:, index])
        moved_all.append(weights[index] - scale[:, None, None] * owned[index])
    moved_cols = lax.psum(
        (column_squares(moved_all[0]), column_squares(moved_all[1]), column_squares(moved_all[2])),
        ("seq", "sub"),
    )
    renewed = [
        rescale(moved_all[index], col_weights[index], moved_cols[index]).astype(jnp.bfloat16)
        for index in range(3)
    ]
    new_gate, new_up, new_down = (
        lax.all_gather(renewed[0], ("seq", "sub"), axis=1, tiled=True),
        lax.all_gather(renewed[1], ("seq", "sub"), axis=1, tiled=True),
        lax.all_gather(renewed[2], ("seq", "sub"), axis=1, tiled=True),
    )
    return apply_fast(queries, new_gate, new_up, new_down)


def block(shape, index_map):
    return pl.BlockSpec(shape, index_map)


def whole(array):
    return pl.BlockSpec(array.shape, lambda *_: (0,) * array.ndim)


def anywhere():
    return pl.BlockSpec(memory_space=pl.ANY)


def call(body, name, positions, grid, operands, in_specs, out_shapes, out_specs, scratch=(), aliases=None, cost=None):
    return pl.pallas_call(
        body,
        name=name,
        out_shape=out_shapes,
        grid_spec=pltpu.PrefetchScalarGridSpec(
            num_scalar_prefetch=1,
            grid=grid,
            in_specs=in_specs,
            out_specs=out_specs,
            scratch_shapes=list(scratch),
        ),
        input_output_aliases=aliases or {},
        compiler_params=pltpu.CompilerParams(vmem_limit_bytes=VMEM_LIMIT),
        cost_estimate=cost,
    )(positions, *operands)


def sds(shape, dtype):
    return jax.ShapeDtypeStruct(shape, dtype)


def rounded_rows(positions, weights, half):
    _, rows, columns = weights[0].shape

    def body(pos, *refs):
        for i in range(3):
            refs[6][0, i] = refs[i][0].astype(BF16)
            refs[7][0, i] = refs[3 + i][0].astype(BF16)

    mine = block((1, rows, columns), lambda s, pos: (pos[0] * half + s, 0, 0))
    other = block((1, rows, columns), lambda s, pos: ((1 - pos[0]) * half + s, 0, 0))
    out = block((1, 3, rows, columns), lambda s, pos: (s, 0, 0, 0))
    shape = sds((half, 3, rows, columns), BF16)
    return call(body, "rounded_rows", positions, (half,), (*weights, *weights), [mine] * 3 + [other] * 3, [shape] * 2, [out] * 2)


def first_piece(positions, own, received, stage, after):
    _, _, rows, columns = own.shape
    width = columns // 2

    def body(pos, own_ref, received_ref, *rest):
        out_ref = rest[-1]
        mine = pl.ds(pl.multiple_of(pos[0] * rows, rows), rows)
        theirs = pl.ds(pl.multiple_of((1 - pos[0]) * rows, rows), rows)
        out_ref[:, mine, :] = own_ref[0]
        out_ref[:, theirs, :] = received_ref[0]

    spec = block((1, 3, rows, width), lambda i, pos: (stage, 0, 0, pos[3]))
    shape = sds((3, 2 * rows, width), BF16)
    return call(body, "first_piece", positions, (1,), (own, received, *after), [spec, spec] + [anywhere()] * len(after), shape, whole(shape))


def gradients(positions, keys, keys_in, target, target_in, pieces, stage, half, tile):
    z_size, _, piece_rows, width = pieces[0].shape
    rows, columns = z_size * 2 * piece_rows, 2 * width
    quarter = rows // z_size
    tokens = keys.shape[1]
    steps = tokens // tile

    def body(pos, k0, k1, t0, t1, p0, p1, p2, p3, keep, send, own_w, squares, w, total):
        step = pl.program_id(0)
        z, x, y = pos[1], pos[2], pos[3]
        mine = pl.ds(pl.multiple_of(x * width, 128), width)
        theirs = pl.ds(pl.multiple_of((1 - x) * width, 128), width)

        @pl.when(step == 0)
        def _():
            for i, (ref, xx, yy) in enumerate(((p0, x, y), (p1, 1 - x, y), (p2, x, 1 - y), (p3, 1 - x, 1 - y))):
                cols = pl.ds(pl.multiple_of(yy * width, 128), width)
                for j in range(z_size):
                    at = pl.ds(pl.multiple_of((z ^ j) * quarter + xx * piece_rows, piece_rows), piece_rows)
                    w[:, at, cols] = ref[j]
            own_w[...] = w[:, pl.ds(pl.multiple_of(z * quarter, quarter), quarter), mine]
            for m in range(3):
                full = w[m].astype(F32)
                squares[m : m + 1, :] = jnp.sum(full * full, axis=0, keepdims=True)

        for n, (k_ref, t_ref) in enumerate(((k0, t0), (k1, t1))):
            k, t = k_ref[0], t_ref[0]
            gate = jnp.dot(k, w[0], preferred_element_type=F32)
            up = jnp.dot(k, w[1], preferred_element_type=F32)
            back = lax.dot_general(t, w[2], (((1,), (1,)), ((), ())), preferred_element_type=F32)
            sig = 0.5 * jnp.tanh(0.5 * gate) + 0.5
            silu = gate * sig
            hidden = (silu * up).astype(BF16)
            grad_up = (back * silu).astype(BF16)
            grad_gate = (back * up * (sig + silu * (1.0 - sig))).astype(BF16)
            for m, (a, b) in enumerate(((k, grad_gate), (k, grad_up), (hidden, t))):
                part = lax.dot_general(a, b, (((0,), (0,)), ((), ())), preferred_element_type=F32)
                if n == 0:
                    @pl.when(step == 0)
                    def _(m=m, part=part):
                        total[m] = part

                    @pl.when(step > 0)
                    def _(m=m, part=part):
                        total[m] += part
                else:
                    total[m] += part

        @pl.when(step == steps - 1)
        def _():
            keep[...] = total[:, :, mine]
            send[...] = total[:, :, theirs].astype(BF16)

    here = block((1, tile, columns), lambda i, pos: (pos[0] * half + stage, i, 0))
    there = block((1, tile, columns), lambda i, pos: (stage, i, 0))
    outs = [sds((3, rows, width), F32), sds((3, rows, width), BF16), sds((3, quarter, width), BF16), sds((8, columns), F32)]
    flops = 6 * 2 * 2 * tokens * rows * columns
    return call(
        body, "gradients", positions, (steps,),
        (keys, keys_in, target, target_in, *pieces),
        [here, there, here, there] + [whole(p) for p in pieces],
        outs, [whole(o) for o in outs],
        [pltpu.VMEM((3, rows, columns), BF16), pltpu.VMEM((3, rows, columns), F32)],
        cost=pl.CostEstimate(flops=flops, bytes_accessed=14 * 2**20, transcendentals=2 * tokens * columns),
    )


def add_halves(positions, keep, received, z_size):
    _, rows, width = keep.shape
    quarter = rows // z_size

    def body(pos, keep_ref, received_ref, own, *sends):
        for j in range(z_size):
            at = pl.ds(pl.multiple_of((pos[1] ^ j) * quarter, quarter), quarter)
            added = keep_ref[:, at, :] + received_ref[:, at, :].astype(F32)
            if j == 0:
                own[...] = added
            else:
                sends[j - 1][...] = added.astype(BF16)

    outs = [sds((3, quarter, width), F32)] + [sds((3, quarter, width), BF16)] * (z_size - 1)
    return call(body, "add_halves", positions, (1,), (keep, received), [whole(keep), whole(received)], outs, [whole(o) for o in outs])


def column_sums(positions, own, received, own_w):
    def body(pos, own_ref, *refs):
        parts, w_ref, grad, sums = refs[:-3], refs[-3], refs[-2], refs[-1]
        sums[...] = jnp.zeros_like(sums)
        for m in range(3):
            g = own_ref[m]
            for part in parts:
                g = g + part[m].astype(F32)
            grad[m] = g
            sums[m : m + 1, :] = jnp.sum(g * g, axis=0, keepdims=True)
            sums[3 + m : 4 + m, :] = jnp.sum(g * w_ref[m].astype(F32), axis=0, keepdims=True)

    outs = [sds(own.shape, F32), sds((8, own.shape[2]), F32)]
    operands = (own, *received, own_w)
    return call(body, "column_sums", positions, (1,), operands, [whole(a) for a in operands], outs, [whole(o) for o in outs])


def renewed_block(positions, grad, own_w, squares, sums, others):
    width = grad.shape[2]

    def body(pos, g_ref, w_ref, sq_ref, sums_ref, *refs):
        out = refs[-1]
        here = sums_ref[...]
        there = jnp.zeros_like(here)
        for i, ref in enumerate(refs[:-1]):
            if i % 2:
                here = here + ref[...]
            else:
                there = there + ref[...]
        mine = pl.ds(pl.multiple_of(pos[2] * width, 128), width)
        for m in range(3):
            total_g = jnp.sum(here[m : m + 1] + there[m : m + 1], axis=1, keepdims=True)
            total_w = jnp.sum(sq_ref[m : m + 1, :], axis=1, keepdims=True)
            scale = STEP_SIZE * jnp.sqrt(total_w + EPSILON) / jnp.sqrt(total_g + EPSILON)
            col_w = sq_ref[m : m + 1, mine]
            col_moved = col_w - 2.0 * scale * here[3 + m : 4 + m] + scale * scale * here[m : m + 1]
            ratio = jnp.sqrt((col_w + EPSILON) / (jnp.maximum(col_moved, 0.0) + EPSILON))
            out[m] = ((w_ref[m].astype(F32) - scale * g_ref[m]) * ratio).astype(BF16)

    operands = (grad, own_w, squares, sums, *others)
    shape = sds(grad.shape, BF16)
    return call(body, "renewed_block", positions, (1,), operands, [whole(a) for a in operands], shape, whole(shape))


def apply_renewed(positions, queries, queries_in, held, swapped, stage, half, tile, out, late):
    z_size, _, quarter, width = held.shape
    rows, columns = z_size * quarter, 2 * width
    heads, tokens, _ = queries.shape
    steps = tokens // tile
    n_late = 0 if late is None else 1
    n_out = 0 if out is None else 1

    def body(pos, q0, q1, h_ref, s_ref, *refs):
        w = refs[-1]
        send_ref, out_refs = refs[-2], refs[n_late + n_out : -2]
        z, x = pos[1], pos[2]

        @pl.when(pl.program_id(0) == 0)
        def _():
            for ref, xx in ((h_ref, x), (s_ref, 1 - x)):
                cols = pl.ds(pl.multiple_of(xx * width, 128), width)
                for j in range(z_size):
                    at = pl.ds(pl.multiple_of((z ^ j) * quarter, quarter), quarter)
                    w[:, at, cols] = ref[j]

        for q_ref, is_own in ((q0, True), (q1, False)):
            q = q_ref[0]
            gate = jnp.dot(q, w[0], preferred_element_type=F32)
            up = jnp.dot(q, w[1], preferred_element_type=F32)
            hidden = (gate * (0.5 * jnp.tanh(0.5 * gate) + 0.5) * up).astype(BF16)
            result = jnp.dot(hidden, w[2], preferred_element_type=F32).astype(BF16)
            if is_own:
                out_refs[0][0] = result
            else:
                send_ref[...] = result

    mine = lambda i, pos: (pos[0] * half + stage, i, 0)
    here = block((1, tile, columns), mine)
    there = block((1, tile, columns), lambda i, pos: (stage, i, 0))
    operands = [queries, queries_in, held, swapped]
    in_specs = [here, there, whole(held), whole(swapped)]
    aliases = {}
    if out is not None:
        aliases = {1 + len(operands): 0}
        operands.append(out)
        in_specs.append(anywhere())
    return call(
        body, "apply_renewed", positions, (steps,), operands, in_specs,
        [sds(queries.shape, BF16), sds((tokens, columns), BF16)],
        [block((1, tile, columns), mine), block((tile, columns), lambda i, pos: (i, 0))],
        [pltpu.VMEM((3, rows, columns), BF16)],
        aliases,
        pl.CostEstimate(flops=3 * 2 * 2 * tokens * rows * columns, bytes_accessed=7 * 2**20, transcendentals=2 * tokens * columns),
    )


def place(positions, out, received, stage, half):
    def body(pos, received_ref, _, out_ref):
        out_ref[0] = received_ref[...]

    tokens, columns = received.shape
    spec = block((1, tokens, columns), lambda i, pos: ((1 - pos[0]) * half + stage, 0, 0))
    return call(body, "place", positions, (1,), (received, out), [whole(received), anywhere()], sds(out.shape, BF16), spec, aliases={2: 0})


def on_device_fast(z_size, queries, keys, values, lr_codes, fast_gate, fast_up, fast_down):
    heads, tokens, _ = queries.shape
    half = heads // 2
    seq_size = 2 * z_size
    core, seq = lax.axis_index("sub"), lax.axis_index("seq")
    positions = jnp.stack([core, seq // 2, seq % 2, lax.axis_index("groups")]).astype(jnp.int32)
    flip = [(0, 1), (1, 0)]
    tile = 512 if tokens % 512 == 0 else tokens

    def over_sub(a):
        return lax.ppermute(a, "sub", flip)

    def over_groups(a):
        return lax.ppermute(a, "groups", flip)

    def over_seq(a, bits):
        return lax.ppermute(a, "seq", [(i, i ^ bits) for i in range(seq_size)])

    def other_half(a):
        return lax.dynamic_slice_in_dim(a, (1 - core) * half, half, axis=0)

    own_rows, sent_rows = rounded_rows(positions, (fast_gate, fast_up, fast_down), half)
    received_rows = over_sub(sent_rows)
    token_rates = (lr_codes.astype(F32) + 1.0) / 16.0
    target = (-token_rates[:, :, None] * values.astype(F32)).astype(BF16)
    keys_in, target_in, queries_in = (over_sub(other_half(a)) for a in (keys, target, queries))

    pieces, after = [], ()
    for stage in range(half):
        piece = first_piece(positions, own_rows, received_rows, stage, after)
        after = tuple(over_seq(piece, 2 * j) for j in range(1, z_size))
        held = jnp.stack((piece, *after))
        swapped = over_seq(held, 1)
        pieces.append((held, swapped, over_groups(held), over_groups(swapped)))

    out, late = None, None
    for stage in range(half):
        keep, send, own_w, squares = gradients(
            positions, keys, keys_in, target, target_in, pieces[stage], stage, half, tile
        )
        own, *sends = add_halves(positions, keep, over_seq(send, 1), z_size)
        received = [over_seq(a, 2 * (j + 1)) for j, a in enumerate(sends)]
        grad, sums = column_sums(positions, own, received, own_w)
        others = [over_seq(sums, bits) for bits in range(1, seq_size)]
        renewed = renewed_block(positions, grad, own_w, squares, sums, others)
        held = jnp.stack([renewed] + [over_seq(renewed, 2 * j) for j in range(1, z_size)])
        out, sent = apply_renewed(
            positions, queries, queries_in, held, over_seq(held, 1), stage, half, tile, out, None
        )
        late = late or []
        late.append(over_sub(sent))
    for stage in range(half):
        out = place(positions, out, late[stage], stage, half)
    return out


def solution(mesh):
    seq, sub, groups = mesh.shape["seq"], mesh.shape["sub"], mesh.shape["groups"]

    def on_device(queries, *rest):
        fits = sub == 2 and groups == 2 and seq in (4, 8, 16) and queries.shape[0] % 2 == 0 and rest[3].shape[1] * seq * sub == 512
        if fits:
            return on_device_fast(seq // 2, queries, *rest)
        return on_device_generic(queries, *rest)

    return jax.shard_map(
        on_device,
        mesh=mesh,
        in_specs=(
            P("head", ("groups", "seq", "sub"), None),
            P("head", ("groups", "seq", "sub"), None),
            P("head", ("groups", "seq", "sub"), None),
            P("head", ("groups", "seq", "sub")),
            P("head", ("seq", "sub"), None),
            P("head", ("seq", "sub"), None),
            P("head", ("seq", "sub"), None),
        ),
        out_specs=P("head", ("groups", "seq", "sub"), None),
        check_vma=False,
    )
```

```python
import functools

import jax
import jax.numpy as jnp
from jax import lax
from jax.experimental import pallas as pl
from jax.experimental.pallas import tpu as pltpu
from jax.sharding import PartitionSpec as P

EPSILON = 1e-06
STEP_SIZE = 0.5
BF16 = jnp.bfloat16
F32 = jnp.float32
VMEM_LIMIT = 56 * 1024 * 1024


def column_squares(matrix):
    return jnp.sum(matrix * matrix, axis=1)


def rescale(moved, col_weight, col_moved):
    return moved * jnp.sqrt((col_weight + EPSILON) / (col_moved + EPSILON))[:, None, :]


def step_scale(col_weight, grad_total):
    return (
        STEP_SIZE * jnp.sqrt(jnp.sum(col_weight, axis=1) + EPSILON) / jnp.sqrt(grad_total + EPSILON)
    )


def apply_fast(queries, gate_b, up_b, down_b):
    query_gate = jnp.einsum("htd,hdf->htf", queries, gate_b, preferred_element_type=jnp.float32)
    query_up = jnp.einsum("htd,hdf->htf", queries, up_b, preferred_element_type=jnp.float32)
    query_hidden = (jax.nn.silu(query_gate) * query_up).astype(jnp.bfloat16)
    return jnp.einsum(
        "htf,hfd->htd", query_hidden, down_b, preferred_element_type=jnp.float32
    ).astype(jnp.bfloat16)


def local_grads(keys, target, gate_b, up_b, down_b):
    gate_pre = jnp.einsum("htd,hdf->htf", keys, gate_b, preferred_element_type=jnp.float32)
    up_pre = jnp.einsum("htd,hdf->htf", keys, up_b, preferred_element_type=jnp.float32)
    sigmoid_gate = jax.nn.sigmoid(gate_pre)
    hidden = (gate_pre * sigmoid_gate * up_pre).astype(jnp.bfloat16)
    back = jnp.einsum("htd,hfd->htf", target, down_b, preferred_element_type=jnp.float32)
    grad_gate_pre = (back * up_pre * sigmoid_gate * (1.0 + gate_pre * (1.0 - sigmoid_gate))).astype(
        jnp.bfloat16
    )
    grad_up_pre = (back * gate_pre * sigmoid_gate).astype(jnp.bfloat16)
    grad_gate = jnp.einsum("htd,htf->hdf", keys, grad_gate_pre, preferred_element_type=jnp.float32)
    grad_up = jnp.einsum("htd,htf->hdf", keys, grad_up_pre, preferred_element_type=jnp.float32)
    grad_down = jnp.einsum("htf,htd->hfd", hidden, target, preferred_element_type=jnp.float32)
    return (grad_gate, grad_up, grad_down)


def on_device_generic(queries, keys, values, lr_codes, fast_gate, fast_up, fast_down):
    token_rates = (lr_codes.astype(jnp.float32) + 1.0) / 16.0
    target = (-token_rates[:, :, None] * values.astype(jnp.float32)).astype(jnp.bfloat16)
    gate_b, up_b, down_b = (
        lax.all_gather(fast_gate.astype(jnp.bfloat16), ("seq", "sub"), axis=1, tiled=True),
        lax.all_gather(fast_up.astype(jnp.bfloat16), ("seq", "sub"), axis=1, tiled=True),
        lax.all_gather(fast_down.astype(jnp.bfloat16), ("seq", "sub"), axis=1, tiled=True),
    )
    grad_gate, grad_up, grad_down = local_grads(keys, target, gate_b, up_b, down_b)
    owned = (
        lax.psum_scatter(grad_gate, ("seq", "sub"), scatter_dimension=1, tiled=True),
        lax.psum_scatter(grad_up, ("seq", "sub"), scatter_dimension=1, tiled=True),
        lax.psum_scatter(grad_down, ("seq", "sub"), scatter_dimension=1, tiled=True),
    )
    weights = (fast_gate, fast_up, fast_down)
    grad_local = jnp.stack(
        [
            jnp.sum(owned[0] * owned[0], axis=(1, 2)),
            jnp.sum(owned[1] * owned[1], axis=(1, 2)),
            jnp.sum(owned[2] * owned[2], axis=(1, 2)),
        ],
        axis=1,
    )
    col_gate, col_up, col_down, grad_totals = lax.psum(
        (column_squares(fast_gate), column_squares(fast_up), column_squares(fast_down), grad_local),
        ("seq", "sub"),
    )
    col_weights = (col_gate, col_up, col_down)
    moved_all = []
    for index in range(3):
        scale = step_scale(col_weights[index], grad_totals[:, index])
        moved_all.append(weights[index] - scale[:, None, None] * owned[index])
    moved_cols = lax.psum(
        (column_squares(moved_all[0]), column_squares(moved_all[1]), column_squares(moved_all[2])),
        ("seq", "sub"),
    )
    renewed = [
        rescale(moved_all[index], col_weights[index], moved_cols[index]).astype(jnp.bfloat16)
        for index in range(3)
    ]
    new_gate, new_up, new_down = (
        lax.all_gather(renewed[0], ("seq", "sub"), axis=1, tiled=True),
        lax.all_gather(renewed[1], ("seq", "sub"), axis=1, tiled=True),
        lax.all_gather(renewed[2], ("seq", "sub"), axis=1, tiled=True),
    )
    return apply_fast(queries, new_gate, new_up, new_down)


CHUNKS = ((3,), (2,), (1, 0))


def block(shape, index_map):
    return pl.BlockSpec(shape, index_map)


def whole(array):
    return pl.BlockSpec(array.shape, lambda *_: (0,) * array.ndim)


def anywhere():
    return pl.BlockSpec(memory_space=pl.ANY)


def call(body, name, positions, grid, operands, in_specs, out_shapes, out_specs, scratch=(), aliases=None, cost=None):
    return pl.pallas_call(
        body,
        name=name,
        out_shape=out_shapes,
        grid_spec=pltpu.PrefetchScalarGridSpec(
            num_scalar_prefetch=1,
            grid=grid,
            in_specs=in_specs,
            out_specs=out_specs,
            scratch_shapes=list(scratch),
        ),
        input_output_aliases=aliases or {},
        compiler_params=pltpu.CompilerParams(vmem_limit_bytes=VMEM_LIMIT),
        cost_estimate=cost,
    )(positions, *operands)


def sds(shape, dtype):
    return jax.ShapeDtypeStruct(shape, dtype)


def first_pieces(positions, own, received, chunk, after):
    heads, rows, columns = own[0].shape
    half, width = heads // 2, columns // 2

    def body(pos, *refs):
        mine = pl.ds(pl.multiple_of(pos[0] * rows, rows), rows)
        theirs = pl.ds(pl.multiple_of((1 - pos[0]) * rows, rows), rows)
        for j, out_ref in enumerate(refs[-half:]):
            for i, k in enumerate(chunk):
                head = pos[1] ^ (j ^ k)
                for m in range(3):
                    out_ref[i, m, mine, :] = refs[m][head].astype(BF16)
                    out_ref[i, m, theirs, :] = refs[3 + m][head].astype(BF16)

    spec = block((half, rows, width), lambda i, pos: (pos[0], 0, pos[3]))
    shape = sds((len(chunk), 3, 2 * rows, width), BF16)
    return call(
        body, "first_pieces", positions, (1,), (*own, *received, *after),
        [spec] * 6 + [anywhere()] * len(after), [shape] * half, [whole(shape)] * half,
    )


def gradients(positions, keys, values, rates, pieces, place_in_chunk, k, half, tile, after):
    z_size, _, _, piece_rows, width = pieces[0].shape
    rows, columns = z_size * 2 * piece_rows, 2 * width
    tokens = keys[0].shape[1]
    lanes = rates[0].shape[2]
    steps = tokens // tile
    last = k == 0

    def body(pos, k0, k1, v0, v1, r0, r1, p0, p1, p2, p3, *rest):
        keep, send = rest[len(after) : len(after) + 2]
        w, total = rest[-2:]
        step = pl.program_id(0)
        z, x, y = pos[1], pos[2], pos[3]
        mine = pl.ds(pl.multiple_of(x * width, 128), width)
        theirs = pl.ds(pl.multiple_of((1 - x) * width, 128), width)

        @pl.when(step == 0)
        def _():
            for ref, xx, yy in ((p0, x, y), (p1, 1 - x, y), (p2, x, 1 - y), (p3, 1 - x, 1 - y)):
                cols = pl.ds(pl.multiple_of(yy * width, 128), width)
                for j in range(z_size):
                    at = pl.ds(pl.multiple_of((z ^ j) * 2 * piece_rows + xx * piece_rows, piece_rows), piece_rows)
                    w[:, at, cols] = ref[j, 0]
            if last:
                own_w, squares = rest[len(after) + 2 : len(after) + 4]
                own_w[...] = w[:, :, mine]
                for m in range(3):
                    full = w[m].astype(F32)
                    squares[m : m + 1, :] = jnp.sum(full * full, axis=0, keepdims=True)

        for n, (k_ref, v_ref, r_ref) in enumerate(((k0, v0, r0), (k1, v1, r1))):
            key = k_ref[0]
            rate = jnp.concatenate([r_ref[0].astype(F32)] * (columns // lanes), axis=1)
            t = (-rate * v_ref[0].astype(F32)).astype(BF16)
            gate = jnp.dot(key, w[0], preferred_element_type=F32)
            up = jnp.dot(key, w[1], preferred_element_type=F32)
            back = lax.dot_general(t, w[2], (((1,), (1,)), ((), ())), preferred_element_type=F32)
            sig = 0.5 * jnp.tanh(0.5 * gate) + 0.5
            silu = gate * sig
            hidden = (silu * up).astype(BF16)
            grad_up = (back * silu).astype(BF16)
            grad_gate = (back * up * (sig + silu * (1.0 - sig))).astype(BF16)
            for m, (a, b) in enumerate(((key, grad_gate), (key, grad_up), (hidden, t))):
                part = lax.dot_general(a, b, (((0,), (0,)), ((), ())), preferred_element_type=F32)
                if n == 0:
                    @pl.when(step == 0)
                    def _(m=m, part=part):
                        total[m] = part

                    @pl.when(step > 0)
                    def _(m=m, part=part):
                        total[m] += part
                else:
                    total[m] += part

        @pl.when(step == steps - 1)
        def _():
            keep[...] = total[:, :, mine]
            send[...] = total[:, :, theirs].astype(BF16)

    at = lambda i, pos: (pos[0] * half + (pos[1] ^ k), i, 0)
    rows_of, rates_of = block((1, tile, columns), at), block((1, tile, lanes), at)
    piece = block((z_size, 1, 3, piece_rows, width), lambda i, pos: (0, place_in_chunk, 0, 0, 0))
    outs = [sds((3, rows, width), F32), sds((3, rows, width), BF16)]
    if last:
        outs += [sds((3, rows, width), BF16), sds((8, columns), F32)]
    return call(
        body, "gradients", positions, (steps,),
        (*keys, *values, *rates, *pieces, *after),
        [rows_of] * 4 + [rates_of] * 2 + [piece] * 4 + [anywhere()] * len(after),
        outs, [whole(o) for o in outs],
        [pltpu.VMEM((3, rows, columns), BF16), pltpu.VMEM((3, rows, columns), F32)],
        cost=pl.CostEstimate(flops=6 * 2 * 2 * tokens * rows * columns, bytes_accessed=14 * 2**20, transcendentals=2 * tokens * columns),
    )


def added(positions, keep, received, after):
    def body(pos, keep_ref, *refs):
        for m in range(3):
            total = keep_ref[m]
            for ref in refs[: len(received)]:
                total = total + ref[m].astype(F32)
            refs[-1][m] = total.astype(BF16)

    operands = (keep, *received)
    shape = sds(keep.shape, BF16)
    specs = [whole(a) for a in operands] + [anywhere()] * len(after)
    return call(body, "added", positions, (1,), (*operands, *after), specs, shape, whole(shape))


def total_gradient(positions, keep, received):
    def body(pos, keep_ref, *refs):
        grad, sums = refs[-2:]
        sums[...] = jnp.zeros_like(sums)
        for m in range(3):
            total = keep_ref[m]
            for ref in refs[:-2]:
                total = total + ref[m].astype(F32)
            grad[m] = total
            columns = jnp.sum(total * total, axis=0, keepdims=True)
            sums[m : m + 1, :] = jnp.broadcast_to(jnp.sum(columns, axis=1, keepdims=True), (1, sums.shape[1]))

    outs = [sds(keep.shape, F32), sds((8, 128), F32)]
    operands = (keep, *received)
    return call(body, "total_gradient", positions, (1,), operands, [whole(a) for a in operands], outs, [whole(o) for o in outs])


def renewed_block(positions, grad, own_w, squares, sums, sums_in):
    width = grad.shape[2]

    def body(pos, g_ref, w_ref, sq_ref, sums_ref, sums_in_ref, out):
        mine = pl.ds(pl.multiple_of(pos[2] * width, 128), width)
        for m in range(3):
            total_g = sums_ref[m : m + 1, :1] + sums_in_ref[m : m + 1, :1]
            total_w = jnp.sum(sq_ref[m : m + 1, :], axis=1, keepdims=True)
            scale = STEP_SIZE * jnp.sqrt(total_w + EPSILON) / jnp.sqrt(total_g + EPSILON)
            moved = w_ref[m].astype(F32) - scale * g_ref[m]
            col_moved = jnp.sum(moved * moved, axis=0, keepdims=True)
            out[m] = (moved * jnp.sqrt((sq_ref[m : m + 1, mine] + EPSILON) / (col_moved + EPSILON))).astype(BF16)

    operands = (grad, own_w, squares, sums, sums_in)
    shape = sds(grad.shape, BF16)
    return call(body, "renewed_block", positions, (1,), operands, [whole(a) for a in operands], shape, whole(shape))


def apply_renewed(positions, queries, queries_in, held, swapped, k, half, tile, out):
    _, rows, width = held.shape
    columns = 2 * width
    heads, tokens, _ = queries.shape
    steps = tokens // tile

    def body(pos, q0, q1, h_ref, s_ref, *refs):
        out_ref, send_ref, w = refs[-3:]
        x = pos[2]

        @pl.when(pl.program_id(0) == 0)
        def _():
            w[:, :, pl.ds(pl.multiple_of(x * width, 128), width)] = h_ref[...]
            w[:, :, pl.ds(pl.multiple_of((1 - x) * width, 128), width)] = s_ref[...]

        for q_ref, is_own in ((q0, True), (q1, False)):
            q = q_ref[0]
            gate = jnp.dot(q, w[0], preferred_element_type=F32)
            up = jnp.dot(q, w[1], preferred_element_type=F32)
            hidden = (gate * (0.5 * jnp.tanh(0.5 * gate) + 0.5) * up).astype(BF16)
            result = jnp.dot(hidden, w[2], preferred_element_type=F32).astype(BF16)
            if is_own:
                out_ref[0] = result
            else:
                send_ref[...] = result

    here = block((1, tile, columns), lambda i, pos: (pos[0] * half + (pos[1] ^ k), i, 0))
    operands = [queries, queries_in, held, swapped]
    in_specs = [here, here, whole(held), whole(swapped)]
    aliases = {}
    if out is not None:
        aliases = {1 + len(operands): 0}
        operands.append(out)
        in_specs.append(anywhere())
    return call(
        body, "apply_renewed", positions, (steps,), operands, in_specs,
        [sds(queries.shape, BF16), sds((tokens, columns), BF16)],
        [here, block((tile, columns), lambda i, pos: (i, 0))],
        [pltpu.VMEM((3, rows, columns), BF16)],
        aliases,
        pl.CostEstimate(flops=3 * 2 * 2 * tokens * rows * columns, bytes_accessed=7 * 2**20, transcendentals=2 * tokens * columns),
    )


def place(positions, out, received, ks, half):
    tokens, columns = received[0].shape

    def body(pos, *refs):
        for i in range(len(ks)):
            @pl.when(pl.program_id(0) == i)
            def _(i=i):
                refs[-1][0] = refs[i][...]

    def at(i, pos):
        k = ks[0]
        for n, other in enumerate(ks[1:], 1):
            k = jnp.where(i == n, other, k)
        return ((1 - pos[0]) * half + (pos[1] ^ k), 0, 0)

    n = len(ks)
    return call(
        body, "place", positions, (n,), (*received, out), [whole(r) for r in received] + [anywhere()],
        sds(out.shape, BF16), block((1, tokens, columns), at), aliases={1 + n: 0},
    )


def on_device_fast(queries, keys, values, lr_codes, fast_gate, fast_up, fast_down):
    heads, tokens, _ = queries.shape
    half = heads // 2
    core, seq = lax.axis_index("sub"), lax.axis_index("seq")
    positions = jnp.stack([core, seq // 2, seq % 2, lax.axis_index("groups")]).astype(jnp.int32)
    flip = [(0, 1), (1, 0)]
    tile = 512 if tokens % 512 == 0 else tokens

    def over_sub(a):
        return lax.ppermute(a, "sub", flip)

    def over_groups(a):
        return lax.ppermute(a, "groups", flip)

    def over_x(a):
        return lax.ppermute(a, "seq", [(i, i ^ 1) for i in range(8)])

    def over_z(a, j):
        return lax.ppermute(a, "seq", [(i, i ^ (2 * j)) for i in range(8)])

    weights = (fast_gate, fast_up, fast_down)
    rows_in = tuple(over_sub(w) for w in weights)
    all_keys, all_values = (keys, over_sub(keys)), (values, over_sub(values))
    rates = tuple(
        jnp.broadcast_to(((codes.astype(F32) + 1.0) / 16.0).astype(BF16)[:, :, None], (*codes.shape, 128))
        for codes in (lr_codes, over_sub(lr_codes))
    )
    queries_in = over_sub(queries)

    def chunk_pieces(chunk, after):
        own, *sends = first_pieces(positions, weights, rows_in, chunk, after)
        return own, [over_z(a, j) for j, a in enumerate(sends, 1)]

    pieces = {}

    def chunk_spread(chunk, own, received):
        held = jnp.stack((own, *received))
        swapped = over_x(held)
        everything = (held, swapped, over_groups(held), over_groups(swapped))
        for i, k in enumerate(chunk):
            pieces[k] = (everything, i)
        return held

    def head_gradients(k, after):
        keep, send, *rest = gradients(positions, all_keys, all_values, rates, *pieces[k], k, half, tile, after)
        return keep, over_x(send), *rest

    first = chunk_pieces(CHUNKS[0], ())
    second = chunk_pieces(CHUNKS[1], (first[0],))
    held = chunk_spread(CHUNKS[0], *first)
    third = chunk_pieces(CHUNKS[2], (second[0], held))
    held = chunk_spread(CHUNKS[1], *second)
    keep3, in3 = head_gradients(3, (third[0], held))
    held = chunk_spread(CHUNKS[2], *third)
    keep2, in2 = head_gradients(2, (keep3, held))
    sum3 = added(positions, keep3, (in3,), (keep2,))
    from1 = over_z(sum3, 1)
    keep1, in1 = head_gradients(1, (sum3,))
    sum2 = added(positions, keep2, (in2, from1), (keep1,))
    from2 = over_z(sum2, 2)
    keep0, in0, own_w, squares = head_gradients(0, (sum2,))
    from1 = over_z(added(positions, keep1, (in1,), (keep0,)), 1)
    grad, sums = total_gradient(positions, keep0, (in0, from1, from2))
    renewed = renewed_block(positions, grad, own_w, squares, sums, over_x(sums))

    matrices = {0: (renewed, over_x(renewed))}
    from2 = over_z(renewed, 2)
    from3 = over_z(from2, 1)
    matrices[2] = (from2, over_x(from2))
    matrices[1] = (over_z(renewed, 1), over_z(matrices[0][1], 1))
    matrices[3] = (from3, over_x(from3))

    out, returned = None, {}
    for order in ((0, 2), (1, 3)):
        for k in order:
            out, sent = apply_renewed(positions, queries, queries_in, *matrices[k], k, half, tile, out)
            returned[k] = over_sub(sent)
        out = place(positions, out, [returned[k] for k in order], order, half)
    return out


def solution(mesh):
    seq, sub, groups = mesh.shape["seq"], mesh.shape["sub"], mesh.shape["groups"]

    def on_device(queries, *rest):
        rows, columns = rest[3].shape[1:]
        fits = (groups, seq, sub, queries.shape[0]) == (2, 8, 2, 8) and rows % 32 == 0 and columns == seq * sub * rows and columns % 256 == 0
        return (on_device_fast if fits else on_device_generic)(queries, *rest)

    return jax.shard_map(
        on_device,
        mesh=mesh,
        in_specs=(
            P("head", ("groups", "seq", "sub"), None),
            P("head", ("groups", "seq", "sub"), None),
            P("head", ("groups", "seq", "sub"), None),
            P("head", ("groups", "seq", "sub")),
            P("head", ("seq", "sub"), None),
            P("head", ("seq", "sub"), None),
            P("head", ("seq", "sub"), None),
        ),
        out_specs=P("head", ("groups", "seq", "sub"), None),
        check_vma=False,
    )
```

```python
import functools

import jax
import jax.numpy as jnp
from jax import lax
from jax.experimental import pallas as pl
from jax.experimental.pallas import tpu as pltpu
from jax.sharding import PartitionSpec as P

EPSILON = 1e-06
STEP_SIZE = 0.5
BF16 = jnp.bfloat16
F32 = jnp.float32
VMEM_LIMIT = 64 * 1024 * 1024


def column_squares(matrix):
    return jnp.sum(matrix * matrix, axis=1)


def rescale(moved, col_weight, col_moved):
    return moved * jnp.sqrt((col_weight + EPSILON) / (col_moved + EPSILON))[:, None, :]


def step_scale(col_weight, grad_total):
    return (
        STEP_SIZE * jnp.sqrt(jnp.sum(col_weight, axis=1) + EPSILON) / jnp.sqrt(grad_total + EPSILON)
    )


def apply_fast(queries, gate_b, up_b, down_b):
    query_gate = jnp.einsum("htd,hdf->htf", queries, gate_b, preferred_element_type=jnp.float32)
    query_up = jnp.einsum("htd,hdf->htf", queries, up_b, preferred_element_type=jnp.float32)
    query_hidden = (jax.nn.silu(query_gate) * query_up).astype(jnp.bfloat16)
    return jnp.einsum(
        "htf,hfd->htd", query_hidden, down_b, preferred_element_type=jnp.float32
    ).astype(jnp.bfloat16)


def local_grads(keys, target, gate_b, up_b, down_b):
    gate_pre = jnp.einsum("htd,hdf->htf", keys, gate_b, preferred_element_type=jnp.float32)
    up_pre = jnp.einsum("htd,hdf->htf", keys, up_b, preferred_element_type=jnp.float32)
    sigmoid_gate = jax.nn.sigmoid(gate_pre)
    hidden = (gate_pre * sigmoid_gate * up_pre).astype(jnp.bfloat16)
    back = jnp.einsum("htd,hfd->htf", target, down_b, preferred_element_type=jnp.float32)
    grad_gate_pre = (back * up_pre * sigmoid_gate * (1.0 + gate_pre * (1.0 - sigmoid_gate))).astype(
        jnp.bfloat16
    )
    grad_up_pre = (back * gate_pre * sigmoid_gate).astype(jnp.bfloat16)
    grad_gate = jnp.einsum("htd,htf->hdf", keys, grad_gate_pre, preferred_element_type=jnp.float32)
    grad_up = jnp.einsum("htd,htf->hdf", keys, grad_up_pre, preferred_element_type=jnp.float32)
    grad_down = jnp.einsum("htf,htd->hfd", hidden, target, preferred_element_type=jnp.float32)
    return (grad_gate, grad_up, grad_down)


def on_device_generic(queries, keys, values, lr_codes, fast_gate, fast_up, fast_down):
    token_rates = (lr_codes.astype(jnp.float32) + 1.0) / 16.0
    target = (-token_rates[:, :, None] * values.astype(jnp.float32)).astype(jnp.bfloat16)
    gate_b, up_b, down_b = (
        lax.all_gather(fast_gate.astype(jnp.bfloat16), ("seq", "sub"), axis=1, tiled=True),
        lax.all_gather(fast_up.astype(jnp.bfloat16), ("seq", "sub"), axis=1, tiled=True),
        lax.all_gather(fast_down.astype(jnp.bfloat16), ("seq", "sub"), axis=1, tiled=True),
    )
    grad_gate, grad_up, grad_down = local_grads(keys, target, gate_b, up_b, down_b)
    owned = (
        lax.psum_scatter(grad_gate, ("seq", "sub"), scatter_dimension=1, tiled=True),
        lax.psum_scatter(grad_up, ("seq", "sub"), scatter_dimension=1, tiled=True),
        lax.psum_scatter(grad_down, ("seq", "sub"), scatter_dimension=1, tiled=True),
    )
    weights = (fast_gate, fast_up, fast_down)
    grad_local = jnp.stack(
        [
            jnp.sum(owned[0] * owned[0], axis=(1, 2)),
            jnp.sum(owned[1] * owned[1], axis=(1, 2)),
            jnp.sum(owned[2] * owned[2], axis=(1, 2)),
        ],
        axis=1,
    )
    col_gate, col_up, col_down, grad_totals = lax.psum(
        (column_squares(fast_gate), column_squares(fast_up), column_squares(fast_down), grad_local),
        ("seq", "sub"),
    )
    col_weights = (col_gate, col_up, col_down)
    moved_all = []
    for index in range(3):
        scale = step_scale(col_weights[index], grad_totals[:, index])
        moved_all.append(weights[index] - scale[:, None, None] * owned[index])
    moved_cols = lax.psum(
        (column_squares(moved_all[0]), column_squares(moved_all[1]), column_squares(moved_all[2])),
        ("seq", "sub"),
    )
    renewed = [
        rescale(moved_all[index], col_weights[index], moved_cols[index]).astype(jnp.bfloat16)
        for index in range(3)
    ]
    new_gate, new_up, new_down = (
        lax.all_gather(renewed[0], ("seq", "sub"), axis=1, tiled=True),
        lax.all_gather(renewed[1], ("seq", "sub"), axis=1, tiled=True),
        lax.all_gather(renewed[2], ("seq", "sub"), axis=1, tiled=True),
    )
    return apply_fast(queries, new_gate, new_up, new_down)


def block(shape, index_map):
    return pl.BlockSpec(shape, index_map)


def whole(array):
    return pl.BlockSpec(array.shape, lambda *_: (0,) * array.ndim)


def anywhere():
    return pl.BlockSpec(memory_space=pl.ANY)


def call(body, name, positions, grid, operands, in_specs, out_shapes, out_specs, scratch=(), aliases=None, estimate=None, vmem=VMEM_LIMIT):
    return pl.pallas_call(
        body,
        name=name,
        out_shape=out_shapes,
        grid_spec=pltpu.PrefetchScalarGridSpec(
            num_scalar_prefetch=1,
            grid=grid,
            in_specs=in_specs,
            out_specs=out_specs,
            scratch_shapes=list(scratch),
        ),
        input_output_aliases=aliases or {},
        compiler_params=pltpu.CompilerParams(vmem_limit_bytes=vmem),
        cost_estimate=estimate,
    )(positions, *operands)


def sds(shape, dtype):
    return jax.ShapeDtypeStruct(shape, dtype)


def cost(microseconds):
    return pl.CostEstimate(flops=0, bytes_accessed=int(microseconds * 3e6), transcendentals=0)


def first_pieces(positions, own, received, k, after):
    heads, rows, columns = own[0].shape
    half, width = heads // 2, columns // 2

    def body(pos, *refs):
        mine = pl.ds(pl.multiple_of(pos[0] * rows, rows), rows)
        theirs = pl.ds(pl.multiple_of((1 - pos[0]) * rows, rows), rows)
        everything, sends = refs[-half - 1], refs[-half:]
        for head in range(half):
            for m in range(3):
                everything[head, m, mine, :] = refs[m][head].astype(BF16)
                everything[head, m, theirs, :] = refs[3 + m][head].astype(BF16)
        for j, out_ref in enumerate(sends):
            out_ref[...] = everything[pos[1] ^ (j ^ k)]

    spec = block((half, rows, width), lambda i, pos: (pos[0], 0, pos[3]))
    outs = [sds((half, 3, 2 * rows, width), BF16)] + [sds((3, 2 * rows, width), BF16)] * half
    return call(
        body, "first_pieces", positions, (1,), (*own, *received, *after),
        [spec] * 6 + [anywhere()] * len(after), outs, [whole(o) for o in outs], vmem=60 * 1024 * 1024,
    )


def next_pieces(positions, arrived, rows, k, after, handed=None):
    half = len(arrived)
    more = [] if k is None else list(rows)

    passed = [] if handed is None else [handed]

    def body(pos, *refs):
        held, *sends = refs[half + len(more) + len(after) + len(passed) :]
        for j in range(half):
            held[j] = refs[j][...]
        if more:
            height = rows[0].shape[2]
            for ref, x in ((refs[half], pos[2]), (refs[half + 1], 1 - pos[2])):
                at = pl.ds(pl.multiple_of(x * height, height), height)
                for j in range(half):
                    sends[j][:, at, :] = ref[pos[1] ^ (j ^ k)]

    outs = [sds((half, *arrived[0].shape), BF16)]
    if more:
        outs += [sds((3, 2 * rows[0].shape[2], rows[0].shape[3]), BF16)] * half
    operands = (*arrived, *more)
    others = (*after, *passed)
    aliases = {len(operands) + len(others): len(outs)} if passed else {}
    return call(
        body, "next_pieces", positions, (1,), (*operands, *others),
        [whole(a) for a in operands] + [anywhere()] * len(others),
        outs + [sds(p.shape, p.dtype) for p in passed], [whole(o) for o in outs] + [anywhere() for _ in passed],
        aliases=aliases, estimate=cost(3),
    )


def copied(positions, array, after):
    def body(pos, in_ref, *rest):
        rest[-1][...] = in_ref[...]

    shape = sds(array.shape, BF16)
    return call(body, "copied", positions, (1,), (array, *after), [whole(array)] + [anywhere()] * len(after), shape, whole(shape))


def other_half(positions, array, half, after):
    def body(pos, in_ref, *rest):
        rest[-1][...] = in_ref[...]

    _, tokens, columns = array.shape
    spec = block((1, tokens // 2, columns), lambda i, j, pos: ((1 - pos[0]) * half + i, j, 0))
    out = block((1, tokens // 2, columns), lambda i, j, pos: (i, j, 0))
    return call(
        body, "other_half", positions, (half, 2), (array, *after), [spec] + [anywhere()] * len(after),
        sds((half, tokens, columns), BF16), out, estimate=cost(3),
    )


def gradients(positions, keys, values, rates, pieces, k, half, tile, after, cuts):
    z_size, _, piece_rows, width = pieces[0].shape
    columns = keys[0].shape[2]
    rows = columns
    quarter = rows // z_size
    tokens = keys[0].shape[1]
    lanes = rates[0].shape[2]
    steps = tokens // tile
    last = k == 0

    def body(pos, k0, k1, v0, v1, r0, r1, *rest):
        parts, rest = rest[: len(pieces)], rest[len(pieces) + len(after) :]
        keep, sends = rest[0], rest[1 : 1 + cuts]
        w, total = rest[-2:]
        step = pl.program_id(0)
        z, x, y = pos[1], pos[2], pos[3]
        mine = pl.ds(pl.multiple_of(x * width, 128), width)
        theirs = pl.ds(pl.multiple_of((1 - x) * width, 128), width)

        @pl.when(step == 0)
        def _():
            places = ((0, y), (0, 1 - y)) if len(parts) == 2 else ((x, y), (1 - x, y), (x, 1 - y), (1 - x, 1 - y))
            for ref, (xx, yy) in zip(parts, places):
                cols = pl.ds(pl.multiple_of(yy * width, 128), width)
                for j in range(z_size):
                    at = pl.ds(pl.multiple_of((z ^ j) * quarter + xx * piece_rows, piece_rows), piece_rows)
                    w[:, at, cols] = ref[j]
            if last:
                own_w, squares = rest[1 + cuts : 3 + cuts]
                own_w[...] = w[:, :, mine]
                for m in range(3):
                    full = w[m].astype(F32)
                    squares[m : m + 1, :] = jnp.sum(full * full, axis=0, keepdims=True)

        for n, (k_ref, v_ref, r_ref) in enumerate(((k0, v0, r0), (k1, v1, r1))):
            key = k_ref[0]
            rate = jnp.concatenate([r_ref[0].astype(F32)] * (columns // lanes), axis=1)
            t = (-rate * v_ref[0].astype(F32)).astype(BF16)
            gate = jnp.dot(key, w[0], preferred_element_type=F32)
            up = jnp.dot(key, w[1], preferred_element_type=F32)
            back = lax.dot_general(t, w[2], (((1,), (1,)), ((), ())), preferred_element_type=F32)
            sig = 0.5 * jnp.tanh(0.5 * gate) + 0.5
            silu = gate * sig
            hidden = (silu * up).astype(BF16)
            grad_up = (back * silu).astype(BF16)
            grad_gate = (back * up * (sig + silu * (1.0 - sig))).astype(BF16)
            for m, (a, b) in enumerate(((key, grad_gate), (key, grad_up), (hidden, t))):
                part = lax.dot_general(a, b, (((0,), (0,)), ((), ())), preferred_element_type=F32)
                if n == 0:
                    @pl.when(step == 0)
                    def _(m=m, part=part):
                        total[m] = part

                    @pl.when(step > 0)
                    def _(m=m, part=part):
                        total[m] += part
                else:
                    total[m] += part

        @pl.when(step == steps - 1)
        def _():
            keep[...] = total[:, :, mine]
            for c in range(cuts):
                sends[c][...] = total[:, c * (rows // cuts) : (c + 1) * (rows // cuts), theirs].astype(BF16)

    at = lambda i, pos: (pos[0] * half + (pos[1] ^ k), i, 0)
    rows_of, rates_of = block((1, tile, columns), at), block((1, tile, lanes), at)
    outs = [sds((3, rows, width), F32)] + [sds((3, rows // cuts, width), BF16)] * cuts
    if last:
        outs += [sds((3, rows, width), BF16), sds((8, columns), F32)]
    return call(
        body, "gradients", positions, (steps,),
        (*keys, *values, *rates, *pieces, *after),
        [rows_of] * 4 + [rates_of] * 2 + [whole(p) for p in pieces] + [anywhere()] * len(after),
        outs, [whole(o) for o in outs],
        [pltpu.VMEM((3, rows, columns), BF16), pltpu.VMEM((3, rows, columns), F32)],
        estimate=pl.CostEstimate(flops=6 * 2 * 2 * tokens * rows * columns, bytes_accessed=14 * 2**20, transcendentals=2 * tokens * columns),
    )


def added(positions, keep, received, after, dtype=BF16, microseconds=1, cuts=1):
    rows = keep.shape[1]

    def body(pos, keep_ref, *refs):
        for m in range(3):
            for c in range(cuts):
                at = pl.ds(c * (rows // cuts), rows // cuts)
                total = keep_ref[m, at, :] + refs[c][m].astype(F32)
                for ref in refs[cuts : len(received)]:
                    total = total + ref[m, at, :].astype(F32)
                refs[-1][m, at, :] = total.astype(dtype)

    operands = (keep, *received)
    shape = sds(keep.shape, dtype)
    specs = [whole(a) for a in operands] + [anywhere()] * len(after)
    return call(body, "added", positions, (1,), (*operands, *after), specs, shape, whole(shape), estimate=cost(microseconds))


def total_gradient(positions, keep, received):
    def body(pos, keep_ref, *refs):
        grad, sums = refs[-2:]
        sums[...] = jnp.zeros_like(sums)
        for m in range(3):
            total = keep_ref[m]
            for ref in refs[:-2]:
                total = total + ref[m].astype(F32)
            grad[m] = total
            columns = jnp.sum(total * total, axis=0, keepdims=True)
            sums[m : m + 1, :] = jnp.broadcast_to(jnp.sum(columns, axis=1, keepdims=True), (1, sums.shape[1]))

    outs = [sds(keep.shape, F32), sds((8, 128), F32)]
    operands = (keep, *received)
    return call(body, "total_gradient", positions, (1,), operands, [whole(a) for a in operands], outs, [whole(o) for o in outs])


def renewed_block(positions, grad, own_w, squares, sums, sums_in):
    width = grad.shape[2]

    def body(pos, g_ref, w_ref, sq_ref, sums_ref, sums_in_ref, out):
        mine = pl.ds(pl.multiple_of(pos[2] * width, 128), width)
        for m in range(3):
            total_g = sums_ref[m : m + 1, :1] + sums_in_ref[m : m + 1, :1]
            total_w = jnp.sum(sq_ref[m : m + 1, :], axis=1, keepdims=True)
            scale = STEP_SIZE * jnp.sqrt(total_w + EPSILON) / jnp.sqrt(total_g + EPSILON)
            moved = w_ref[m].astype(F32) - scale * g_ref[m]
            col_moved = jnp.sum(moved * moved, axis=0, keepdims=True)
            out[m] = (moved * jnp.sqrt((sq_ref[m : m + 1, mine] + EPSILON) / (col_moved + EPSILON))).astype(BF16)

    operands = (grad, own_w, squares, sums, sums_in)
    shape = sds(grad.shape, BF16)
    return call(body, "renewed_block", positions, (1,), operands, [whole(a) for a in operands], shape, whole(shape))


def apply_renewed(positions, queries, queries_in, held, swapped, k, half, tile, out, late, after):
    _, rows, width = held.shape
    columns = 2 * width
    heads, tokens, _ = queries.shape
    steps = tokens // tile
    blocks = [b for _, b in late]
    first = len(after) + len(blocks) + (0 if out is None else 1)

    def body(pos, q0, q1, h_ref, s_ref, *refs):
        late_refs = refs[: len(blocks)]
        out_ref, send_ref, w, result, sems, late_sems = refs[first:]
        x, step = pos[2], pl.program_id(0)

        def placed(i):
            head = pos[0] * half + (pos[1] ^ k)
            return pltpu.make_async_copy(result.at[i], out_ref.at[head, pl.ds(i * tile, tile)], sems.at[i])

        def brought(i):
            head = (1 - pos[0]) * half + (pos[1] ^ late[i][0])
            return pltpu.make_async_copy(late_refs[i], out_ref.at[head], late_sems.at[i])

        @pl.when(step == 0)
        def _():
            for i in range(len(blocks)):
                brought(i).start()
            w[:, :, pl.ds(pl.multiple_of(x * width, 128), width)] = h_ref[...]
            w[:, :, pl.ds(pl.multiple_of((1 - x) * width, 128), width)] = s_ref[...]

        for q_ref, is_own in ((q0, True), (q1, False)):
            q = q_ref[0]
            gate = jnp.dot(q, w[0], preferred_element_type=F32)
            up = jnp.dot(q, w[1], preferred_element_type=F32)
            hidden = (gate * (0.5 * jnp.tanh(0.5 * gate) + 0.5) * up).astype(BF16)
            values = jnp.dot(hidden, w[2], preferred_element_type=F32).astype(BF16)
            if is_own:
                for i in range(steps):
                    @pl.when(step == i)
                    def _(i=i, values=values):
                        result[i] = values
                        placed(i).start()
            else:
                send_ref[...] = values

        @pl.when(step == steps - 1)
        def _():
            for i in range(steps):
                placed(i).wait()
            for i in range(len(blocks)):
                brought(i).wait()

    here = block((1, tile, columns), lambda i, pos: (pos[0] * half + (pos[1] ^ k), i, 0))
    there = block((1, tile, columns), lambda i, pos: (pos[1] ^ k, i, 0))
    operands = [queries, queries_in, held, swapped, *blocks, *after]
    in_specs = [here, there, whole(held), whole(swapped)] + [whole(b) for b in blocks] + [anywhere()] * len(after)
    aliases = {}
    if out is not None:
        aliases = {1 + len(operands): 0}
        operands.append(out)
        in_specs.append(anywhere())
    return call(
        body, "apply_renewed", positions, (steps,), operands, in_specs,
        [sds(queries.shape, BF16), sds((tokens, columns), BF16)],
        [anywhere(), block((tile, columns), lambda i, pos: (i, 0))],
        [
            pltpu.VMEM((3, rows, columns), BF16), pltpu.VMEM((steps, tile, columns), BF16),
            pltpu.SemaphoreType.DMA((steps,)), pltpu.SemaphoreType.DMA((max(len(blocks), 1),)),
        ],
        aliases,
        pl.CostEstimate(flops=3 * 2 * 2 * tokens * rows * columns, bytes_accessed=7 * 2**20, transcendentals=2 * tokens * columns),
    )


def place(positions, out, late, half):
    n = len(late)

    def body(pos, *refs):
        out_ref, sems = refs[-2:]
        copies = [
            pltpu.make_async_copy(refs[i], out_ref.at[(1 - pos[0]) * half + (pos[1] ^ k)], sems.at[i])
            for i, (k, _) in enumerate(late)
        ]
        for copy in copies:
            copy.start()
        for copy in copies:
            copy.wait()

    return call(
        body, "place", positions, (1,), (*(b for _, b in late), out), [whole(b) for _, b in late] + [anywhere()],
        sds(out.shape, BF16), anywhere(), [pltpu.SemaphoreType.DMA((n,))], {1 + n: 0}, cost(1),
    )


def on_device_fast(queries, keys, values, lr_codes, fast_gate, fast_up, fast_down):
    heads, tokens, _ = queries.shape
    half = heads // 2
    core, seq = lax.axis_index("sub"), lax.axis_index("seq")
    positions = jnp.stack([core, seq // 2, seq % 2, lax.axis_index("groups")]).astype(jnp.int32)
    flip = [(0, 1), (1, 0)]
    tile = 512 if tokens % 512 == 0 else tokens

    def over_sub(a):
        return lax.ppermute(a, "sub", flip)

    def over_groups(a):
        return lax.ppermute(a, "groups", flip)

    def over_x(a):
        return lax.ppermute(a, "seq", [(i, i ^ 1) for i in range(8)])

    def over_z(a, j):
        return lax.ppermute(a, "seq", [(i, i ^ (2 * j)) for i in range(8)])

    weights = (fast_gate, fast_up, fast_down)
    rows_in = tuple(over_sub(w) for w in weights)
    all_keys, all_values = (keys, over_sub(keys)), (values, over_sub(values))
    rates = tuple(
        jnp.broadcast_to(((codes.astype(F32) + 1.0) / 16.0).astype(BF16)[:, :, None], (*codes.shape, 128))
        for codes in (lr_codes, over_sub(lr_codes))
    )
    def head_gradients(k, pieces, after):
        keep, send, *rest = gradients(positions, all_keys, all_values, rates, pieces, k, half, tile, after, 1)
        return keep, over_x(send), *rest

    def turn(pieces, k, after, handed=None):
        arrived = (pieces[0], *(over_z(a, j) for j, a in enumerate(pieces[1:], 1)))
        return next_pieces(positions, arrived, rows, k, after, handed)

    everything, *pieces = first_pieces(positions, weights, rows_in, 3, ())
    rows = (everything, over_x(everything))
    held, *pieces = turn(pieces, 2, ())
    swapped = over_x(held)
    pieces3 = (held, swapped, over_groups(held), over_groups(swapped))
    sent_queries = other_half(positions, queries, half, (held,))
    queries_in = over_sub(sent_queries)
    held, *pieces = turn(pieces, 1, (*pieces3, sent_queries, *rates))
    pieces2 = (held, over_groups(held))
    keep3, *sends = gradients(positions, all_keys, all_values, rates, pieces3, 3, half, tile, (held,), 4)
    in3 = [over_x(a) for a in sends]
    held, *pieces = turn(pieces, 0, (keep3, pieces2[1]))
    pieces1 = (held, over_groups(held))
    sum3 = added(positions, keep3, in3, (held,), cuts=4)
    from1 = over_z(sum3, 1)
    keep2, in2 = head_gradients(2, pieces2, (sum3,))
    (held,) = turn(pieces, None, (keep2, pieces1[1]))
    pieces0 = (held, over_groups(held))
    keep1, in1 = head_gradients(1, pieces1, (held,))
    sum2 = added(positions, keep2, (in2, from1), (keep1, pieces0[1]))
    from2 = over_z(sum2, 2)
    keep0, in0, own_w, squares = head_gradients(0, pieces0, (sum2,))
    sum1 = added(positions, keep1, (in1,), (keep0,))
    from1 = over_z(sum1, 1)
    partial = added(positions, keep0, (from2,), (sum1,), F32, 8)
    grad, sums = total_gradient(positions, partial, (in0, from1))
    renewed = renewed_block(positions, grad, own_w, squares, sums, over_x(sums))

    swapped = over_x(renewed)
    from1, from2 = over_z(renewed, 1), over_z(renewed, 2)
    from3 = over_z(from2, 1)
    matrices = {0: (renewed, swapped), 2: (from2, over_x(from2)), 3: (from3, over_x(from3))}

    def head_output(k, out, late, after):
        out, sent = apply_renewed(positions, queries, queries_in, *matrices[k], k, half, tile, out, late, after)
        return out, (k, over_sub(sent))

    out, late0 = head_output(0, None, (), (from1, from2))
    swapped_late = copied(positions, swapped, (from3, out))
    matrices[1] = (from1, over_z(swapped_late, 1))
    out, late2 = head_output(2, out, (), (swapped_late,))
    out, late1 = head_output(1, out, (late0,), matrices[3])
    out, late3 = head_output(3, out, (late2,), ())
    return place(positions, out, (late1, late3), half)


def solution(mesh):
    seq, sub, groups = mesh.shape["seq"], mesh.shape["sub"], mesh.shape["groups"]

    def on_device(queries, *rest):
        rows, columns = rest[3].shape[1:]
        fits = (groups, seq, sub, queries.shape[0]) == (2, 8, 2, 8) and rows % 32 == 0 and columns == seq * sub * rows and columns % 256 == 0
        return (on_device_fast if fits else on_device_generic)(queries, *rest)

    return jax.shard_map(
        on_device,
        mesh=mesh,
        in_specs=(
            P("head", ("groups", "seq", "sub"), None),
            P("head", ("groups", "seq", "sub"), None),
            P("head", ("groups", "seq", "sub"), None),
            P("head", ("groups", "seq", "sub")),
            P("head", ("seq", "sub"), None),
            P("head", ("seq", "sub"), None),
            P("head", ("seq", "sub"), None),
        ),
        out_specs=P("head", ("groups", "seq", "sub"), None),
        check_vma=False,
    )
```

```python
import functools

import jax
import jax.numpy as jnp
from jax import lax
from jax.experimental import pallas as pl
from jax.experimental.pallas import tpu as pltpu
from jax.sharding import PartitionSpec as P

EPSILON = 1e-06
STEP_SIZE = 0.5
BF16 = jnp.bfloat16
F32 = jnp.float32
VMEM_LIMIT = 64 * 1024 * 1024


def column_squares(matrix):
    return jnp.sum(matrix * matrix, axis=1)


def rescale(moved, col_weight, col_moved):
    return moved * jnp.sqrt((col_weight + EPSILON) / (col_moved + EPSILON))[:, None, :]


def step_scale(col_weight, grad_total):
    return (
        STEP_SIZE * jnp.sqrt(jnp.sum(col_weight, axis=1) + EPSILON) / jnp.sqrt(grad_total + EPSILON)
    )


def apply_fast(queries, gate_b, up_b, down_b):
    query_gate = jnp.einsum("htd,hdf->htf", queries, gate_b, preferred_element_type=jnp.float32)
    query_up = jnp.einsum("htd,hdf->htf", queries, up_b, preferred_element_type=jnp.float32)
    query_hidden = (jax.nn.silu(query_gate) * query_up).astype(jnp.bfloat16)
    return jnp.einsum(
        "htf,hfd->htd", query_hidden, down_b, preferred_element_type=jnp.float32
    ).astype(jnp.bfloat16)


def local_grads(keys, target, gate_b, up_b, down_b):
    gate_pre = jnp.einsum("htd,hdf->htf", keys, gate_b, preferred_element_type=jnp.float32)
    up_pre = jnp.einsum("htd,hdf->htf", keys, up_b, preferred_element_type=jnp.float32)
    sigmoid_gate = jax.nn.sigmoid(gate_pre)
    hidden = (gate_pre * sigmoid_gate * up_pre).astype(jnp.bfloat16)
    back = jnp.einsum("htd,hfd->htf", target, down_b, preferred_element_type=jnp.float32)
    grad_gate_pre = (back * up_pre * sigmoid_gate * (1.0 + gate_pre * (1.0 - sigmoid_gate))).astype(
        jnp.bfloat16
    )
    grad_up_pre = (back * gate_pre * sigmoid_gate).astype(jnp.bfloat16)
    grad_gate = jnp.einsum("htd,htf->hdf", keys, grad_gate_pre, preferred_element_type=jnp.float32)
    grad_up = jnp.einsum("htd,htf->hdf", keys, grad_up_pre, preferred_element_type=jnp.float32)
    grad_down = jnp.einsum("htf,htd->hfd", hidden, target, preferred_element_type=jnp.float32)
    return (grad_gate, grad_up, grad_down)


def on_device_generic(queries, keys, values, lr_codes, fast_gate, fast_up, fast_down):
    token_rates = (lr_codes.astype(jnp.float32) + 1.0) / 16.0
    target = (-token_rates[:, :, None] * values.astype(jnp.float32)).astype(jnp.bfloat16)
    gate_b, up_b, down_b = (
        lax.all_gather(fast_gate.astype(jnp.bfloat16), ("seq", "sub"), axis=1, tiled=True),
        lax.all_gather(fast_up.astype(jnp.bfloat16), ("seq", "sub"), axis=1, tiled=True),
        lax.all_gather(fast_down.astype(jnp.bfloat16), ("seq", "sub"), axis=1, tiled=True),
    )
    grad_gate, grad_up, grad_down = local_grads(keys, target, gate_b, up_b, down_b)
    owned = (
        lax.psum_scatter(grad_gate, ("seq", "sub"), scatter_dimension=1, tiled=True),
        lax.psum_scatter(grad_up, ("seq", "sub"), scatter_dimension=1, tiled=True),
        lax.psum_scatter(grad_down, ("seq", "sub"), scatter_dimension=1, tiled=True),
    )
    weights = (fast_gate, fast_up, fast_down)
    grad_local = jnp.stack(
        [
            jnp.sum(owned[0] * owned[0], axis=(1, 2)),
            jnp.sum(owned[1] * owned[1], axis=(1, 2)),
            jnp.sum(owned[2] * owned[2], axis=(1, 2)),
        ],
        axis=1,
    )
    col_gate, col_up, col_down, grad_totals = lax.psum(
        (column_squares(fast_gate), column_squares(fast_up), column_squares(fast_down), grad_local),
        ("seq", "sub"),
    )
    col_weights = (col_gate, col_up, col_down)
    moved_all = []
    for index in range(3):
        scale = step_scale(col_weights[index], grad_totals[:, index])
        moved_all.append(weights[index] - scale[:, None, None] * owned[index])
    moved_cols = lax.psum(
        (column_squares(moved_all[0]), column_squares(moved_all[1]), column_squares(moved_all[2])),
        ("seq", "sub"),
    )
    renewed = [
        rescale(moved_all[index], col_weights[index], moved_cols[index]).astype(jnp.bfloat16)
        for index in range(3)
    ]
    new_gate, new_up, new_down = (
        lax.all_gather(renewed[0], ("seq", "sub"), axis=1, tiled=True),
        lax.all_gather(renewed[1], ("seq", "sub"), axis=1, tiled=True),
        lax.all_gather(renewed[2], ("seq", "sub"), axis=1, tiled=True),
    )
    return apply_fast(queries, new_gate, new_up, new_down)


def block(shape, index_map):
    return pl.BlockSpec(shape, index_map)


def whole(array):
    return pl.BlockSpec(array.shape, lambda *_: (0,) * array.ndim)


def anywhere():
    return pl.BlockSpec(memory_space=pl.ANY)


def call(body, name, positions, grid, operands, in_specs, out_shapes, out_specs, scratch=(), aliases=None, estimate=None, vmem=VMEM_LIMIT):
    return pl.pallas_call(
        body,
        name=name,
        out_shape=out_shapes,
        grid_spec=pltpu.PrefetchScalarGridSpec(
            num_scalar_prefetch=1,
            grid=grid,
            in_specs=in_specs,
            out_specs=out_specs,
            scratch_shapes=list(scratch),
        ),
        input_output_aliases=aliases or {},
        compiler_params=pltpu.CompilerParams(vmem_limit_bytes=vmem),
        cost_estimate=estimate,
    )(positions, *operands)


def sds(shape, dtype):
    return jax.ShapeDtypeStruct(shape, dtype)


def cost(microseconds):
    return pl.CostEstimate(flops=0, bytes_accessed=int(microseconds * 3e6), transcendentals=0)


def first_pieces(positions, own, received, k, after):
    heads, rows, columns = own[0].shape
    half, width = heads // 2, columns // 2

    def body(pos, *refs):
        mine = pl.ds(pl.multiple_of(pos[0] * rows, rows), rows)
        theirs = pl.ds(pl.multiple_of((1 - pos[0]) * rows, rows), rows)
        everything, sends = refs[-half - 1], refs[-half:]
        for head in range(half):
            for m in range(3):
                everything[head, m, mine, :] = refs[m][head].astype(BF16)
                everything[head, m, theirs, :] = refs[3 + m][head].astype(BF16)
        for j, out_ref in enumerate(sends):
            out_ref[...] = everything[pos[1] ^ (j ^ k)]

    spec = block((half, rows, width), lambda i, pos: (pos[0], 0, pos[3]))
    outs = [sds((half, 3, 2 * rows, width), BF16)] + [sds((3, 2 * rows, width), BF16)] * half
    return call(
        body, "first_pieces", positions, (1,), (*own, *received, *after),
        [spec] * 6 + [anywhere()] * len(after), outs, [whole(o) for o in outs], vmem=60 * 1024 * 1024,
    )


def next_pieces(positions, arrived, rows, k, after, handed=None):
    half = len(arrived)
    more = [] if k is None else list(rows)

    passed = [] if handed is None else [handed]

    def body(pos, *refs):
        held, *sends = refs[half + len(more) + len(after) + len(passed) :]
        for j in range(half):
            held[j] = refs[j][...]
        if more:
            height = rows[0].shape[2]
            for ref, x in ((refs[half], pos[2]), (refs[half + 1], 1 - pos[2])):
                at = pl.ds(pl.multiple_of(x * height, height), height)
                for j in range(half):
                    sends[j][:, at, :] = ref[pos[1] ^ (j ^ k)]

    outs = [sds((half, *arrived[0].shape), BF16)]
    if more:
        outs += [sds((3, 2 * rows[0].shape[2], rows[0].shape[3]), BF16)] * half
    operands = (*arrived, *more)
    others = (*after, *passed)
    aliases = {len(operands) + len(others): len(outs)} if passed else {}
    return call(
        body, "next_pieces", positions, (1,), (*operands, *others),
        [whole(a) for a in operands] + [anywhere()] * len(others),
        outs + [sds(p.shape, p.dtype) for p in passed], [whole(o) for o in outs] + [anywhere() for _ in passed],
        aliases=aliases, estimate=cost(3),
    )


def copied(positions, array, after):
    def body(pos, in_ref, *rest):
        rest[-1][...] = in_ref[...]

    shape = sds(array.shape, BF16)
    return call(body, "copied", positions, (1,), (array, *after), [whole(array)] + [anywhere()] * len(after), shape, whole(shape))


def token_rates(positions, codes, half, after):
    tokens = codes[0].shape[1]

    def body(pos, *refs):
        head = pos[0] * half + pl.program_id(0)
        for ref, out_ref in zip(refs, refs[-2:]):
            row = (ref[pl.ds(head, 1), :].astype(F32) + 1.0) / 16.0
            out_ref[0] = jnp.broadcast_to(row, (128, tokens)).T.astype(BF16)

    shape = sds((half, tokens, 128), BF16)
    out = block((1, tokens, 128), lambda i, pos: (i, 0, 0))
    return call(
        body, "token_rates", positions, (half,), (*codes, *after), [whole(c) for c in codes] + [anywhere()] * len(after),
        [shape] * 2, [out] * 2,
    )


def other_half(positions, array, half, after):
    def body(pos, in_ref, *rest):
        rest[-1][...] = in_ref[...]

    _, tokens, columns = array.shape
    spec = block((1, tokens // 2, columns), lambda i, j, pos: ((1 - pos[0]) * half + i, j, 0))
    out = block((1, tokens // 2, columns), lambda i, j, pos: (i, j, 0))
    return call(
        body, "other_half", positions, (half, 2), (array, *after), [spec] + [anywhere()] * len(after),
        sds((half, tokens, columns), BF16), out, estimate=cost(3),
    )


def gradients(positions, keys, values, rates, pieces, k, half, after, cuts):
    z_size, _, piece_rows, width = pieces[0].shape
    tokens, columns = keys[0].shape[1:]
    lanes = rates[0].shape[2]
    rows = columns
    quarter = rows // z_size
    tile = tokens // 2 if tokens % 32 == 0 else tokens
    chunks = 2 * tokens // tile
    last = k == 0
    n_in = 6 + len(pieces) + len(after)

    def body(pos, *refs):
        streams, parts = (refs[0:2], refs[2:4], refs[4:6]), refs[6 : 6 + len(pieces)]
        keep, sends = refs[n_in], refs[n_in + 1 : n_in + 1 + cuts]
        w, key, value, rate, back_gate, back_up, hidden, target, total, rounded, sems_w, sems_in, sems_out = refs[-13:]
        z, x, y = pos[1], pos[2], pos[3]
        mine = pl.ds(pl.multiple_of(x * width, 128), width)
        theirs = pl.ds(pl.multiple_of((1 - x) * width, 128), width)

        places = ((0, y), (0, 1 - y)) if len(parts) == 2 else ((x, y), (1 - x, y), (x, 1 - y), (1 - x, 1 - y))
        weight_copies = []
        for n, (ref, (xx, yy)) in enumerate(zip(parts, places)):
            cols = pl.ds(pl.multiple_of(yy * width, 128), width)
            for j in range(z_size):
                at = pl.ds(pl.multiple_of((z ^ j) * quarter + xx * piece_rows, piece_rows), piece_rows)
                weight_copies.append(pltpu.make_async_copy(ref.at[j], w.at[:, at, cols], sems_w.at[n, j]))
        token_copies = []
        for c in range(chunks):
            source, first = divmod(c * tile, tokens)
            here = pl.ds(c * tile, tile)
            there = pl.ds(first, tile)
            heads = (pos[0] * half + (z ^ k),) * 2 + (z ^ k,)
            token_copies.append([
                pltpu.make_async_copy(pair[source].at[head, there], buffer.at[here], sems_in.at[n, c])
                for n, (pair, head, buffer) in enumerate(zip(streams, heads, (key, value, rate)))
            ])
        for copy in weight_copies + [copy for group in token_copies for copy in group]:
            copy.start()
        for copy in weight_copies:
            copy.wait()
        out_copies = []
        if last:
            own_w, squares = refs[n_in + 1 + cuts : n_in + 3 + cuts]
            out_copies.append(pltpu.make_async_copy(w.at[:, :, mine], own_w, sems_out.at[3, 0]))
            out_copies[-1].start()
            for m in range(3):
                full = w[m].astype(F32)
                squares[m : m + 1, :] = jnp.sum(full * full, axis=0, keepdims=True)

        for c in range(chunks):
            for copy in token_copies[c]:
                copy.wait()
            here = pl.ds(c * tile, tile)
            tokens_rate = jnp.concatenate([rate[here, :].astype(F32)] * (columns // lanes), axis=1)
            t = (-tokens_rate * value[here, :].astype(F32)).astype(BF16)
            target[here, :] = t
            gate = jnp.dot(key[here, :], w[0], preferred_element_type=F32)
            up = jnp.dot(key[here, :], w[1], preferred_element_type=F32)
            back = lax.dot_general(t, w[2], (((1,), (1,)), ((), ())), preferred_element_type=F32)
            sig = 0.5 * jnp.tanh(0.5 * gate) + 0.5
            silu = gate * sig
            hidden[here, :] = (silu * up).astype(BF16)
            back_up[here, :] = (back * silu).astype(BF16)
            back_gate[here, :] = (back * up * (sig + silu * (1.0 - sig))).astype(BF16)
        for m, (a, b) in enumerate(((key, back_gate), (key, back_up), (hidden, target))):
            total[m] = lax.dot_general(a[...], b[...], (((0,), (0,)), ((), ())), preferred_element_type=F32)
            rounded[m] = total[m, :, theirs].astype(BF16)
            copies = [pltpu.make_async_copy(total.at[m, :, mine], keep.at[m], sems_out.at[m, cuts])]
            for n in range(cuts):
                cut = pl.ds(n * (rows // cuts), rows // cuts)
                copies.append(pltpu.make_async_copy(rounded.at[m, cut], sends[n].at[m], sems_out.at[m, n]))
            for copy in copies:
                copy.start()
            out_copies += copies
        for copy in out_copies:
            copy.wait()

    outs = [sds((3, rows, width), F32)] + [sds((3, rows // cuts, width), BF16)] * cuts
    out_specs = [anywhere()] * len(outs)
    if last:
        outs += [sds((3, rows, width), BF16), sds((8, columns), F32)]
        out_specs += [anywhere(), whole(outs[-1])]
    operands = (*keys, *values, *rates, *pieces, *after)
    bf16_rows = pltpu.VMEM((2 * tokens, columns), BF16)
    return call(
        body, "gradients", positions, (1,), operands, [anywhere()] * len(operands), outs, out_specs,
        [
            pltpu.VMEM((3, rows, columns), BF16), bf16_rows, bf16_rows, pltpu.VMEM((2 * tokens, lanes), BF16),
            bf16_rows, bf16_rows, bf16_rows, bf16_rows,
            pltpu.VMEM((3, rows, columns), F32), pltpu.VMEM((3, rows, width), BF16),
            pltpu.SemaphoreType.DMA((len(pieces), z_size)), pltpu.SemaphoreType.DMA((3, chunks)), pltpu.SemaphoreType.DMA((4, cuts + 1)),
        ],
        estimate=pl.CostEstimate(flops=6 * 2 * 2 * tokens * rows * columns, bytes_accessed=14 * 2**20, transcendentals=2 * tokens * columns),
    )


def added(positions, keep, received, after, dtype=BF16, microseconds=1, cuts=1):
    rows = keep.shape[1]

    def body(pos, keep_ref, *refs):
        for m in range(3):
            for c in range(cuts):
                at = pl.ds(c * (rows // cuts), rows // cuts)
                total = keep_ref[m, at, :] + refs[c][m].astype(F32)
                for ref in refs[cuts : len(received)]:
                    total = total + ref[m, at, :].astype(F32)
                refs[-1][m, at, :] = total.astype(dtype)

    operands = (keep, *received)
    shape = sds(keep.shape, dtype)
    specs = [whole(a) for a in operands] + [anywhere()] * len(after)
    return call(body, "added", positions, (1,), (*operands, *after), specs, shape, whole(shape), estimate=cost(microseconds))


def total_gradient(positions, keep, received):
    def body(pos, keep_ref, *refs):
        grad, sums = refs[-2:]
        sums[...] = jnp.zeros_like(sums)
        for m in range(3):
            total = keep_ref[m]
            for ref in refs[:-2]:
                total = total + ref[m].astype(F32)
            grad[m] = total
            columns = jnp.sum(total * total, axis=0, keepdims=True)
            sums[m : m + 1, :] = jnp.broadcast_to(jnp.sum(columns, axis=1, keepdims=True), (1, sums.shape[1]))

    outs = [sds(keep.shape, F32), sds((8, 128), F32)]
    operands = (keep, *received)
    return call(body, "total_gradient", positions, (1,), operands, [whole(a) for a in operands], outs, [whole(o) for o in outs])


def renewed_block(positions, grad, own_w, squares, sums, sums_in):
    width = grad.shape[2]

    def body(pos, g_ref, w_ref, sq_ref, sums_ref, sums_in_ref, out):
        mine = pl.ds(pl.multiple_of(pos[2] * width, 128), width)
        for m in range(3):
            total_g = sums_ref[m : m + 1, :1] + sums_in_ref[m : m + 1, :1]
            total_w = jnp.sum(sq_ref[m : m + 1, :], axis=1, keepdims=True)
            scale = STEP_SIZE * jnp.sqrt(total_w + EPSILON) / jnp.sqrt(total_g + EPSILON)
            moved = w_ref[m].astype(F32) - scale * g_ref[m]
            col_moved = jnp.sum(moved * moved, axis=0, keepdims=True)
            out[m] = (moved * jnp.sqrt((sq_ref[m : m + 1, mine] + EPSILON) / (col_moved + EPSILON))).astype(BF16)

    operands = (grad, own_w, squares, sums, sums_in)
    shape = sds(grad.shape, BF16)
    return call(body, "renewed_block", positions, (1,), operands, [whole(a) for a in operands], shape, whole(shape))


def apply_renewed(positions, queries, queries_in, held, swapped, k, half, out, late, after):
    _, rows, width = held.shape
    columns = 2 * width
    heads, tokens, _ = queries.shape
    tile = tokens // 2 if tokens % 32 == 0 else tokens
    chunks = 2 * tokens // tile
    blocks = [b for _, b in late]
    n_in = 4 + len(blocks) + len(after) + (0 if out is None else 1)

    def body(pos, q0, q1, held_ref, swapped_ref, *refs):
        late_refs = refs[: len(blocks)]
        out_ref, send_ref, w, query, result, brought, sems_in, sems_q, sems_out, sems_late = refs[n_in - 4 :]
        x = pos[2]
        heads_of = (pos[0] * half + (pos[1] ^ k), pos[1] ^ k)
        weights = [
            pltpu.make_async_copy(ref, w.at[:, :, pl.ds(pl.multiple_of(xx * width, 128), width)], sems_in.at[n])
            for n, (ref, xx) in enumerate(((held_ref, x), (swapped_ref, 1 - x)))
        ]
        loads, stores = [], []
        for c in range(chunks):
            source, first = divmod(c * tile, tokens)
            here, there = pl.ds(c * tile, tile), pl.ds(first, tile)
            loads.append(pltpu.make_async_copy((q0, q1)[source].at[heads_of[source], there], query.at[here], sems_q.at[c]))
            to = send_ref.at[there] if source else out_ref.at[heads_of[0], there]
            stores.append(pltpu.make_async_copy(result.at[here], to, sems_out.at[c]))
        late_in = [pltpu.make_async_copy(ref, brought.at[n], sems_late.at[n, 0]) for n, ref in enumerate(late_refs)]
        late_out = [
            pltpu.make_async_copy(brought.at[n], out_ref.at[(1 - pos[0]) * half + (pos[1] ^ late[n][0])], sems_late.at[n, 1])
            for n in range(len(blocks))
        ]
        for copy in weights + loads + late_in:
            copy.start()
        for copy in weights:
            copy.wait()
        for c in range(chunks):
            loads[c].wait()
            here = pl.ds(c * tile, tile)
            q = query[here, :]
            gate = jnp.dot(q, w[0], preferred_element_type=F32)
            up = jnp.dot(q, w[1], preferred_element_type=F32)
            hidden = (gate * (0.5 * jnp.tanh(0.5 * gate) + 0.5) * up).astype(BF16)
            result[here, :] = jnp.dot(hidden, w[2], preferred_element_type=F32).astype(BF16)
            stores[c].start()
            if c == 0:
                for n in range(len(blocks)):
                    late_in[n].wait()
                    late_out[n].start()
        for copy in stores + late_out:
            copy.wait()

    operands = [queries, queries_in, held, swapped, *blocks, *after]
    aliases = {}
    if out is not None:
        aliases = {1 + len(operands): 0}
        operands.append(out)
    return call(
        body, "apply_renewed", positions, (1,), operands, [anywhere()] * len(operands),
        [sds(queries.shape, BF16), sds((tokens, columns), BF16)], [anywhere()] * 2,
        [
            pltpu.VMEM((3, rows, columns), BF16), pltpu.VMEM((2 * tokens, columns), BF16), pltpu.VMEM((2 * tokens, columns), BF16),
            pltpu.VMEM((max(len(blocks), 1), tokens, columns), BF16),
            pltpu.SemaphoreType.DMA((2,)), pltpu.SemaphoreType.DMA((chunks,)), pltpu.SemaphoreType.DMA((chunks,)),
            pltpu.SemaphoreType.DMA((max(len(blocks), 1), 2)),
        ],
        aliases,
        pl.CostEstimate(flops=3 * 2 * 2 * tokens * rows * columns, bytes_accessed=7 * 2**20, transcendentals=2 * tokens * columns),
    )


def place(positions, out, late, half):
    n = len(late)
    tokens, columns = late[0][1].shape
    cuts = 4 if tokens % 64 == 0 else 1
    tile = tokens // cuts

    def body(pos, *refs):
        out_ref, held, sems_in, sems_out = refs[-4:]
        pairs = []
        for i, (k, _) in enumerate(late):
            head = (1 - pos[0]) * half + (pos[1] ^ k)
            for c in range(cuts):
                at = pl.ds(c * tile, tile)
                pairs.append((
                    pltpu.make_async_copy(refs[i].at[at], held.at[i, at], sems_in.at[i, c]),
                    pltpu.make_async_copy(held.at[i, at], out_ref.at[head, at], sems_out.at[i, c]),
                ))
        for first, _ in pairs:
            first.start()
        for first, second in pairs:
            first.wait()
            second.start()
        for _, second in pairs:
            second.wait()

    return call(
        body, "place", positions, (1,), (*(b for _, b in late), out), [anywhere()] * (n + 1),
        sds(out.shape, BF16), anywhere(),
        [pltpu.VMEM((n, tokens, columns), BF16), pltpu.SemaphoreType.DMA((n, cuts)), pltpu.SemaphoreType.DMA((n, cuts))],
        {1 + n: 0}, cost(1),
    )


def on_device_fast(queries, keys, values, lr_codes, fast_gate, fast_up, fast_down):
    heads, tokens, _ = queries.shape
    half = heads // 2
    core, seq = lax.axis_index("sub"), lax.axis_index("seq")
    positions = jnp.stack([core, seq // 2, seq % 2, lax.axis_index("groups")]).astype(jnp.int32)
    flip = [(0, 1), (1, 0)]

    def over_sub(a):
        return lax.ppermute(a, "sub", flip)

    def over_groups(a):
        return lax.ppermute(a, "groups", flip)

    def over_x(a):
        return lax.ppermute(a, "seq", [(i, i ^ 1) for i in range(8)])

    def over_z(a, j):
        return lax.ppermute(a, "seq", [(i, i ^ (2 * j)) for i in range(8)])

    weights = (fast_gate, fast_up, fast_down)
    rows_in = tuple(over_sub(w) for w in weights)
    all_keys, all_values = (keys, over_sub(keys)), (values, over_sub(values))
    codes = (lr_codes, over_sub(lr_codes))

    def head_gradients(k, pieces, after):
        keep, send, *rest = gradients(positions, all_keys, all_values, rates, pieces, k, half, after, 1)
        return keep, over_x(send), *rest

    def turn(pieces, k, after, handed=None):
        arrived = (pieces[0], *(over_z(a, j) for j, a in enumerate(pieces[1:], 1)))
        return next_pieces(positions, arrived, rows, k, after, handed)

    everything, *pieces = first_pieces(positions, weights, rows_in, 3, ())
    rows = (everything, over_x(everything))
    held, *pieces = turn(pieces, 2, ())
    swapped = over_x(held)
    pieces3 = (held, swapped, over_groups(held), over_groups(swapped))
    rates = token_rates(positions, codes, half, (held,))
    queries_in = over_sub(other_half(positions, queries, half, (held,)))
    held, *pieces = turn(pieces, 1, (*pieces3, *rates))
    pieces2 = (held, over_groups(held))
    keep3, *sends = gradients(positions, all_keys, all_values, rates, pieces3, 3, half, (held,), 4)
    held, *pieces = turn(pieces, 0, (keep3, pieces2[1]))
    pieces1 = (held, over_groups(held))
    keep2, send2 = gradients(positions, all_keys, all_values, rates, pieces2, 2, half, (held,), 1)
    in3 = [over_x(a) for a in sends]
    sum3 = added(positions, keep3, in3, (keep2,), cuts=4)
    from1 = over_z(sum3, 1)
    (held,) = turn(pieces, None, (sum3, pieces1[1]))
    pieces0 = (held, over_groups(held))
    keep1, send1 = gradients(positions, all_keys, all_values, rates, pieces1, 1, half, (held,), 1)
    in2 = over_x(send2)
    sum2 = added(positions, keep2, (in2, from1), (keep1,))
    from2 = over_z(sum2, 2)
    keep0, in0, own_w, squares = head_gradients(0, pieces0, (sum2,))
    in1 = over_x(send1)
    sum1 = added(positions, keep1, (in1,), (keep0,))
    from1 = over_z(sum1, 1)
    partial = added(positions, keep0, (from2,), (sum1,), F32, 8)
    grad, sums = total_gradient(positions, partial, (in0, from1))
    renewed = renewed_block(positions, grad, own_w, squares, sums, over_x(sums))

    swapped = over_x(renewed)
    from1, from2 = over_z(renewed, 1), over_z(renewed, 2)
    from3 = over_z(from2, 1)
    matrices = {0: (renewed, swapped), 2: (from2, over_x(from2)), 3: (from3, over_x(from3))}

    def head_output(k, out, late, after):
        out, sent = apply_renewed(positions, queries, queries_in, *matrices[k], k, half, out, late, after)
        return out, (k, over_sub(sent))

    out, late0 = head_output(0, None, (), (from1, from2))
    swapped_late = copied(positions, swapped, (from3, out))
    matrices[1] = (from1, over_z(swapped_late, 1))
    out, late2 = head_output(2, out, (), (swapped_late,))
    out, late1 = head_output(1, out, (late0,), matrices[3])
    out, late3 = head_output(3, out, (late2,), ())
    return place(positions, out, (late1, late3), half)


def solution(mesh):
    seq, sub, groups = mesh.shape["seq"], mesh.shape["sub"], mesh.shape["groups"]

    def on_device(queries, *rest):
        rows, columns = rest[3].shape[1:]
        fits = (groups, seq, sub, queries.shape[0]) == (2, 8, 2, 8) and rows % 32 == 0 and columns == seq * sub * rows and columns % 256 == 0
        return (on_device_fast if fits else on_device_generic)(queries, *rest)

    return jax.shard_map(
        on_device,
        mesh=mesh,
        in_specs=(
            P("head", ("groups", "seq", "sub"), None),
            P("head", ("groups", "seq", "sub"), None),
            P("head", ("groups", "seq", "sub"), None),
            P("head", ("groups", "seq", "sub")),
            P("head", ("seq", "sub"), None),
            P("head", ("seq", "sub"), None),
            P("head", ("seq", "sub"), None),
        ),
        out_specs=P("head", ("groups", "seq", "sub"), None),
        check_vma=False,
    )
```

```python
import functools

import jax
import jax.numpy as jnp
from jax import lax
from jax.experimental import pallas as pl
from jax.experimental.pallas import tpu as pltpu
from jax.sharding import PartitionSpec as P

EPSILON = 1e-06
STEP_SIZE = 0.5
BF16 = jnp.bfloat16
F32 = jnp.float32
VMEM_LIMIT = 64 * 1024 * 1024


def column_squares(matrix):
    return jnp.sum(matrix * matrix, axis=1)


def rescale(moved, col_weight, col_moved):
    return moved * jnp.sqrt((col_weight + EPSILON) / (col_moved + EPSILON))[:, None, :]


def step_scale(col_weight, grad_total):
    return (
        STEP_SIZE * jnp.sqrt(jnp.sum(col_weight, axis=1) + EPSILON) / jnp.sqrt(grad_total + EPSILON)
    )


def apply_fast(queries, gate_b, up_b, down_b):
    query_gate = jnp.einsum("htd,hdf->htf", queries, gate_b, preferred_element_type=jnp.float32)
    query_up = jnp.einsum("htd,hdf->htf", queries, up_b, preferred_element_type=jnp.float32)
    query_hidden = (jax.nn.silu(query_gate) * query_up).astype(jnp.bfloat16)
    return jnp.einsum(
        "htf,hfd->htd", query_hidden, down_b, preferred_element_type=jnp.float32
    ).astype(jnp.bfloat16)


def local_grads(keys, target, gate_b, up_b, down_b):
    gate_pre = jnp.einsum("htd,hdf->htf", keys, gate_b, preferred_element_type=jnp.float32)
    up_pre = jnp.einsum("htd,hdf->htf", keys, up_b, preferred_element_type=jnp.float32)
    sigmoid_gate = jax.nn.sigmoid(gate_pre)
    hidden = (gate_pre * sigmoid_gate * up_pre).astype(jnp.bfloat16)
    back = jnp.einsum("htd,hfd->htf", target, down_b, preferred_element_type=jnp.float32)
    grad_gate_pre = (back * up_pre * sigmoid_gate * (1.0 + gate_pre * (1.0 - sigmoid_gate))).astype(
        jnp.bfloat16
    )
    grad_up_pre = (back * gate_pre * sigmoid_gate).astype(jnp.bfloat16)
    grad_gate = jnp.einsum("htd,htf->hdf", keys, grad_gate_pre, preferred_element_type=jnp.float32)
    grad_up = jnp.einsum("htd,htf->hdf", keys, grad_up_pre, preferred_element_type=jnp.float32)
    grad_down = jnp.einsum("htf,htd->hfd", hidden, target, preferred_element_type=jnp.float32)
    return (grad_gate, grad_up, grad_down)


def on_device_generic(queries, keys, values, lr_codes, fast_gate, fast_up, fast_down):
    token_rates = (lr_codes.astype(jnp.float32) + 1.0) / 16.0
    target = (-token_rates[:, :, None] * values.astype(jnp.float32)).astype(jnp.bfloat16)
    gate_b, up_b, down_b = (
        lax.all_gather(fast_gate.astype(jnp.bfloat16), ("seq", "sub"), axis=1, tiled=True),
        lax.all_gather(fast_up.astype(jnp.bfloat16), ("seq", "sub"), axis=1, tiled=True),
        lax.all_gather(fast_down.astype(jnp.bfloat16), ("seq", "sub"), axis=1, tiled=True),
    )
    grad_gate, grad_up, grad_down = local_grads(keys, target, gate_b, up_b, down_b)
    owned = (
        lax.psum_scatter(grad_gate, ("seq", "sub"), scatter_dimension=1, tiled=True),
        lax.psum_scatter(grad_up, ("seq", "sub"), scatter_dimension=1, tiled=True),
        lax.psum_scatter(grad_down, ("seq", "sub"), scatter_dimension=1, tiled=True),
    )
    weights = (fast_gate, fast_up, fast_down)
    grad_local = jnp.stack(
        [
            jnp.sum(owned[0] * owned[0], axis=(1, 2)),
            jnp.sum(owned[1] * owned[1], axis=(1, 2)),
            jnp.sum(owned[2] * owned[2], axis=(1, 2)),
        ],
        axis=1,
    )
    col_gate, col_up, col_down, grad_totals = lax.psum(
        (column_squares(fast_gate), column_squares(fast_up), column_squares(fast_down), grad_local),
        ("seq", "sub"),
    )
    col_weights = (col_gate, col_up, col_down)
    moved_all = []
    for index in range(3):
        scale = step_scale(col_weights[index], grad_totals[:, index])
        moved_all.append(weights[index] - scale[:, None, None] * owned[index])
    moved_cols = lax.psum(
        (column_squares(moved_all[0]), column_squares(moved_all[1]), column_squares(moved_all[2])),
        ("seq", "sub"),
    )
    renewed = [
        rescale(moved_all[index], col_weights[index], moved_cols[index]).astype(jnp.bfloat16)
        for index in range(3)
    ]
    new_gate, new_up, new_down = (
        lax.all_gather(renewed[0], ("seq", "sub"), axis=1, tiled=True),
        lax.all_gather(renewed[1], ("seq", "sub"), axis=1, tiled=True),
        lax.all_gather(renewed[2], ("seq", "sub"), axis=1, tiled=True),
    )
    return apply_fast(queries, new_gate, new_up, new_down)


def block(shape, index_map):
    return pl.BlockSpec(shape, index_map)


def whole(array):
    return pl.BlockSpec(array.shape, lambda *_: (0,) * array.ndim)


def anywhere():
    return pl.BlockSpec(memory_space=pl.ANY)


def call(body, name, positions, grid, operands, in_specs, out_shapes, out_specs, scratch=(), aliases=None, estimate=None, vmem=VMEM_LIMIT):
    return pl.pallas_call(
        body,
        name=name,
        out_shape=out_shapes,
        grid_spec=pltpu.PrefetchScalarGridSpec(
            num_scalar_prefetch=1,
            grid=grid,
            in_specs=in_specs,
            out_specs=out_specs,
            scratch_shapes=list(scratch),
        ),
        input_output_aliases=aliases or {},
        compiler_params=pltpu.CompilerParams(vmem_limit_bytes=vmem),
        cost_estimate=estimate,
    )(positions, *operands)


def sds(shape, dtype):
    return jax.ShapeDtypeStruct(shape, dtype)


def cost(microseconds):
    return pl.CostEstimate(flops=0, bytes_accessed=int(microseconds * 3e6), transcendentals=0)


def first_pieces(positions, own, received, k, after):
    heads, rows, columns = own[0].shape
    half, width = heads // 2, columns // 2

    def body(pos, *refs):
        mine = pl.ds(pl.multiple_of(pos[0] * rows, rows), rows)
        theirs = pl.ds(pl.multiple_of((1 - pos[0]) * rows, rows), rows)
        everything, sends = refs[-half - 1], refs[-half:]
        for head in range(half):
            for m in range(3):
                everything[head, m, mine, :] = refs[m][head].astype(BF16)
                everything[head, m, theirs, :] = refs[3 + m][head].astype(BF16)
        for j, out_ref in enumerate(sends):
            out_ref[...] = everything[pos[1] ^ (j ^ k)]

    spec = block((half, rows, width), lambda i, pos: (pos[0], 0, pos[3]))
    outs = [sds((half, 3, 2 * rows, width), BF16)] + [sds((3, 2 * rows, width), BF16)] * half
    return call(
        body, "first_pieces", positions, (1,), (*own, *received, *after),
        [spec] * 6 + [anywhere()] * len(after), outs, [whole(o) for o in outs], vmem=60 * 1024 * 1024,
    )


def next_pieces(positions, arrived, rows, k, after, handed=None):
    half = len(arrived)
    more = [] if k is None else list(rows)

    passed = [] if handed is None else [handed]

    def body(pos, *refs):
        held, *sends = refs[half + len(more) + len(after) + len(passed) :]
        for j in range(half):
            held[j] = refs[j][...]
        if more:
            height = rows[0].shape[2]
            for ref, x in ((refs[half], pos[2]), (refs[half + 1], 1 - pos[2])):
                at = pl.ds(pl.multiple_of(x * height, height), height)
                for j in range(half):
                    sends[j][:, at, :] = ref[pos[1] ^ (j ^ k)]

    outs = [sds((half, *arrived[0].shape), BF16)]
    if more:
        outs += [sds((3, 2 * rows[0].shape[2], rows[0].shape[3]), BF16)] * half
    operands = (*arrived, *more)
    others = (*after, *passed)
    aliases = {len(operands) + len(others): len(outs)} if passed else {}
    return call(
        body, "next_pieces", positions, (1,), (*operands, *others),
        [whole(a) for a in operands] + [anywhere()] * len(others),
        outs + [sds(p.shape, p.dtype) for p in passed], [whole(o) for o in outs] + [anywhere() for _ in passed],
        aliases=aliases, estimate=cost(3),
    )


def copied(positions, array, after):
    def body(pos, in_ref, *rest):
        rest[-1][...] = in_ref[...]

    shape = sds(array.shape, BF16)
    return call(body, "copied", positions, (1,), (array, *after), [whole(array)] + [anywhere()] * len(after), shape, whole(shape))


def token_rates(positions, codes, half, after):
    tokens = codes[0].shape[1]

    def body(pos, *refs):
        head = pos[0] * half + pl.program_id(0)
        for ref, out_ref in zip(refs, refs[-2:]):
            row = (ref[pl.ds(head, 1), :].astype(F32) + 1.0) / 16.0
            out_ref[0] = jnp.broadcast_to(row, (128, tokens)).T.astype(BF16)

    shape = sds((half, tokens, 128), BF16)
    out = block((1, tokens, 128), lambda i, pos: (i, 0, 0))
    return call(
        body, "token_rates", positions, (half,), (*codes, *after), [whole(c) for c in codes] + [anywhere()] * len(after),
        [shape] * 2, [out] * 2,
    )


def other_half(positions, array, half, after):
    def body(pos, in_ref, *rest):
        rest[-1][...] = in_ref[...]

    _, tokens, columns = array.shape
    spec = block((1, tokens // 2, columns), lambda i, j, pos: ((1 - pos[0]) * half + i, j, 0))
    out = block((1, tokens // 2, columns), lambda i, j, pos: (i, j, 0))
    return call(
        body, "other_half", positions, (half, 2), (array, *after), [spec] + [anywhere()] * len(after),
        sds((half, tokens, columns), BF16), out, estimate=cost(3),
    )


def gradients(positions, keys, values, rates, pieces, k, half, after, cuts):
    z_size, _, piece_rows, width = pieces[0].shape
    tokens, columns = keys[0].shape[1:]
    lanes = rates[0].shape[2]
    rows = columns
    quarter = rows // z_size
    tile = tokens // 2 if tokens % 32 == 0 else tokens
    chunks = 2 * tokens // tile
    last = k == 0
    n_in = 6 + len(pieces) + len(after)

    def body(pos, *refs):
        streams, parts = (refs[0:2], refs[2:4], refs[4:6]), refs[6 : 6 + len(pieces)]
        keep, sends = refs[n_in], refs[n_in + 1 : n_in + 1 + cuts]
        w, key, value, rate, grads, hidden, target, total, rounded, sems_w, sems_in, sems_out = refs[-12:]
        z, x, y = pos[1], pos[2], pos[3]
        mine = pl.ds(pl.multiple_of(x * width, 128), width)
        theirs = pl.ds(pl.multiple_of((1 - x) * width, 128), width)

        places = ((0, y), (0, 1 - y)) if len(parts) == 2 else ((x, y), (1 - x, y), (x, 1 - y), (1 - x, 1 - y))
        weight_copies = []
        for n, (ref, (xx, yy)) in enumerate(zip(parts, places)):
            cols = pl.ds(pl.multiple_of(yy * width, 128), width)
            for j in range(z_size):
                at = pl.ds(pl.multiple_of((z ^ j) * quarter + xx * piece_rows, piece_rows), piece_rows)
                weight_copies.append(pltpu.make_async_copy(ref.at[j], w.at[:, at, cols], sems_w.at[n, j]))
        token_copies = []
        heads = (pos[0] * half + (z ^ k),) * 2 + (z ^ k,)
        for c in range(chunks):
            source, first = divmod(c * tile, tokens)
            here = pl.ds(c * tile, tile)
            there = pl.ds(first, tile)
            token_copies.append([
                pltpu.make_async_copy(pair[source].at[head, there], buffer.at[here], sems_in.at[n, c])
                for n, (pair, head, buffer) in enumerate(zip(streams, heads, (key, value, rate)))
            ])
        for copy in weight_copies + [copy for group in token_copies for copy in group]:
            copy.start()
        for copy in weight_copies:
            copy.wait()

        def own_copy():
            return pltpu.make_async_copy(w.at[:, :, mine], refs[n_in + 1 + cuts], sems_out.at[3, 0])

        def out_copies(m):
            copies = [pltpu.make_async_copy(total.at[m, :, mine], keep.at[m], sems_out.at[m, cuts])]
            for n in range(cuts):
                cut = pl.ds(n * (rows // cuts), rows // cuts)
                copies.append(pltpu.make_async_copy(rounded.at[m, cut], sends[n].at[m], sems_out.at[m, n]))
            return copies

        if last:
            own_copy().start()
            squares = refs[n_in + 2 + cuts]
            for m in range(3):
                full = w[m].astype(F32)
                squares[m : m + 1, :] = jnp.sum(full * full, axis=0, keepdims=True)

        @pl.loop(0, chunks)
        def _(c):
            here = pl.ds(pl.multiple_of(c * tile, tile), tile)
            for n, (pair, head, buffer) in enumerate(zip(streams, heads, (key, value, rate))):
                pltpu.make_async_copy(pair[0].at[head, pl.ds(0, tile)], buffer.at[here], sems_in.at[n, c]).wait()
            tokens_rate = jnp.concatenate([rate[here, :].astype(F32)] * (columns // lanes), axis=1)
            t = (-tokens_rate * value[here, :].astype(F32)).astype(BF16)
            target[here, :] = t
            gate = jnp.dot(key[here, :], w[0], preferred_element_type=F32)
            up = jnp.dot(key[here, :], w[1], preferred_element_type=F32)
            back = lax.dot_general(t, w[2], (((1,), (1,)), ((), ())), preferred_element_type=F32)
            sig = 0.5 * jnp.tanh(0.5 * gate) + 0.5
            silu = gate * sig
            hidden[here, :] = (silu * up).astype(BF16)
            grads[1, here, :] = (back * silu).astype(BF16)
            grads[0, here, :] = (back * up * (sig + silu * (1.0 - sig))).astype(BF16)

        def product(m, a, b):
            total[m] = lax.dot_general(a, b, (((0,), (0,)), ((), ())), preferred_element_type=F32)
            rounded[m] = total[m, :, theirs].astype(BF16)
            for copy in out_copies(m):
                copy.start()

        @pl.loop(0, 2)
        def _(m):
            product(m, key[...], grads[m])

        product(2, hidden[...], target[...])
        for m in range(3):
            for copy in out_copies(m):
                copy.wait()
        if last:
            own_copy().wait()

    outs = [sds((3, rows, width), F32)] + [sds((3, rows // cuts, width), BF16)] * cuts
    out_specs = [anywhere()] * len(outs)
    if last:
        outs += [sds((3, rows, width), BF16), sds((8, columns), F32)]
        out_specs += [anywhere(), whole(outs[-1])]
    operands = (*keys, *values, *rates, *pieces, *after)
    bf16_rows = pltpu.VMEM((2 * tokens, columns), BF16)
    return call(
        body, "gradients", positions, (1,), operands, [anywhere()] * len(operands), outs, out_specs,
        [
            pltpu.VMEM((3, rows, columns), BF16), bf16_rows, bf16_rows, pltpu.VMEM((2 * tokens, lanes), BF16),
            pltpu.VMEM((2, 2 * tokens, columns), BF16), bf16_rows, bf16_rows,
            pltpu.VMEM((3, rows, columns), F32), pltpu.VMEM((3, rows, width), BF16),
            pltpu.SemaphoreType.DMA((len(pieces), z_size)), pltpu.SemaphoreType.DMA((3, chunks)), pltpu.SemaphoreType.DMA((4, cuts + 1)),
        ],
        estimate=pl.CostEstimate(flops=6 * 2 * 2 * tokens * rows * columns, bytes_accessed=14 * 2**20, transcendentals=2 * tokens * columns),
    )


def added(positions, keep, received, after, dtype=BF16, microseconds=1, cuts=1):
    rows = keep.shape[1]

    def body(pos, keep_ref, *refs):
        for m in range(3):
            for c in range(cuts):
                at = pl.ds(c * (rows // cuts), rows // cuts)
                total = keep_ref[m, at, :] + refs[c][m].astype(F32)
                for ref in refs[cuts : len(received)]:
                    total = total + ref[m, at, :].astype(F32)
                refs[-1][m, at, :] = total.astype(dtype)

    operands = (keep, *received)
    shape = sds(keep.shape, dtype)
    specs = [whole(a) for a in operands] + [anywhere()] * len(after)
    return call(body, "added", positions, (1,), (*operands, *after), specs, shape, whole(shape), estimate=cost(microseconds))


def total_gradient(positions, keep, received):
    def body(pos, keep_ref, *refs):
        grad, sums = refs[-2:]
        sums[...] = jnp.zeros_like(sums)
        for m in range(3):
            total = keep_ref[m]
            for ref in refs[:-2]:
                total = total + ref[m].astype(F32)
            grad[m] = total
            columns = jnp.sum(total * total, axis=0, keepdims=True)
            sums[m : m + 1, :] = jnp.broadcast_to(jnp.sum(columns, axis=1, keepdims=True), (1, sums.shape[1]))

    outs = [sds(keep.shape, F32), sds((8, 128), F32)]
    operands = (keep, *received)
    return call(body, "total_gradient", positions, (1,), operands, [whole(a) for a in operands], outs, [whole(o) for o in outs])


def renewed_block(positions, grad, own_w, squares, sums, sums_in):
    width = grad.shape[2]

    def body(pos, g_ref, w_ref, sq_ref, sums_ref, sums_in_ref, out):
        mine = pl.ds(pl.multiple_of(pos[2] * width, 128), width)
        for m in range(3):
            total_g = sums_ref[m : m + 1, :1] + sums_in_ref[m : m + 1, :1]
            total_w = jnp.sum(sq_ref[m : m + 1, :], axis=1, keepdims=True)
            scale = STEP_SIZE * jnp.sqrt(total_w + EPSILON) / jnp.sqrt(total_g + EPSILON)
            moved = w_ref[m].astype(F32) - scale * g_ref[m]
            col_moved = jnp.sum(moved * moved, axis=0, keepdims=True)
            out[m] = (moved * jnp.sqrt((sq_ref[m : m + 1, mine] + EPSILON) / (col_moved + EPSILON))).astype(BF16)

    operands = (grad, own_w, squares, sums, sums_in)
    shape = sds(grad.shape, BF16)
    return call(body, "renewed_block", positions, (1,), operands, [whole(a) for a in operands], shape, whole(shape))


def apply_renewed(positions, queries, queries_in, held, swapped, k, half, out, late, after):
    _, rows, width = held.shape
    columns = 2 * width
    heads, tokens, _ = queries.shape
    tile = tokens // 2 if tokens % 32 == 0 else tokens
    chunks = 2 * tokens // tile
    blocks = [b for _, b in late]
    n_in = 4 + len(blocks) + len(after) + (0 if out is None else 1)

    def body(pos, q0, q1, held_ref, swapped_ref, *refs):
        late_refs = refs[: len(blocks)]
        out_ref, send_ref, w, query, result, brought, sems_in, sems_q, sems_out, sems_late = refs[n_in - 4 :]
        x = pos[2]
        heads_of = (pos[0] * half + (pos[1] ^ k), pos[1] ^ k)
        weights = [
            pltpu.make_async_copy(ref, w.at[:, :, pl.ds(pl.multiple_of(xx * width, 128), width)], sems_in.at[n])
            for n, (ref, xx) in enumerate(((held_ref, x), (swapped_ref, 1 - x)))
        ]
        loads, stores = [], []
        for c in range(chunks):
            source, first = divmod(c * tile, tokens)
            here, there = pl.ds(c * tile, tile), pl.ds(first, tile)
            loads.append(pltpu.make_async_copy((q0, q1)[source].at[heads_of[source], there], query.at[here], sems_q.at[c]))
            to = send_ref.at[there] if source else out_ref.at[heads_of[0], there]
            stores.append(pltpu.make_async_copy(result.at[here], to, sems_out.at[c]))
        late_in = [pltpu.make_async_copy(ref, brought.at[n], sems_late.at[n, 0]) for n, ref in enumerate(late_refs)]
        late_out = [
            pltpu.make_async_copy(brought.at[n], out_ref.at[(1 - pos[0]) * half + (pos[1] ^ late[n][0])], sems_late.at[n, 1])
            for n in range(len(blocks))
        ]
        for copy in weights + loads + late_in:
            copy.start()
        for copy in weights:
            copy.wait()

        @pl.loop(0, chunks)
        def _(c):
            here = pl.ds(pl.multiple_of(c * tile, tile), tile)
            there = pl.ds(pl.multiple_of(lax.rem(c * tile, tokens), tile), tile)
            pltpu.make_async_copy(q1.at[heads_of[1], pl.ds(0, tile)], query.at[here], sems_q.at[c]).wait()
            q = query[here, :]
            gate = jnp.dot(q, w[0], preferred_element_type=F32)
            up = jnp.dot(q, w[1], preferred_element_type=F32)
            hidden = (gate * (0.5 * jnp.tanh(0.5 * gate) + 0.5) * up).astype(BF16)
            result[here, :] = jnp.dot(hidden, w[2], preferred_element_type=F32).astype(BF16)

            @pl.when(c < chunks // 2)
            def _():
                pltpu.make_async_copy(result.at[here], out_ref.at[heads_of[0], there], sems_out.at[c]).start()

            @pl.when(c >= chunks // 2)
            def _():
                pltpu.make_async_copy(result.at[here], send_ref.at[there], sems_out.at[c]).start()

            @pl.when(c == 0)
            def _():
                for n in range(len(blocks)):
                    late_in[n].wait()
                    late_out[n].start()

        for copy in stores + late_out:
            copy.wait()

    operands = [queries, queries_in, held, swapped, *blocks, *after]
    aliases = {}
    if out is not None:
        aliases = {1 + len(operands): 0}
        operands.append(out)
    return call(
        body, "apply_renewed", positions, (1,), operands, [anywhere()] * len(operands),
        [sds(queries.shape, BF16), sds((tokens, columns), BF16)], [anywhere()] * 2,
        [
            pltpu.VMEM((3, rows, columns), BF16), pltpu.VMEM((2 * tokens, columns), BF16), pltpu.VMEM((2 * tokens, columns), BF16),
            pltpu.VMEM((max(len(blocks), 1), tokens, columns), BF16),
            pltpu.SemaphoreType.DMA((2,)), pltpu.SemaphoreType.DMA((chunks,)), pltpu.SemaphoreType.DMA((chunks,)),
            pltpu.SemaphoreType.DMA((max(len(blocks), 1), 2)),
        ],
        aliases,
        pl.CostEstimate(flops=3 * 2 * 2 * tokens * rows * columns, bytes_accessed=7 * 2**20, transcendentals=2 * tokens * columns),
    )


def place(positions, out, late, half):
    n = len(late)
    tokens, columns = late[0][1].shape
    cuts = 4 if tokens % 64 == 0 else 1
    tile = tokens // cuts

    def body(pos, *refs):
        out_ref, held, sems_in, sems_out = refs[-4:]
        pairs = []
        for i, (k, _) in enumerate(late):
            head = (1 - pos[0]) * half + (pos[1] ^ k)
            for c in range(cuts):
                at = pl.ds(c * tile, tile)
                pairs.append((
                    pltpu.make_async_copy(refs[i].at[at], held.at[i, at], sems_in.at[i, c]),
                    pltpu.make_async_copy(held.at[i, at], out_ref.at[head, at], sems_out.at[i, c]),
                ))
        for first, _ in pairs:
            first.start()
        for first, second in pairs:
            first.wait()
            second.start()
        for _, second in pairs:
            second.wait()

    return call(
        body, "place", positions, (1,), (*(b for _, b in late), out), [anywhere()] * (n + 1),
        sds(out.shape, BF16), anywhere(),
        [pltpu.VMEM((n, tokens, columns), BF16), pltpu.SemaphoreType.DMA((n, cuts)), pltpu.SemaphoreType.DMA((n, cuts))],
        {1 + n: 0}, cost(1),
    )


def on_device_fast(queries, keys, values, lr_codes, fast_gate, fast_up, fast_down):
    heads, tokens, _ = queries.shape
    half = heads // 2
    core, seq = lax.axis_index("sub"), lax.axis_index("seq")
    positions = jnp.stack([core, seq // 2, seq % 2, lax.axis_index("groups")]).astype(jnp.int32)
    flip = [(0, 1), (1, 0)]

    def over_sub(a):
        return lax.ppermute(a, "sub", flip)

    def over_groups(a):
        return lax.ppermute(a, "groups", flip)

    def over_x(a):
        return lax.ppermute(a, "seq", [(i, i ^ 1) for i in range(8)])

    def over_z(a, j):
        return lax.ppermute(a, "seq", [(i, i ^ (2 * j)) for i in range(8)])

    weights = (fast_gate, fast_up, fast_down)
    rows_in = tuple(over_sub(w) for w in weights)
    all_keys, all_values = (keys, over_sub(keys)), (values, over_sub(values))
    codes = (lr_codes, over_sub(lr_codes))

    def head_gradients(k, pieces, after):
        keep, send, *rest = gradients(positions, all_keys, all_values, rates, pieces, k, half, after, 1)
        return keep, over_x(send), *rest

    def turn(pieces, k, after, handed=None):
        arrived = (pieces[0], *(over_z(a, j) for j, a in enumerate(pieces[1:], 1)))
        return next_pieces(positions, arrived, rows, k, after, handed)

    everything, *pieces = first_pieces(positions, weights, rows_in, 3, ())
    rows = (everything, over_x(everything))
    held, *pieces = turn(pieces, 2, ())
    swapped = over_x(held)
    pieces3 = (held, swapped, over_groups(held), over_groups(swapped))
    rates = token_rates(positions, codes, half, (held,))
    queries_in = over_sub(other_half(positions, queries, half, (held,)))
    held, *pieces = turn(pieces, 1, (*pieces3, *rates))
    pieces2 = (held, over_groups(held))
    keep3, *sends = gradients(positions, all_keys, all_values, rates, pieces3, 3, half, (held,), 4)
    held, *pieces = turn(pieces, 0, (keep3, pieces2[1]))
    pieces1 = (held, over_groups(held))
    keep2, send2 = gradients(positions, all_keys, all_values, rates, pieces2, 2, half, (held,), 1)
    in3 = [over_x(a) for a in sends]
    sum3 = added(positions, keep3, in3, (keep2,), cuts=4)
    from1 = over_z(sum3, 1)
    (held,) = turn(pieces, None, (sum3, pieces1[1]))
    pieces0 = (held, over_groups(held))
    keep1, send1 = gradients(positions, all_keys, all_values, rates, pieces1, 1, half, (held,), 1)
    in2 = over_x(send2)
    sum2 = added(positions, keep2, (in2, from1), (keep1,))
    from2 = over_z(sum2, 2)
    keep0, in0, own_w, squares = head_gradients(0, pieces0, (sum2,))
    in1 = over_x(send1)
    sum1 = added(positions, keep1, (in1,), (keep0,))
    from1 = over_z(sum1, 1)
    partial = added(positions, keep0, (from2,), (sum1,), F32, 8)
    grad, sums = total_gradient(positions, partial, (in0, from1))
    renewed = renewed_block(positions, grad, own_w, squares, sums, over_x(sums))

    swapped = over_x(renewed)
    from1, from2 = over_z(renewed, 1), over_z(renewed, 2)
    from3 = over_z(from2, 1)
    matrices = {0: (renewed, swapped), 2: (from2, over_x(from2)), 3: (from3, over_x(from3))}

    def head_output(k, out, late, after):
        out, sent = apply_renewed(positions, queries, queries_in, *matrices[k], k, half, out, late, after)
        return out, (k, over_sub(sent))

    out, late0 = head_output(0, None, (), (from1, from2))
    swapped_late = copied(positions, swapped, (from3, out))
    matrices[1] = (from1, over_z(swapped_late, 1))
    out, late2 = head_output(2, out, (), (swapped_late,))
    out, late1 = head_output(1, out, (late0,), matrices[3])
    out, late3 = head_output(3, out, (late2,), ())
    return place(positions, out, (late1, late3), half)


def solution(mesh):
    seq, sub, groups = mesh.shape["seq"], mesh.shape["sub"], mesh.shape["groups"]

    def on_device(queries, *rest):
        rows, columns = rest[3].shape[1:]
        fits = (groups, seq, sub, queries.shape[0]) == (2, 8, 2, 8) and rows % 32 == 0 and columns == seq * sub * rows and columns % 256 == 0
        return (on_device_fast if fits else on_device_generic)(queries, *rest)

    return jax.shard_map(
        on_device,
        mesh=mesh,
        in_specs=(
            P("head", ("groups", "seq", "sub"), None),
            P("head", ("groups", "seq", "sub"), None),
            P("head", ("groups", "seq", "sub"), None),
            P("head", ("groups", "seq", "sub")),
            P("head", ("seq", "sub"), None),
            P("head", ("seq", "sub"), None),
            P("head", ("seq", "sub"), None),
        ),
        out_specs=P("head", ("groups", "seq", "sub"), None),
        check_vma=False,
    )
```

```python
import functools

import jax
import jax.numpy as jnp
from jax import lax
from jax.experimental import pallas as pl
from jax.experimental.pallas import tpu as pltpu
from jax.sharding import PartitionSpec as P

EPSILON = 1e-06
STEP_SIZE = 0.5
BF16 = jnp.bfloat16
F32 = jnp.float32
VMEM_LIMIT = 64 * 1024 * 1024


def column_squares(matrix):
    return jnp.sum(matrix * matrix, axis=1)


def rescale(moved, col_weight, col_moved):
    return moved * jnp.sqrt((col_weight + EPSILON) / (col_moved + EPSILON))[:, None, :]


def step_scale(col_weight, grad_total):
    return (
        STEP_SIZE * jnp.sqrt(jnp.sum(col_weight, axis=1) + EPSILON) / jnp.sqrt(grad_total + EPSILON)
    )


def apply_fast(queries, gate_b, up_b, down_b):
    query_gate = jnp.einsum("htd,hdf->htf", queries, gate_b, preferred_element_type=jnp.float32)
    query_up = jnp.einsum("htd,hdf->htf", queries, up_b, preferred_element_type=jnp.float32)
    query_hidden = (jax.nn.silu(query_gate) * query_up).astype(jnp.bfloat16)
    return jnp.einsum(
        "htf,hfd->htd", query_hidden, down_b, preferred_element_type=jnp.float32
    ).astype(jnp.bfloat16)


def local_grads(keys, target, gate_b, up_b, down_b):
    gate_pre = jnp.einsum("htd,hdf->htf", keys, gate_b, preferred_element_type=jnp.float32)
    up_pre = jnp.einsum("htd,hdf->htf", keys, up_b, preferred_element_type=jnp.float32)
    sigmoid_gate = jax.nn.sigmoid(gate_pre)
    hidden = (gate_pre * sigmoid_gate * up_pre).astype(jnp.bfloat16)
    back = jnp.einsum("htd,hfd->htf", target, down_b, preferred_element_type=jnp.float32)
    grad_gate_pre = (back * up_pre * sigmoid_gate * (1.0 + gate_pre * (1.0 - sigmoid_gate))).astype(
        jnp.bfloat16
    )
    grad_up_pre = (back * gate_pre * sigmoid_gate).astype(jnp.bfloat16)
    grad_gate = jnp.einsum("htd,htf->hdf", keys, grad_gate_pre, preferred_element_type=jnp.float32)
    grad_up = jnp.einsum("htd,htf->hdf", keys, grad_up_pre, preferred_element_type=jnp.float32)
    grad_down = jnp.einsum("htf,htd->hfd", hidden, target, preferred_element_type=jnp.float32)
    return (grad_gate, grad_up, grad_down)


def on_device_generic(queries, keys, values, lr_codes, fast_gate, fast_up, fast_down):
    token_rates = (lr_codes.astype(jnp.float32) + 1.0) / 16.0
    target = (-token_rates[:, :, None] * values.astype(jnp.float32)).astype(jnp.bfloat16)
    gate_b, up_b, down_b = (
        lax.all_gather(fast_gate.astype(jnp.bfloat16), ("seq", "sub"), axis=1, tiled=True),
        lax.all_gather(fast_up.astype(jnp.bfloat16), ("seq", "sub"), axis=1, tiled=True),
        lax.all_gather(fast_down.astype(jnp.bfloat16), ("seq", "sub"), axis=1, tiled=True),
    )
    grad_gate, grad_up, grad_down = local_grads(keys, target, gate_b, up_b, down_b)
    owned = (
        lax.psum_scatter(grad_gate, ("seq", "sub"), scatter_dimension=1, tiled=True),
        lax.psum_scatter(grad_up, ("seq", "sub"), scatter_dimension=1, tiled=True),
        lax.psum_scatter(grad_down, ("seq", "sub"), scatter_dimension=1, tiled=True),
    )
    weights = (fast_gate, fast_up, fast_down)
    grad_local = jnp.stack(
        [
            jnp.sum(owned[0] * owned[0], axis=(1, 2)),
            jnp.sum(owned[1] * owned[1], axis=(1, 2)),
            jnp.sum(owned[2] * owned[2], axis=(1, 2)),
        ],
        axis=1,
    )
    col_gate, col_up, col_down, grad_totals = lax.psum(
        (column_squares(fast_gate), column_squares(fast_up), column_squares(fast_down), grad_local),
        ("seq", "sub"),
    )
    col_weights = (col_gate, col_up, col_down)
    moved_all = []
    for index in range(3):
        scale = step_scale(col_weights[index], grad_totals[:, index])
        moved_all.append(weights[index] - scale[:, None, None] * owned[index])
    moved_cols = lax.psum(
        (column_squares(moved_all[0]), column_squares(moved_all[1]), column_squares(moved_all[2])),
        ("seq", "sub"),
    )
    renewed = [
        rescale(moved_all[index], col_weights[index], moved_cols[index]).astype(jnp.bfloat16)
        for index in range(3)
    ]
    new_gate, new_up, new_down = (
        lax.all_gather(renewed[0], ("seq", "sub"), axis=1, tiled=True),
        lax.all_gather(renewed[1], ("seq", "sub"), axis=1, tiled=True),
        lax.all_gather(renewed[2], ("seq", "sub"), axis=1, tiled=True),
    )
    return apply_fast(queries, new_gate, new_up, new_down)


def block(shape, index_map):
    return pl.BlockSpec(shape, index_map)


def whole(array):
    return pl.BlockSpec(array.shape, lambda *_: (0,) * array.ndim)


def anywhere():
    return pl.BlockSpec(memory_space=pl.ANY)


def call(body, name, positions, grid, operands, in_specs, out_shapes, out_specs, scratch=(), aliases=None, estimate=None, vmem=VMEM_LIMIT):
    return pl.pallas_call(
        body,
        name=name,
        out_shape=out_shapes,
        grid_spec=pltpu.PrefetchScalarGridSpec(
            num_scalar_prefetch=1,
            grid=grid,
            in_specs=in_specs,
            out_specs=out_specs,
            scratch_shapes=list(scratch),
        ),
        input_output_aliases=aliases or {},
        compiler_params=pltpu.CompilerParams(vmem_limit_bytes=vmem),
        cost_estimate=estimate,
    )(positions, *operands)


def sds(shape, dtype):
    return jax.ShapeDtypeStruct(shape, dtype)


def cost(microseconds):
    return pl.CostEstimate(flops=0, bytes_accessed=int(microseconds * 3e6), transcendentals=0)


def first_pieces(positions, own, received, k, after):
    heads, rows, columns = own[0].shape
    half, width = heads // 2, columns // 2

    def body(pos, *refs):
        mine = pl.ds(pl.multiple_of(pos[0] * rows, rows), rows)
        theirs = pl.ds(pl.multiple_of((1 - pos[0]) * rows, rows), rows)
        everything, sends = refs[-half - 1], refs[-half:]
        for head in range(half):
            for m in range(3):
                everything[head, m, mine, :] = refs[m][head].astype(BF16)
                everything[head, m, theirs, :] = refs[3 + m][head].astype(BF16)
        for j, out_ref in enumerate(sends):
            out_ref[...] = everything[pos[1] ^ (j ^ k)]

    spec = block((half, rows, width), lambda i, pos: (pos[0], 0, pos[3]))
    outs = [sds((half, 3, 2 * rows, width), BF16)] + [sds((3, 2 * rows, width), BF16)] * half
    return call(
        body, "first_pieces", positions, (1,), (*own, *received, *after),
        [spec] * 6 + [anywhere()] * len(after), outs, [whole(o) for o in outs], vmem=60 * 1024 * 1024,
    )


def next_pieces(positions, arrived, rows, k, after, handed=None):
    half = len(arrived)
    more = [] if k is None else list(rows)

    passed = [] if handed is None else [handed]

    def body(pos, *refs):
        held, *sends = refs[half + len(more) + len(after) + len(passed) :]
        for j in range(half):
            held[j] = refs[j][...]
        if more:
            height = rows[0].shape[2]
            for ref, x in ((refs[half], pos[2]), (refs[half + 1], 1 - pos[2])):
                at = pl.ds(pl.multiple_of(x * height, height), height)
                for j in range(half):
                    sends[j][:, at, :] = ref[pos[1] ^ (j ^ k)]

    outs = [sds((half, *arrived[0].shape), BF16)]
    if more:
        outs += [sds((3, 2 * rows[0].shape[2], rows[0].shape[3]), BF16)] * half
    operands = (*arrived, *more)
    others = (*after, *passed)
    aliases = {len(operands) + len(others): len(outs)} if passed else {}
    return call(
        body, "next_pieces", positions, (1,), (*operands, *others),
        [whole(a) for a in operands] + [anywhere()] * len(others),
        outs + [sds(p.shape, p.dtype) for p in passed], [whole(o) for o in outs] + [anywhere() for _ in passed],
        aliases=aliases, estimate=cost(3),
    )


def handed_on(positions, array, after):
    def body(pos, *refs):
        refs[-1][...] = jnp.zeros_like(refs[-1])

    shapes = [sds(array.shape, BF16), sds((8, 128), F32)]
    return call(
        body, "handed_on", positions, (1,), (array, *after), [anywhere()] * (1 + len(after)), shapes,
        [anywhere(), whole(shapes[1])], aliases={1: 0},
    )


def token_rates(positions, codes, half, after):
    tokens = codes[0].shape[1]

    def body(pos, *refs):
        head = pos[0] * half + pl.program_id(0)
        for ref, out_ref in zip(refs, refs[-2:]):
            row = (ref[pl.ds(head, 1), :].astype(F32) + 1.0) / 16.0
            out_ref[0] = jnp.broadcast_to(row, (128, tokens)).T.astype(BF16)

    shape = sds((half, tokens, 128), BF16)
    out = block((1, tokens, 128), lambda i, pos: (i, 0, 0))
    return call(
        body, "token_rates", positions, (half,), (*codes, *after), [whole(c) for c in codes] + [anywhere()] * len(after),
        [shape] * 2, [out] * 2,
    )


def other_half(positions, array, half, after):
    def body(pos, in_ref, *rest):
        rest[-1][...] = in_ref[...]

    _, tokens, columns = array.shape
    spec = block((1, tokens // 2, columns), lambda i, j, pos: ((1 - pos[0]) * half + i, j, 0))
    out = block((1, tokens // 2, columns), lambda i, j, pos: (i, j, 0))
    return call(
        body, "other_half", positions, (half, 2), (array, *after), [spec] + [anywhere()] * len(after),
        sds((half, tokens, columns), BF16), out, estimate=cost(3),
    )


def gradients(positions, keys, values, rates, pieces, k, half, after, cuts):
    z_size, _, piece_rows, width = pieces[0].shape
    tokens, columns = keys[0].shape[1:]
    lanes = rates[0].shape[2]
    rows = columns
    quarter = rows // z_size
    tile = tokens // 2 if tokens % 32 == 0 else tokens
    chunks = 2 * tokens // tile
    last = k == 0
    n_in = 6 + len(pieces) + len(after)

    def body(pos, *refs):
        streams, parts = (refs[0:2], refs[2:4], refs[4:6]), refs[6 : 6 + len(pieces)]
        keep, sends = refs[n_in], refs[n_in + 1 : n_in + 1 + cuts]
        w, key, value, rate, grads, hidden, target, total, rounded, sems_w, sems_in, sems_out = refs[-12:]
        z, x, y = pos[1], pos[2], pos[3]
        mine = pl.ds(pl.multiple_of(x * width, 128), width)
        theirs = pl.ds(pl.multiple_of((1 - x) * width, 128), width)

        places = ((0, y), (0, 1 - y)) if len(parts) == 2 else ((x, y), (1 - x, y), (x, 1 - y), (1 - x, 1 - y))
        weight_copies = []
        for n, (ref, (xx, yy)) in enumerate(zip(parts, places)):
            cols = pl.ds(pl.multiple_of(yy * width, 128), width)
            for j in range(z_size):
                at = pl.ds(pl.multiple_of((z ^ j) * quarter + xx * piece_rows, piece_rows), piece_rows)
                weight_copies.append(pltpu.make_async_copy(ref.at[j], w.at[:, at, cols], sems_w.at[n, j]))
        token_copies = []
        heads = (pos[0] * half + (z ^ k),) * 2 + (z ^ k,)
        for c in range(chunks):
            source, first = divmod(c * tile, tokens)
            here = pl.ds(c * tile, tile)
            there = pl.ds(first, tile)
            token_copies.append([
                pltpu.make_async_copy(pair[source].at[head, there], buffer.at[here], sems_in.at[n, c])
                for n, (pair, head, buffer) in enumerate(zip(streams, heads, (key, value, rate)))
            ])
        for copy in weight_copies + [copy for group in token_copies for copy in group]:
            copy.start()
        for copy in weight_copies:
            copy.wait()

        def own_copy():
            return pltpu.make_async_copy(w.at[:, :, mine], refs[n_in + 1 + cuts], sems_out.at[3, 0])

        def out_copies(m):
            copies = [pltpu.make_async_copy(total.at[m, :, mine], keep.at[m], sems_out.at[m, cuts])]
            for n in range(cuts):
                cut = pl.ds(n * (rows // cuts), rows // cuts)
                copies.append(pltpu.make_async_copy(rounded.at[m, cut], sends[n].at[m], sems_out.at[m, n]))
            return copies

        if last:
            own_copy().start()
            squares = refs[n_in + 2 + cuts]
            for m in range(3):
                full = w[m].astype(F32)
                squares[m : m + 1, :] = jnp.sum(full * full, axis=0, keepdims=True)

        @pl.loop(0, chunks)
        def _(c):
            here = pl.ds(pl.multiple_of(c * tile, tile), tile)
            for n, (pair, head, buffer) in enumerate(zip(streams, heads, (key, value, rate))):
                pltpu.make_async_copy(pair[0].at[head, pl.ds(0, tile)], buffer.at[here], sems_in.at[n, c]).wait()
            tokens_rate = jnp.concatenate([rate[here, :].astype(F32)] * (columns // lanes), axis=1)
            t = (-tokens_rate * value[here, :].astype(F32)).astype(BF16)
            target[here, :] = t
            gate = jnp.dot(key[here, :], w[0], preferred_element_type=F32)
            up = jnp.dot(key[here, :], w[1], preferred_element_type=F32)
            back = lax.dot_general(t, w[2], (((1,), (1,)), ((), ())), preferred_element_type=F32)
            sig = 0.5 * jnp.tanh(0.5 * gate) + 0.5
            silu = gate * sig
            hidden[here, :] = (silu * up).astype(BF16)
            grads[1, here, :] = (back * silu).astype(BF16)
            grads[0, here, :] = (back * up * (sig + silu * (1.0 - sig))).astype(BF16)

        def product(m, a, b):
            total[m] = lax.dot_general(a, b, (((0,), (0,)), ((), ())), preferred_element_type=F32)
            rounded[m] = total[m, :, theirs].astype(BF16)
            for copy in out_copies(m):
                copy.start()

        @pl.loop(0, 2)
        def _(m):
            product(m, key[...], grads[m])

        product(2, hidden[...], target[...])
        for m in range(3):
            for copy in out_copies(m):
                copy.wait()
        if last:
            own_copy().wait()

    outs = [sds((3, rows, width), F32)] + [sds((3, rows // cuts, width), BF16)] * cuts
    out_specs = [anywhere()] * len(outs)
    if last:
        outs += [sds((3, rows, width), BF16), sds((8, columns), F32)]
        out_specs += [anywhere(), whole(outs[-1])]
    operands = (*keys, *values, *rates, *pieces, *after)
    bf16_rows = pltpu.VMEM((2 * tokens, columns), BF16)
    return call(
        body, "gradients", positions, (1,), operands, [anywhere()] * len(operands), outs, out_specs,
        [
            pltpu.VMEM((3, rows, columns), BF16), bf16_rows, bf16_rows, pltpu.VMEM((2 * tokens, lanes), BF16),
            pltpu.VMEM((2, 2 * tokens, columns), BF16), bf16_rows, bf16_rows,
            pltpu.VMEM((3, rows, columns), F32), pltpu.VMEM((3, rows, width), BF16),
            pltpu.SemaphoreType.DMA((len(pieces), z_size)), pltpu.SemaphoreType.DMA((3, chunks)), pltpu.SemaphoreType.DMA((4, cuts + 1)),
        ],
        estimate=pl.CostEstimate(flops=6 * 2 * 2 * tokens * rows * columns, bytes_accessed=14 * 2**20, transcendentals=2 * tokens * columns),
    )


def added(positions, keep, received, after, dtype=BF16, microseconds=1, cuts=1):
    rows = keep.shape[1]

    def body(pos, keep_ref, *refs):
        for m in range(3):
            for c in range(cuts):
                at = pl.ds(c * (rows // cuts), rows // cuts)
                total = keep_ref[m, at, :] + refs[c][m].astype(F32)
                for ref in refs[cuts : len(received)]:
                    total = total + ref[m, at, :].astype(F32)
                refs[-1][m, at, :] = total.astype(dtype)

    operands = (keep, *received)
    shape = sds(keep.shape, dtype)
    specs = [whole(a) for a in operands] + [anywhere()] * len(after)
    return call(body, "added", positions, (1,), (*operands, *after), specs, shape, whole(shape), estimate=cost(microseconds))


def total_gradient(positions, keep, received):
    def body(pos, keep_ref, *refs):
        grad, sums = refs[-2:]
        sums[...] = jnp.zeros_like(sums)
        for m in range(3):
            total = keep_ref[m]
            for ref in refs[:-2]:
                total = total + ref[m].astype(F32)
            grad[m] = total
            columns = jnp.sum(total * total, axis=0, keepdims=True)
            sums[m : m + 1, :] = jnp.broadcast_to(jnp.sum(columns, axis=1, keepdims=True), (1, sums.shape[1]))

    outs = [sds(keep.shape, F32), sds((8, 128), F32)]
    operands = (keep, *received)
    return call(body, "total_gradient", positions, (1,), operands, [whole(a) for a in operands], outs, [whole(o) for o in outs])


def renewed_block(positions, grad, own_w, squares, sums, sums_in):
    width = grad.shape[2]

    def body(pos, g_ref, w_ref, sq_ref, sums_ref, sums_in_ref, out):
        mine = pl.ds(pl.multiple_of(pos[2] * width, 128), width)
        for m in range(3):
            total_g = sums_ref[m : m + 1, :1] + sums_in_ref[m : m + 1, :1]
            total_w = jnp.sum(sq_ref[m : m + 1, :], axis=1, keepdims=True)
            scale = STEP_SIZE * jnp.sqrt(total_w + EPSILON) / jnp.sqrt(total_g + EPSILON)
            moved = w_ref[m].astype(F32) - scale * g_ref[m]
            col_moved = jnp.sum(moved * moved, axis=0, keepdims=True)
            out[m] = (moved * jnp.sqrt((sq_ref[m : m + 1, mine] + EPSILON) / (col_moved + EPSILON))).astype(BF16)

    operands = (grad, own_w, squares, sums, sums_in)
    shape = sds(grad.shape, BF16)
    return call(body, "renewed_block", positions, (1,), operands, [whole(a) for a in operands], shape, whole(shape))


def apply_renewed(positions, queries, queries_in, held, swapped, k, half, out, late, after):
    _, rows, width = held.shape
    columns = 2 * width
    heads, tokens, _ = queries.shape
    tile = tokens // 2 if tokens % 32 == 0 else tokens
    chunks = 2 * tokens // tile
    blocks = [b for _, b in late]
    n_in = 4 + len(blocks) + len(after) + (0 if out is None else 1)

    def body(pos, q0, q1, held_ref, swapped_ref, *refs):
        late_refs = refs[: len(blocks)]
        out_ref, send_ref, w, query, result, brought, sems_in, sems_q, sems_out, sems_late = refs[n_in - 4 :]
        x = pos[2]
        heads_of = (pos[0] * half + (pos[1] ^ k), pos[1] ^ k)
        weights = [
            pltpu.make_async_copy(ref, w.at[:, :, pl.ds(pl.multiple_of(xx * width, 128), width)], sems_in.at[n])
            for n, (ref, xx) in enumerate(((held_ref, x), (swapped_ref, 1 - x)))
        ]
        loads, stores = [], []
        for c in range(chunks):
            source, first = divmod(c * tile, tokens)
            here, there = pl.ds(c * tile, tile), pl.ds(first, tile)
            loads.append(pltpu.make_async_copy((q0, q1)[source].at[heads_of[source], there], query.at[here], sems_q.at[c]))
            to = send_ref.at[there] if source else out_ref.at[heads_of[0], there]
            stores.append(pltpu.make_async_copy(result.at[here], to, sems_out.at[c]))
        late_in = [pltpu.make_async_copy(ref, brought.at[n], sems_late.at[n, 0]) for n, ref in enumerate(late_refs)]
        late_out = [
            pltpu.make_async_copy(brought.at[n], out_ref.at[(1 - pos[0]) * half + (pos[1] ^ late[n][0])], sems_late.at[n, 1])
            for n in range(len(blocks))
        ]
        for copy in weights + loads + late_in:
            copy.start()
        for copy in weights:
            copy.wait()

        for n in range(len(blocks)):
            late_in[n].wait()
            late_out[n].start()
        for copy in loads:
            copy.wait()

        def front(c):
            q = query[c * tile : (c + 1) * tile, :]
            return jnp.dot(q, w[0], preferred_element_type=F32), jnp.dot(q, w[1], preferred_element_type=F32)

        following = front(0)
        for c in range(chunks):
            gate, up = following
            if c + 1 < chunks:
                following = front(c + 1)
            hidden = (gate * (0.5 * jnp.tanh(0.5 * gate) + 0.5) * up).astype(BF16)
            result[c * tile : (c + 1) * tile, :] = jnp.dot(hidden, w[2], preferred_element_type=F32).astype(BF16)
            stores[c].start()
        for copy in stores + late_out:
            copy.wait()

    operands = [queries, queries_in, held, swapped, *blocks, *after]
    aliases = {}
    if out is not None:
        aliases = {1 + len(operands): 0}
        operands.append(out)
    return call(
        body, "apply_renewed", positions, (1,), operands, [anywhere()] * len(operands),
        [sds(queries.shape, BF16), sds((tokens, columns), BF16)], [anywhere()] * 2,
        [
            pltpu.VMEM((3, rows, columns), BF16), pltpu.VMEM((2 * tokens, columns), BF16), pltpu.VMEM((2 * tokens, columns), BF16),
            pltpu.VMEM((max(len(blocks), 1), tokens, columns), BF16),
            pltpu.SemaphoreType.DMA((2,)), pltpu.SemaphoreType.DMA((chunks,)), pltpu.SemaphoreType.DMA((chunks,)),
            pltpu.SemaphoreType.DMA((max(len(blocks), 1), 2)),
        ],
        aliases,
        pl.CostEstimate(flops=3 * 2 * 2 * tokens * rows * columns, bytes_accessed=7 * 2**20, transcendentals=2 * tokens * columns),
    )


def place(positions, out, late, half):
    n = len(late)
    tokens, columns = late[0][1].shape
    cuts = 4 if tokens % 64 == 0 else 1
    tile = tokens // cuts

    def body(pos, *refs):
        out_ref, held, sems_in, sems_out = refs[-4:]
        pairs = []
        for i, (k, _) in enumerate(late):
            head = (1 - pos[0]) * half + (pos[1] ^ k)
            for c in range(cuts):
                at = pl.ds(c * tile, tile)
                pairs.append((
                    pltpu.make_async_copy(refs[i].at[at], held.at[i, at], sems_in.at[i, c]),
                    pltpu.make_async_copy(held.at[i, at], out_ref.at[head, at], sems_out.at[i, c]),
                ))
        for first, _ in pairs:
            first.start()
        for first, second in pairs:
            first.wait()
            second.start()
        for _, second in pairs:
            second.wait()

    return call(
        body, "place", positions, (1,), (*(b for _, b in late), out), [anywhere()] * (n + 1),
        sds(out.shape, BF16), anywhere(),
        [pltpu.VMEM((n, tokens, columns), BF16), pltpu.SemaphoreType.DMA((n, cuts)), pltpu.SemaphoreType.DMA((n, cuts))],
        {1 + n: 0}, cost(1),
    )


def on_device_fast(queries, keys, values, lr_codes, fast_gate, fast_up, fast_down):
    heads, tokens, _ = queries.shape
    half = heads // 2
    core, seq = lax.axis_index("sub"), lax.axis_index("seq")
    positions = jnp.stack([core, seq // 2, seq % 2, lax.axis_index("groups")]).astype(jnp.int32)
    flip = [(0, 1), (1, 0)]

    def over_sub(a):
        return lax.ppermute(a, "sub", flip)

    def over_groups(a):
        return lax.ppermute(a, "groups", flip)

    def over_x(a):
        return lax.ppermute(a, "seq", [(i, i ^ 1) for i in range(8)])

    def over_z(a, j):
        return lax.ppermute(a, "seq", [(i, i ^ (2 * j)) for i in range(8)])

    weights = (fast_gate, fast_up, fast_down)
    rows_in = tuple(over_sub(w) for w in weights)
    all_keys, all_values = (keys, over_sub(keys)), (values, over_sub(values))
    codes = (lr_codes, over_sub(lr_codes))

    def head_gradients(k, pieces, after):
        keep, send, *rest = gradients(positions, all_keys, all_values, rates, pieces, k, half, after, 1)
        return keep, over_x(send), *rest

    def turn(pieces, k, after, handed=None):
        arrived = (pieces[0], *(over_z(a, j) for j, a in enumerate(pieces[1:], 1)))
        return next_pieces(positions, arrived, rows, k, after, handed)

    everything, *pieces = first_pieces(positions, weights, rows_in, 3, ())
    rows = (everything, over_x(everything))
    held, *pieces = turn(pieces, 2, ())
    swapped = over_x(held)
    pieces3 = (held, swapped, over_groups(held), over_groups(swapped))
    rates = token_rates(positions, codes, half, (held,))
    queries_in = over_sub(other_half(positions, queries, half, (held,)))
    held, *pieces = turn(pieces, 1, (*pieces3, *rates))
    pieces2 = (held, over_groups(held))
    keep3, *sends = gradients(positions, all_keys, all_values, rates, pieces3, 3, half, (held,), 4)
    held, *pieces = turn(pieces, 0, (keep3, pieces2[1]))
    pieces1 = (held, over_groups(held))
    keep2, send2 = gradients(positions, all_keys, all_values, rates, pieces2, 2, half, (held,), 1)
    in3 = [over_x(a) for a in sends]
    sum3 = added(positions, keep3, in3, (keep2,), cuts=4)
    from1 = over_z(sum3, 1)
    (held,) = turn(pieces, None, (sum3, pieces1[1]))
    pieces0 = (held, over_groups(held))
    keep1, send1 = gradients(positions, all_keys, all_values, rates, pieces1, 1, half, (held,), 1)
    in2 = over_x(send2)
    sum2 = added(positions, keep2, (in2, from1), (keep1,))
    from2 = over_z(sum2, 2)
    keep0, in0, own_w, squares = head_gradients(0, pieces0, (sum2,))
    in1 = over_x(send1)
    sum1 = added(positions, keep1, (in1,), (keep0,))
    from1 = over_z(sum1, 1)
    partial = added(positions, keep0, (from2,), (sum1,), F32, 8)
    grad, sums = total_gradient(positions, partial, (in0, from1))
    renewed = renewed_block(positions, grad, own_w, squares, sums, over_x(sums))

    swapped = over_x(renewed)
    from1, from2 = over_z(renewed, 1), over_z(renewed, 2)
    from3 = over_z(from2, 1)
    matrices = {0: (renewed, swapped), 2: (from2, over_x(from2)), 3: (from3, over_x(from3))}

    def head_output(k, out, late, after):
        out, sent = apply_renewed(positions, queries, queries_in, *matrices[k], k, half, out, late, after)
        return out, (k, over_sub(sent))

    out, late0 = head_output(0, None, (), (from1, from2))
    swapped_late, _ = handed_on(positions, swapped, (from3, out))
    matrices[1] = (from1, over_z(swapped_late, 1))
    out, late2 = head_output(2, out, (), (swapped_late,))
    out, late1 = head_output(1, out, (late0,), matrices[3])
    out, late3 = head_output(3, out, (late2,), ())
    out = place(positions, out, (late1,), half)
    return place(positions, out, (late3,), half)


def solution(mesh):
    seq, sub, groups = mesh.shape["seq"], mesh.shape["sub"], mesh.shape["groups"]

    def on_device(queries, *rest):
        rows, columns = rest[3].shape[1:]
        fits = (groups, seq, sub, queries.shape[0]) == (2, 8, 2, 8) and rows % 32 == 0 and columns == seq * sub * rows and columns % 256 == 0
        return (on_device_fast if fits else on_device_generic)(queries, *rest)

    return jax.shard_map(
        on_device,
        mesh=mesh,
        in_specs=(
            P("head", ("groups", "seq", "sub"), None),
            P("head", ("groups", "seq", "sub"), None),
            P("head", ("groups", "seq", "sub"), None),
            P("head", ("groups", "seq", "sub")),
            P("head", ("seq", "sub"), None),
            P("head", ("seq", "sub"), None),
            P("head", ("seq", "sub"), None),
        ),
        out_specs=P("head", ("groups", "seq", "sub"), None),
        check_vma=False,
    )
```

```python
import functools

import jax
import jax.numpy as jnp
from jax import lax
from jax.experimental import pallas as pl
from jax.experimental.pallas import tpu as pltpu
from jax.sharding import PartitionSpec as P

EPSILON = 1e-06
STEP_SIZE = 0.5
BF16 = jnp.bfloat16
F32 = jnp.float32
VMEM_LIMIT = 64 * 1024 * 1024


def column_squares(matrix):
    return jnp.sum(matrix * matrix, axis=1)


def rescale(moved, col_weight, col_moved):
    return moved * jnp.sqrt((col_weight + EPSILON) / (col_moved + EPSILON))[:, None, :]


def step_scale(col_weight, grad_total):
    return (
        STEP_SIZE * jnp.sqrt(jnp.sum(col_weight, axis=1) + EPSILON) / jnp.sqrt(grad_total + EPSILON)
    )


def apply_fast(queries, gate_b, up_b, down_b):
    query_gate = jnp.einsum("htd,hdf->htf", queries, gate_b, preferred_element_type=jnp.float32)
    query_up = jnp.einsum("htd,hdf->htf", queries, up_b, preferred_element_type=jnp.float32)
    query_hidden = (jax.nn.silu(query_gate) * query_up).astype(jnp.bfloat16)
    return jnp.einsum(
        "htf,hfd->htd", query_hidden, down_b, preferred_element_type=jnp.float32
    ).astype(jnp.bfloat16)


def local_grads(keys, target, gate_b, up_b, down_b):
    gate_pre = jnp.einsum("htd,hdf->htf", keys, gate_b, preferred_element_type=jnp.float32)
    up_pre = jnp.einsum("htd,hdf->htf", keys, up_b, preferred_element_type=jnp.float32)
    sigmoid_gate = jax.nn.sigmoid(gate_pre)
    hidden = (gate_pre * sigmoid_gate * up_pre).astype(jnp.bfloat16)
    back = jnp.einsum("htd,hfd->htf", target, down_b, preferred_element_type=jnp.float32)
    grad_gate_pre = (back * up_pre * sigmoid_gate * (1.0 + gate_pre * (1.0 - sigmoid_gate))).astype(
        jnp.bfloat16
    )
    grad_up_pre = (back * gate_pre * sigmoid_gate).astype(jnp.bfloat16)
    grad_gate = jnp.einsum("htd,htf->hdf", keys, grad_gate_pre, preferred_element_type=jnp.float32)
    grad_up = jnp.einsum("htd,htf->hdf", keys, grad_up_pre, preferred_element_type=jnp.float32)
    grad_down = jnp.einsum("htf,htd->hfd", hidden, target, preferred_element_type=jnp.float32)
    return (grad_gate, grad_up, grad_down)


def on_device_generic(queries, keys, values, lr_codes, fast_gate, fast_up, fast_down):
    token_rates = (lr_codes.astype(jnp.float32) + 1.0) / 16.0
    target = (-token_rates[:, :, None] * values.astype(jnp.float32)).astype(jnp.bfloat16)
    gate_b, up_b, down_b = (
        lax.all_gather(fast_gate.astype(jnp.bfloat16), ("seq", "sub"), axis=1, tiled=True),
        lax.all_gather(fast_up.astype(jnp.bfloat16), ("seq", "sub"), axis=1, tiled=True),
        lax.all_gather(fast_down.astype(jnp.bfloat16), ("seq", "sub"), axis=1, tiled=True),
    )
    grad_gate, grad_up, grad_down = local_grads(keys, target, gate_b, up_b, down_b)
    owned = (
        lax.psum_scatter(grad_gate, ("seq", "sub"), scatter_dimension=1, tiled=True),
        lax.psum_scatter(grad_up, ("seq", "sub"), scatter_dimension=1, tiled=True),
        lax.psum_scatter(grad_down, ("seq", "sub"), scatter_dimension=1, tiled=True),
    )
    weights = (fast_gate, fast_up, fast_down)
    grad_local = jnp.stack(
        [
            jnp.sum(owned[0] * owned[0], axis=(1, 2)),
            jnp.sum(owned[1] * owned[1], axis=(1, 2)),
            jnp.sum(owned[2] * owned[2], axis=(1, 2)),
        ],
        axis=1,
    )
    col_gate, col_up, col_down, grad_totals = lax.psum(
        (column_squares(fast_gate), column_squares(fast_up), column_squares(fast_down), grad_local),
        ("seq", "sub"),
    )
    col_weights = (col_gate, col_up, col_down)
    moved_all = []
    for index in range(3):
        scale = step_scale(col_weights[index], grad_totals[:, index])
        moved_all.append(weights[index] - scale[:, None, None] * owned[index])
    moved_cols = lax.psum(
        (column_squares(moved_all[0]), column_squares(moved_all[1]), column_squares(moved_all[2])),
        ("seq", "sub"),
    )
    renewed = [
        rescale(moved_all[index], col_weights[index], moved_cols[index]).astype(jnp.bfloat16)
        for index in range(3)
    ]
    new_gate, new_up, new_down = (
        lax.all_gather(renewed[0], ("seq", "sub"), axis=1, tiled=True),
        lax.all_gather(renewed[1], ("seq", "sub"), axis=1, tiled=True),
        lax.all_gather(renewed[2], ("seq", "sub"), axis=1, tiled=True),
    )
    return apply_fast(queries, new_gate, new_up, new_down)


def block(shape, index_map):
    return pl.BlockSpec(shape, index_map)


def whole(array):
    return pl.BlockSpec(array.shape, lambda *_: (0,) * array.ndim)


def anywhere():
    return pl.BlockSpec(memory_space=pl.ANY)


def call(body, name, positions, grid, operands, in_specs, out_shapes, out_specs, scratch=(), aliases=None, estimate=None, vmem=VMEM_LIMIT):
    return pl.pallas_call(
        body,
        name=name,
        out_shape=out_shapes,
        grid_spec=pltpu.PrefetchScalarGridSpec(
            num_scalar_prefetch=1,
            grid=grid,
            in_specs=in_specs,
            out_specs=out_specs,
            scratch_shapes=list(scratch),
        ),
        input_output_aliases=aliases or {},
        compiler_params=pltpu.CompilerParams(vmem_limit_bytes=vmem),
        cost_estimate=estimate,
    )(positions, *operands)


def sds(shape, dtype):
    return jax.ShapeDtypeStruct(shape, dtype)


def cost(microseconds):
    return pl.CostEstimate(flops=0, bytes_accessed=int(microseconds * 3e6), transcendentals=0)


def first_pieces(positions, own, received, k, after):
    heads, rows, columns = own[0].shape
    half, width = heads // 2, columns // 2

    def body(pos, *refs):
        mine = pl.ds(pl.multiple_of(pos[0] * rows, rows), rows)
        theirs = pl.ds(pl.multiple_of((1 - pos[0]) * rows, rows), rows)
        everything, sends = refs[-half - 1], refs[-half:]
        for head in range(half):
            for m in range(3):
                everything[head, m, mine, :] = refs[m][head].astype(BF16)
                everything[head, m, theirs, :] = refs[3 + m][head].astype(BF16)
        for j, out_ref in enumerate(sends):
            out_ref[...] = everything[pos[1] ^ (j ^ k)]

    spec = block((half, rows, width), lambda i, pos: (pos[0], 0, pos[3]))
    outs = [sds((half, 3, 2 * rows, width), BF16)] + [sds((3, 2 * rows, width), BF16)] * half
    return call(
        body, "first_pieces", positions, (1,), (*own, *received, *after),
        [spec] * 6 + [anywhere()] * len(after), outs, [whole(o) for o in outs], vmem=60 * 1024 * 1024,
    )


def next_pieces(positions, arrived, rows, k, after, handed=None):
    half = len(arrived)
    more = [] if k is None else list(rows)

    passed = [] if handed is None else [handed]

    def body(pos, *refs):
        held, *sends = refs[half + len(more) + len(after) + len(passed) :]
        for j in range(half):
            held[j] = refs[j][...]
        if more:
            height = rows[0].shape[2]
            for ref, x in ((refs[half], pos[2]), (refs[half + 1], 1 - pos[2])):
                at = pl.ds(pl.multiple_of(x * height, height), height)
                for j in range(half):
                    sends[j][:, at, :] = ref[pos[1] ^ (j ^ k)]

    outs = [sds((half, *arrived[0].shape), BF16)]
    if more:
        outs += [sds((3, 2 * rows[0].shape[2], rows[0].shape[3]), BF16)] * half
    operands = (*arrived, *more)
    others = (*after, *passed)
    aliases = {len(operands) + len(others): len(outs)} if passed else {}
    return call(
        body, "next_pieces", positions, (1,), (*operands, *others),
        [whole(a) for a in operands] + [anywhere()] * len(others),
        outs + [sds(p.shape, p.dtype) for p in passed], [whole(o) for o in outs] + [anywhere() for _ in passed],
        aliases=aliases, estimate=cost(3),
    )


def handed_on(positions, array, after):
    def body(pos, *refs):
        refs[-1][...] = jnp.zeros_like(refs[-1])

    shapes = [sds(array.shape, BF16), sds((8, 128), F32)]
    return call(
        body, "handed_on", positions, (1,), (array, *after), [anywhere()] * (1 + len(after)), shapes,
        [anywhere(), whole(shapes[1])], aliases={1: 0},
    )


def token_rates(positions, codes, half, after):
    tokens = codes[0].shape[1]

    def body(pos, *refs):
        head = pos[0] * half + pl.program_id(0)
        for ref, out_ref in zip(refs, refs[-2:]):
            row = (ref[pl.ds(head, 1), :].astype(F32) + 1.0) / 16.0
            out_ref[0] = jnp.broadcast_to(row, (128, tokens)).T.astype(BF16)

    shape = sds((half, tokens, 128), BF16)
    out = block((1, tokens, 128), lambda i, pos: (i, 0, 0))
    return call(
        body, "token_rates", positions, (half,), (*codes, *after), [whole(c) for c in codes] + [anywhere()] * len(after),
        [shape] * 2, [out] * 2,
    )


def other_half(positions, array, half, after):
    def body(pos, in_ref, *rest):
        rest[-1][...] = in_ref[...]

    _, tokens, columns = array.shape
    spec = block((1, tokens // 2, columns), lambda i, j, pos: ((1 - pos[0]) * half + i, j, 0))
    out = block((1, tokens // 2, columns), lambda i, j, pos: (i, j, 0))
    return call(
        body, "other_half", positions, (half, 2), (array, *after), [spec] + [anywhere()] * len(after),
        sds((half, tokens, columns), BF16), out, estimate=cost(3),
    )


def gradients(positions, keys, values, rates, pieces, k, half, after, cuts):
    z_size, _, piece_rows, width = pieces[0].shape
    tokens, columns = keys[0].shape[1:]
    lanes = rates[0].shape[2]
    rows = columns
    quarter = rows // z_size
    tile = tokens // 2 if tokens % 32 == 0 else tokens
    chunks = 2 * tokens // tile
    last = k == 0
    n_in = 6 + len(pieces) + len(after)

    def body(pos, *refs):
        streams, parts = (refs[0:2], refs[2:4], refs[4:6]), refs[6 : 6 + len(pieces)]
        keep, sends = refs[n_in], refs[n_in + 1 : n_in + 1 + cuts]
        w, key, value, rate, grads, hidden, target, total, rounded, sems_w, sems_in, sems_out = refs[-12:]
        z, x, y = pos[1], pos[2], pos[3]
        mine = pl.ds(pl.multiple_of(x * width, 128), width)
        theirs = pl.ds(pl.multiple_of((1 - x) * width, 128), width)

        places = ((0, y), (0, 1 - y)) if len(parts) == 2 else ((x, y), (1 - x, y), (x, 1 - y), (1 - x, 1 - y))
        weight_copies = []
        for n, (ref, (xx, yy)) in enumerate(zip(parts, places)):
            cols = pl.ds(pl.multiple_of(yy * width, 128), width)
            for j in range(z_size):
                at = pl.ds(pl.multiple_of((z ^ j) * quarter + xx * piece_rows, piece_rows), piece_rows)
                weight_copies.append(pltpu.make_async_copy(ref.at[j], w.at[:, at, cols], sems_w.at[n, j]))
        token_copies = []
        heads = (pos[0] * half + (z ^ k),) * 2 + (z ^ k,)
        for c in range(chunks):
            source, first = divmod(c * tile, tokens)
            here = pl.ds(c * tile, tile)
            there = pl.ds(first, tile)
            token_copies.append([
                pltpu.make_async_copy(pair[source].at[head, there], buffer.at[here], sems_in.at[n, c])
                for n, (pair, head, buffer) in enumerate(zip(streams, heads, (key, value, rate)))
            ])
        for copy in weight_copies + [copy for group in token_copies for copy in group]:
            copy.start()
        for copy in weight_copies:
            copy.wait()

        def own_copy():
            return pltpu.make_async_copy(w.at[:, :, mine], refs[n_in + 1 + cuts], sems_out.at[3, 0])

        def out_copies(m):
            copies = [pltpu.make_async_copy(total.at[m, :, mine], keep.at[m], sems_out.at[m, cuts])]
            for n in range(cuts):
                cut = pl.ds(n * (rows // cuts), rows // cuts)
                copies.append(pltpu.make_async_copy(rounded.at[m, cut], sends[n].at[m], sems_out.at[m, n]))
            return copies

        if last:
            own_copy().start()

        @pl.loop(0, chunks)
        def _(c):
            here = pl.ds(pl.multiple_of(c * tile, tile), tile)
            for n, (pair, head, buffer) in enumerate(zip(streams, heads, (key, value, rate))):
                pltpu.make_async_copy(pair[0].at[head, pl.ds(0, tile)], buffer.at[here], sems_in.at[n, c]).wait()
            tokens_rate = jnp.concatenate([rate[here, :].astype(F32)] * (columns // lanes), axis=1)
            t = (-tokens_rate * value[here, :].astype(F32)).astype(BF16)
            target[here, :] = t
            gate = jnp.dot(key[here, :], w[0], preferred_element_type=F32)
            up = jnp.dot(key[here, :], w[1], preferred_element_type=F32)
            back = lax.dot_general(t, w[2], (((1,), (1,)), ((), ())), preferred_element_type=F32)
            sig = 0.5 * jnp.tanh(0.5 * gate) + 0.5
            silu = gate * sig
            hidden[here, :] = (silu * up).astype(BF16)
            grads[1, here, :] = (back * silu).astype(BF16)
            grads[0, here, :] = (back * up * (sig + silu * (1.0 - sig))).astype(BF16)

        def product(m, a, b):
            total[m] = lax.dot_general(a, b, (((0,), (0,)), ((), ())), preferred_element_type=F32)
            rounded[m] = total[m, :, theirs].astype(BF16)
            for copy in out_copies(m):
                copy.start()

        @pl.loop(0, 2)
        def _(m):
            product(m, key[...], grads[m])

        if last:
            squares = refs[n_in + 2 + cuts]
            for m in range(3):
                full = w[m].astype(F32)
                squares[m : m + 1, :] = jnp.sum(full * full, axis=0, keepdims=True)
        product(2, hidden[...], target[...])
        for m in range(3):
            for copy in out_copies(m):
                copy.wait()
        if last:
            own_copy().wait()

    outs = [sds((3, rows, width), F32)] + [sds((3, rows // cuts, width), BF16)] * cuts
    out_specs = [anywhere()] * len(outs)
    if last:
        outs += [sds((3, rows, width), BF16), sds((8, columns), F32)]
        out_specs += [anywhere(), whole(outs[-1])]
    operands = (*keys, *values, *rates, *pieces, *after)
    bf16_rows = pltpu.VMEM((2 * tokens, columns), BF16)
    return call(
        body, "gradients", positions, (1,), operands, [anywhere()] * len(operands), outs, out_specs,
        [
            pltpu.VMEM((3, rows, columns), BF16), bf16_rows, bf16_rows, pltpu.VMEM((2 * tokens, lanes), BF16),
            pltpu.VMEM((2, 2 * tokens, columns), BF16), bf16_rows, bf16_rows,
            pltpu.VMEM((3, rows, columns), F32), pltpu.VMEM((3, rows, width), BF16),
            pltpu.SemaphoreType.DMA((len(pieces), z_size)), pltpu.SemaphoreType.DMA((3, chunks)), pltpu.SemaphoreType.DMA((4, cuts + 1)),
        ],
        estimate=pl.CostEstimate(flops=6 * 2 * 2 * tokens * rows * columns, bytes_accessed=14 * 2**20, transcendentals=2 * tokens * columns),
    )


def added(positions, keep, received, after, dtype=BF16, microseconds=1, cuts=1):
    rows = keep.shape[1]

    def body(pos, keep_ref, *refs):
        for m in range(3):
            for c in range(cuts):
                at = pl.ds(c * (rows // cuts), rows // cuts)
                total = keep_ref[m, at, :] + refs[c][m].astype(F32)
                for ref in refs[cuts : len(received)]:
                    total = total + ref[m, at, :].astype(F32)
                refs[-1][m, at, :] = total.astype(dtype)

    operands = (keep, *received)
    shape = sds(keep.shape, dtype)
    specs = [whole(a) for a in operands] + [anywhere()] * len(after)
    return call(body, "added", positions, (1,), (*operands, *after), specs, shape, whole(shape), estimate=cost(microseconds))


def total_gradient(positions, keep, received):
    def body(pos, keep_ref, *refs):
        grad, sums = refs[-2:]
        sums[...] = jnp.zeros_like(sums)
        for m in range(3):
            total = keep_ref[m]
            for ref in refs[:-2]:
                total = total + ref[m].astype(F32)
            grad[m] = total
            columns = jnp.sum(total * total, axis=0, keepdims=True)
            sums[m : m + 1, :] = jnp.broadcast_to(jnp.sum(columns, axis=1, keepdims=True), (1, sums.shape[1]))

    outs = [sds(keep.shape, F32), sds((8, 128), F32)]
    operands = (keep, *received)
    return call(body, "total_gradient", positions, (1,), operands, [whole(a) for a in operands], outs, [whole(o) for o in outs])


def renewed_block(positions, grad, own_w, squares, sums, sums_in):
    width = grad.shape[2]

    def body(pos, g_ref, w_ref, sq_ref, sums_ref, sums_in_ref, out):
        mine = pl.ds(pl.multiple_of(pos[2] * width, 128), width)
        for m in range(3):
            total_g = sums_ref[m : m + 1, :1] + sums_in_ref[m : m + 1, :1]
            total_w = jnp.sum(sq_ref[m : m + 1, :], axis=1, keepdims=True)
            scale = STEP_SIZE * jnp.sqrt(total_w + EPSILON) / jnp.sqrt(total_g + EPSILON)
            moved = w_ref[m].astype(F32) - scale * g_ref[m]
            col_moved = jnp.sum(moved * moved, axis=0, keepdims=True)
            out[m] = (moved * jnp.sqrt((sq_ref[m : m + 1, mine] + EPSILON) / (col_moved + EPSILON))).astype(BF16)

    operands = (grad, own_w, squares, sums, sums_in)
    shape = sds(grad.shape, BF16)
    return call(body, "renewed_block", positions, (1,), operands, [whole(a) for a in operands], shape, whole(shape))


def apply_renewed(positions, queries, queries_in, held, swapped, k, half, out, late, after):
    _, rows, width = held.shape
    columns = 2 * width
    heads, tokens, _ = queries.shape
    tile = tokens // 2 if tokens % 32 == 0 else tokens
    chunks = 2 * tokens // tile
    blocks = [b for _, b in late]
    n_in = 4 + len(blocks) + len(after) + (0 if out is None else 1)

    def body(pos, q0, q1, held_ref, swapped_ref, *refs):
        late_refs = refs[: len(blocks)]
        out_ref, send_ref, w, query, result, brought, sems_in, sems_q, sems_out, sems_late = refs[n_in - 4 :]
        x = pos[2]
        heads_of = (pos[0] * half + (pos[1] ^ k), pos[1] ^ k)
        weights = [
            pltpu.make_async_copy(ref, w.at[:, :, pl.ds(pl.multiple_of(xx * width, 128), width)], sems_in.at[n])
            for n, (ref, xx) in enumerate(((held_ref, x), (swapped_ref, 1 - x)))
        ]
        loads, stores = [], []
        for c in range(chunks):
            source, first = divmod(c * tile, tokens)
            here, there = pl.ds(c * tile, tile), pl.ds(first, tile)
            loads.append(pltpu.make_async_copy((q0, q1)[source].at[heads_of[source], there], query.at[here], sems_q.at[c]))
            to = send_ref.at[there] if source else out_ref.at[heads_of[0], there]
            stores.append(pltpu.make_async_copy(result.at[here], to, sems_out.at[c]))
        late_in = [pltpu.make_async_copy(ref, brought.at[n], sems_late.at[n, 0]) for n, ref in enumerate(late_refs)]
        late_out = [
            pltpu.make_async_copy(brought.at[n], out_ref.at[(1 - pos[0]) * half + (pos[1] ^ late[n][0])], sems_late.at[n, 1])
            for n in range(len(blocks))
        ]
        for copy in weights + loads + late_in:
            copy.start()
        for copy in weights:
            copy.wait()

        for copy in loads:
            copy.wait()

        def front(c):
            q = query[c * tile : (c + 1) * tile, :]
            return jnp.dot(q, w[0], preferred_element_type=F32), jnp.dot(q, w[1], preferred_element_type=F32)

        following = front(0)
        for c in range(chunks):
            gate, up = following
            if c + 1 < chunks:
                following = front(c + 1)
            hidden = (gate * (0.5 * jnp.tanh(0.5 * gate) + 0.5) * up).astype(BF16)
            result[c * tile : (c + 1) * tile, :] = jnp.dot(hidden, w[2], preferred_element_type=F32).astype(BF16)
            stores[c].start()
            if c == 0:
                for n in range(len(blocks)):
                    late_in[n].wait()
                    late_out[n].start()
        for copy in stores + late_out:
            copy.wait()

    operands = [queries, queries_in, held, swapped, *blocks, *after]
    aliases = {}
    if out is not None:
        aliases = {1 + len(operands): 0}
        operands.append(out)
    return call(
        body, "apply_renewed", positions, (1,), operands, [anywhere()] * len(operands),
        [sds(queries.shape, BF16), sds((tokens, columns), BF16)], [anywhere()] * 2,
        [
            pltpu.VMEM((3, rows, columns), BF16), pltpu.VMEM((2 * tokens, columns), BF16), pltpu.VMEM((2 * tokens, columns), BF16),
            pltpu.VMEM((max(len(blocks), 1), tokens, columns), BF16),
            pltpu.SemaphoreType.DMA((2,)), pltpu.SemaphoreType.DMA((chunks,)), pltpu.SemaphoreType.DMA((chunks,)),
            pltpu.SemaphoreType.DMA((max(len(blocks), 1), 2)),
        ],
        aliases,
        pl.CostEstimate(flops=3 * 2 * 2 * tokens * rows * columns, bytes_accessed=7 * 2**20, transcendentals=2 * tokens * columns),
    )


def place(positions, out, late, half):
    n = len(late)
    tokens, columns = late[0][1].shape
    cuts = 4 if tokens % 64 == 0 else 1
    tile = tokens // cuts

    def body(pos, *refs):
        out_ref, held, sems_in, sems_out = refs[-4:]
        pairs = []
        for i, (k, _) in enumerate(late):
            head = (1 - pos[0]) * half + (pos[1] ^ k)
            for c in range(cuts):
                at = pl.ds(c * tile, tile)
                pairs.append((
                    pltpu.make_async_copy(refs[i].at[at], held.at[i, at], sems_in.at[i, c]),
                    pltpu.make_async_copy(held.at[i, at], out_ref.at[head, at], sems_out.at[i, c]),
                ))
        for first, _ in pairs:
            first.start()
        for first, second in pairs:
            first.wait()
            second.start()
        for _, second in pairs:
            second.wait()

    return call(
        body, "place", positions, (1,), (*(b for _, b in late), out), [anywhere()] * (n + 1),
        sds(out.shape, BF16), anywhere(),
        [pltpu.VMEM((n, tokens, columns), BF16), pltpu.SemaphoreType.DMA((n, cuts)), pltpu.SemaphoreType.DMA((n, cuts))],
        {1 + n: 0}, cost(1),
    )


def on_device_fast(queries, keys, values, lr_codes, fast_gate, fast_up, fast_down):
    heads, tokens, _ = queries.shape
    half = heads // 2
    core, seq = lax.axis_index("sub"), lax.axis_index("seq")
    positions = jnp.stack([core, seq // 2, seq % 2, lax.axis_index("groups")]).astype(jnp.int32)
    flip = [(0, 1), (1, 0)]

    def over_sub(a):
        return lax.ppermute(a, "sub", flip)

    def over_groups(a):
        return lax.ppermute(a, "groups", flip)

    def over_x(a):
        return lax.ppermute(a, "seq", [(i, i ^ 1) for i in range(8)])

    def over_z(a, j):
        return lax.ppermute(a, "seq", [(i, i ^ (2 * j)) for i in range(8)])

    weights = (fast_gate, fast_up, fast_down)
    rows_in = tuple(over_sub(w) for w in weights)
    all_keys, all_values = (keys, over_sub(keys)), (values, over_sub(values))
    codes = (lr_codes, over_sub(lr_codes))

    def head_gradients(k, pieces, after):
        keep, send, *rest = gradients(positions, all_keys, all_values, rates, pieces, k, half, after, 1)
        return keep, over_x(send), *rest

    def turn(pieces, k, after, handed=None):
        arrived = (pieces[0], *(over_z(a, j) for j, a in enumerate(pieces[1:], 1)))
        return next_pieces(positions, arrived, rows, k, after, handed)

    everything, *pieces = first_pieces(positions, weights, rows_in, 3, ())
    rows = (everything, over_x(everything))
    held, *pieces = turn(pieces, 2, ())
    swapped = over_x(held)
    pieces3 = (held, swapped, over_groups(held), over_groups(swapped))
    rates = token_rates(positions, codes, half, (held,))
    queries_in = over_sub(other_half(positions, queries, half, (held,)))
    held, *pieces = turn(pieces, 1, (*pieces3, *rates))
    pieces2 = (held, over_groups(held))
    keep3, *sends = gradients(positions, all_keys, all_values, rates, pieces3, 3, half, (held,), 4)
    held, *pieces = turn(pieces, 0, (keep3, pieces2[1]))
    pieces1 = (held, over_groups(held))
    keep2, send2 = gradients(positions, all_keys, all_values, rates, pieces2, 2, half, (held,), 1)
    in3 = [over_x(a) for a in sends]
    sum3 = added(positions, keep3, in3, (keep2,), cuts=4)
    from1 = over_z(sum3, 1)
    (held,) = turn(pieces, None, (sum3, pieces1[1]))
    pieces0 = (held, over_groups(held))
    keep1, send1 = gradients(positions, all_keys, all_values, rates, pieces1, 1, half, (held,), 1)
    in2 = over_x(send2)
    sum2 = added(positions, keep2, (in2, from1), (keep1,))
    from2 = over_z(sum2, 2)
    keep0, in0, own_w, squares = head_gradients(0, pieces0, (sum2,))
    in1 = over_x(send1)
    sum1 = added(positions, keep1, (in1,), (keep0,))
    from1 = over_z(sum1, 1)
    partial = added(positions, keep0, (from2,), (sum1,), F32, 8)
    grad, sums = total_gradient(positions, partial, (in0, from1))
    renewed = renewed_block(positions, grad, own_w, squares, sums, over_x(sums))

    swapped = over_x(renewed)
    from1, from2 = over_z(renewed, 1), over_z(renewed, 2)
    from3 = over_z(from2, 1)
    matrices = {0: (renewed, swapped), 2: (from2, over_x(from2)), 3: (from3, over_x(from3))}

    def head_output(k, out, late, after):
        out, sent = apply_renewed(positions, queries, queries_in, *matrices[k], k, half, out, late, after)
        return out, (k, over_sub(sent))

    out, late0 = head_output(0, None, (), (from1, from2))
    swapped_late, _ = handed_on(positions, swapped, (from3, out))
    matrices[1] = (from1, over_z(swapped_late, 1))
    out, late2 = head_output(2, out, (), (swapped_late,))
    out, late1 = head_output(1, out, (late0,), matrices[3])
    out, late3 = head_output(3, out, (late2,), ())
    out = place(positions, out, (late1,), half)
    return place(positions, out, (late3,), half)


def solution(mesh):
    seq, sub, groups = mesh.shape["seq"], mesh.shape["sub"], mesh.shape["groups"]

    def on_device(queries, *rest):
        rows, columns = rest[3].shape[1:]
        fits = (groups, seq, sub, queries.shape[0]) == (2, 8, 2, 8) and rows % 32 == 0 and columns == seq * sub * rows and columns % 256 == 0
        return (on_device_fast if fits else on_device_generic)(queries, *rest)

    return jax.shard_map(
        on_device,
        mesh=mesh,
        in_specs=(
            P("head", ("groups", "seq", "sub"), None),
            P("head", ("groups", "seq", "sub"), None),
            P("head", ("groups", "seq", "sub"), None),
            P("head", ("groups", "seq", "sub")),
            P("head", ("seq", "sub"), None),
            P("head", ("seq", "sub"), None),
            P("head", ("seq", "sub"), None),
        ),
        out_specs=P("head", ("groups", "seq", "sub"), None),
        check_vma=False,
    )
```

```python
import functools

import jax
import jax.numpy as jnp
from jax import lax
from jax.experimental import pallas as pl
from jax.experimental.pallas import tpu as pltpu
from jax.sharding import PartitionSpec as P

EPSILON = 1e-06
STEP_SIZE = 0.5
BF16 = jnp.bfloat16
F32 = jnp.float32
VMEM_LIMIT = 64 * 1024 * 1024


def column_squares(matrix):
    return jnp.sum(matrix * matrix, axis=1)


def rescale(moved, col_weight, col_moved):
    return moved * jnp.sqrt((col_weight + EPSILON) / (col_moved + EPSILON))[:, None, :]


def step_scale(col_weight, grad_total):
    return (
        STEP_SIZE * jnp.sqrt(jnp.sum(col_weight, axis=1) + EPSILON) / jnp.sqrt(grad_total + EPSILON)
    )


def apply_fast(queries, gate_b, up_b, down_b):
    query_gate = jnp.einsum("htd,hdf->htf", queries, gate_b, preferred_element_type=jnp.float32)
    query_up = jnp.einsum("htd,hdf->htf", queries, up_b, preferred_element_type=jnp.float32)
    query_hidden = (jax.nn.silu(query_gate) * query_up).astype(jnp.bfloat16)
    return jnp.einsum(
        "htf,hfd->htd", query_hidden, down_b, preferred_element_type=jnp.float32
    ).astype(jnp.bfloat16)


def local_grads(keys, target, gate_b, up_b, down_b):
    gate_pre = jnp.einsum("htd,hdf->htf", keys, gate_b, preferred_element_type=jnp.float32)
    up_pre = jnp.einsum("htd,hdf->htf", keys, up_b, preferred_element_type=jnp.float32)
    sigmoid_gate = jax.nn.sigmoid(gate_pre)
    hidden = (gate_pre * sigmoid_gate * up_pre).astype(jnp.bfloat16)
    back = jnp.einsum("htd,hfd->htf", target, down_b, preferred_element_type=jnp.float32)
    grad_gate_pre = (back * up_pre * sigmoid_gate * (1.0 + gate_pre * (1.0 - sigmoid_gate))).astype(
        jnp.bfloat16
    )
    grad_up_pre = (back * gate_pre * sigmoid_gate).astype(jnp.bfloat16)
    grad_gate = jnp.einsum("htd,htf->hdf", keys, grad_gate_pre, preferred_element_type=jnp.float32)
    grad_up = jnp.einsum("htd,htf->hdf", keys, grad_up_pre, preferred_element_type=jnp.float32)
    grad_down = jnp.einsum("htf,htd->hfd", hidden, target, preferred_element_type=jnp.float32)
    return (grad_gate, grad_up, grad_down)


def on_device_generic(queries, keys, values, lr_codes, fast_gate, fast_up, fast_down):
    token_rates = (lr_codes.astype(jnp.float32) + 1.0) / 16.0
    target = (-token_rates[:, :, None] * values.astype(jnp.float32)).astype(jnp.bfloat16)
    gate_b, up_b, down_b = (
        lax.all_gather(fast_gate.astype(jnp.bfloat16), ("seq", "sub"), axis=1, tiled=True),
        lax.all_gather(fast_up.astype(jnp.bfloat16), ("seq", "sub"), axis=1, tiled=True),
        lax.all_gather(fast_down.astype(jnp.bfloat16), ("seq", "sub"), axis=1, tiled=True),
    )
    grad_gate, grad_up, grad_down = local_grads(keys, target, gate_b, up_b, down_b)
    owned = (
        lax.psum_scatter(grad_gate, ("seq", "sub"), scatter_dimension=1, tiled=True),
        lax.psum_scatter(grad_up, ("seq", "sub"), scatter_dimension=1, tiled=True),
        lax.psum_scatter(grad_down, ("seq", "sub"), scatter_dimension=1, tiled=True),
    )
    weights = (fast_gate, fast_up, fast_down)
    grad_local = jnp.stack(
        [
            jnp.sum(owned[0] * owned[0], axis=(1, 2)),
            jnp.sum(owned[1] * owned[1], axis=(1, 2)),
            jnp.sum(owned[2] * owned[2], axis=(1, 2)),
        ],
        axis=1,
    )
    col_gate, col_up, col_down, grad_totals = lax.psum(
        (column_squares(fast_gate), column_squares(fast_up), column_squares(fast_down), grad_local),
        ("seq", "sub"),
    )
    col_weights = (col_gate, col_up, col_down)
    moved_all = []
    for index in range(3):
        scale = step_scale(col_weights[index], grad_totals[:, index])
        moved_all.append(weights[index] - scale[:, None, None] * owned[index])
    moved_cols = lax.psum(
        (column_squares(moved_all[0]), column_squares(moved_all[1]), column_squares(moved_all[2])),
        ("seq", "sub"),
    )
    renewed = [
        rescale(moved_all[index], col_weights[index], moved_cols[index]).astype(jnp.bfloat16)
        for index in range(3)
    ]
    new_gate, new_up, new_down = (
        lax.all_gather(renewed[0], ("seq", "sub"), axis=1, tiled=True),
        lax.all_gather(renewed[1], ("seq", "sub"), axis=1, tiled=True),
        lax.all_gather(renewed[2], ("seq", "sub"), axis=1, tiled=True),
    )
    return apply_fast(queries, new_gate, new_up, new_down)


def block(shape, index_map):
    return pl.BlockSpec(shape, index_map)


def whole(array):
    return pl.BlockSpec(array.shape, lambda *_: (0,) * array.ndim)


def anywhere():
    return pl.BlockSpec(memory_space=pl.ANY)


def call(body, name, positions, grid, operands, in_specs, out_shapes, out_specs, scratch=(), aliases=None, estimate=None, vmem=VMEM_LIMIT):
    return pl.pallas_call(
        body,
        name=name,
        out_shape=out_shapes,
        grid_spec=pltpu.PrefetchScalarGridSpec(
            num_scalar_prefetch=1,
            grid=grid,
            in_specs=in_specs,
            out_specs=out_specs,
            scratch_shapes=list(scratch),
        ),
        input_output_aliases=aliases or {},
        compiler_params=pltpu.CompilerParams(vmem_limit_bytes=vmem),
        cost_estimate=estimate,
    )(positions, *operands)


def sds(shape, dtype):
    return jax.ShapeDtypeStruct(shape, dtype)


def cost(microseconds):
    return pl.CostEstimate(flops=0, bytes_accessed=int(microseconds * 3e6), transcendentals=0)


def first_pieces(positions, own, received, k, after):
    heads, rows, columns = own[0].shape
    half, width = heads // 2, columns // 2

    def body(pos, *refs):
        mine = pl.ds(pl.multiple_of(pos[0] * rows, rows), rows)
        theirs = pl.ds(pl.multiple_of((1 - pos[0]) * rows, rows), rows)
        everything, sends = refs[-half - 1], refs[-half:]
        for head in range(half):
            for m in range(3):
                everything[head, m, mine, :] = refs[m][head].astype(BF16)
                everything[head, m, theirs, :] = refs[3 + m][head].astype(BF16)
        for j, out_ref in enumerate(sends):
            out_ref[...] = everything[pos[1] ^ (j ^ k)]

    spec = block((half, rows, width), lambda i, pos: (pos[0], 0, pos[3]))
    outs = [sds((half, 3, 2 * rows, width), BF16)] + [sds((3, 2 * rows, width), BF16)] * half
    return call(
        body, "first_pieces", positions, (1,), (*own, *received, *after),
        [spec] * 6 + [anywhere()] * len(after), outs, [whole(o) for o in outs], vmem=60 * 1024 * 1024,
    )


def next_pieces(positions, arrived, rows, k, after, handed=None):
    half = len(arrived)
    more = [] if k is None else list(rows)

    passed = [] if handed is None else [handed]

    def body(pos, *refs):
        held, *sends = refs[half + len(more) + len(after) + len(passed) :]
        for j in range(half):
            held[j] = refs[j][...]
        if more:
            height = rows[0].shape[2]
            for ref, x in ((refs[half], pos[2]), (refs[half + 1], 1 - pos[2])):
                at = pl.ds(pl.multiple_of(x * height, height), height)
                for j in range(half):
                    sends[j][:, at, :] = ref[pos[1] ^ (j ^ k)]

    outs = [sds((half, *arrived[0].shape), BF16)]
    if more:
        outs += [sds((3, 2 * rows[0].shape[2], rows[0].shape[3]), BF16)] * half
    operands = (*arrived, *more)
    others = (*after, *passed)
    aliases = {len(operands) + len(others): len(outs)} if passed else {}
    return call(
        body, "next_pieces", positions, (1,), (*operands, *others),
        [whole(a) for a in operands] + [anywhere()] * len(others),
        outs + [sds(p.shape, p.dtype) for p in passed], [whole(o) for o in outs] + [anywhere() for _ in passed],
        aliases=aliases, estimate=cost(3),
    )


def handed_on(positions, array, after):
    def body(pos, *refs):
        refs[-1][...] = jnp.zeros_like(refs[-1])

    shapes = [sds(array.shape, BF16), sds((8, 128), F32)]
    return call(
        body, "handed_on", positions, (1,), (array, *after), [anywhere()] * (1 + len(after)), shapes,
        [anywhere(), whole(shapes[1])], aliases={1: 0},
    )


def token_rates(positions, codes, half, after):
    tokens = codes[0].shape[1]

    def body(pos, *refs):
        head = pos[0] * half + pl.program_id(0)
        for ref, out_ref in zip(refs, refs[-2:]):
            row = (ref[pl.ds(head, 1), :].astype(F32) + 1.0) / 16.0
            out_ref[0] = jnp.broadcast_to(row, (128, tokens)).T.astype(BF16)

    shape = sds((half, tokens, 128), BF16)
    out = block((1, tokens, 128), lambda i, pos: (i, 0, 0))
    return call(
        body, "token_rates", positions, (half,), (*codes, *after), [whole(c) for c in codes] + [anywhere()] * len(after),
        [shape] * 2, [out] * 2,
    )


def other_half(positions, array, half, after):
    def body(pos, in_ref, *rest):
        rest[-1][...] = in_ref[...]

    _, tokens, columns = array.shape
    spec = block((1, tokens // 2, columns), lambda i, j, pos: ((1 - pos[0]) * half + i, j, 0))
    out = block((1, tokens // 2, columns), lambda i, j, pos: (i, j, 0))
    return call(
        body, "other_half", positions, (half, 2), (array, *after), [spec] + [anywhere()] * len(after),
        sds((half, tokens, columns), BF16), out, estimate=cost(3),
    )


def gradients(positions, keys, values, rates, pieces, k, half, after, cuts):
    z_size, _, piece_rows, width = pieces[0].shape
    tokens, columns = keys[0].shape[1:]
    lanes = rates[0].shape[2]
    rows = columns
    quarter = rows // z_size
    tile = tokens // 2 if tokens % 32 == 0 else tokens
    chunks = 2 * tokens // tile
    last = k == 0
    n_in = 6 + len(pieces) + len(after)

    def body(pos, *refs):
        streams, parts = (refs[0:2], refs[2:4], refs[4:6]), refs[6 : 6 + len(pieces)]
        keep, sends = refs[n_in], refs[n_in + 1 : n_in + 1 + cuts]
        w, key, value, rate, grads, hidden, target, total, rounded, sems_w, sems_in, sems_out = refs[-12:]
        z, x, y = pos[1], pos[2], pos[3]
        mine = pl.ds(pl.multiple_of(x * width, 128), width)
        theirs = pl.ds(pl.multiple_of((1 - x) * width, 128), width)

        places = ((0, y), (0, 1 - y)) if len(parts) == 2 else ((x, y), (1 - x, y), (x, 1 - y), (1 - x, 1 - y))
        weight_copies = []
        for n, (ref, (xx, yy)) in enumerate(zip(parts, places)):
            cols = pl.ds(pl.multiple_of(yy * width, 128), width)
            for j in range(z_size):
                at = pl.ds(pl.multiple_of((z ^ j) * quarter + xx * piece_rows, piece_rows), piece_rows)
                weight_copies.append(pltpu.make_async_copy(ref.at[j], w.at[:, at, cols], sems_w.at[n, j]))
        token_copies = []
        heads = (pos[0] * half + (z ^ k),) * 2 + (z ^ k,)
        for c in range(chunks):
            source, first = divmod(c * tile, tokens)
            here = pl.ds(c * tile, tile)
            there = pl.ds(first, tile)
            token_copies.append([
                pltpu.make_async_copy(pair[source].at[head, there], buffer.at[here], sems_in.at[n, c])
                for n, (pair, head, buffer) in enumerate(zip(streams, heads, (key, value, rate)))
            ])
        for copy in weight_copies + [copy for group in token_copies for copy in group]:
            copy.start()
        for copy in weight_copies:
            copy.wait()

        def own_copy():
            return pltpu.make_async_copy(w.at[:, :, mine], refs[n_in + 1 + cuts], sems_out.at[3, 0])

        def out_copies(m):
            copies = [pltpu.make_async_copy(total.at[m, :, mine], keep.at[m], sems_out.at[m, cuts])]
            for n in range(cuts):
                cut = pl.ds(n * (rows // cuts), rows // cuts)
                copies.append(pltpu.make_async_copy(rounded.at[m, cut], sends[n].at[m], sems_out.at[m, n]))
            return copies

        if last:
            own_copy().start()

        @pl.loop(0, chunks)
        def _(c):
            here = pl.ds(pl.multiple_of(c * tile, tile), tile)
            for n, (pair, head, buffer) in enumerate(zip(streams, heads, (key, value, rate))):
                pltpu.make_async_copy(pair[0].at[head, pl.ds(0, tile)], buffer.at[here], sems_in.at[n, c]).wait()
            tokens_rate = jnp.concatenate([rate[here, :].astype(F32)] * (columns // lanes), axis=1)
            t = (-tokens_rate * value[here, :].astype(F32)).astype(BF16)
            target[here, :] = t
            gate = jnp.dot(key[here, :], w[0], preferred_element_type=F32)
            up = jnp.dot(key[here, :], w[1], preferred_element_type=F32)
            back = lax.dot_general(t, w[2], (((1,), (1,)), ((), ())), preferred_element_type=F32)
            sig = 0.5 * jnp.tanh(0.5 * gate) + 0.5
            silu = gate * sig
            hidden[here, :] = (silu * up).astype(BF16)
            grads[1, here, :] = (back * silu).astype(BF16)
            grads[0, here, :] = (back * up * (sig + silu * (1.0 - sig))).astype(BF16)

        def product(m, a, b):
            total[m] = lax.dot_general(a, b, (((0,), (0,)), ((), ())), preferred_element_type=F32)
            rounded[m] = total[m, :, theirs].astype(BF16)
            for copy in out_copies(m):
                copy.start()

        @pl.loop(0, 2)
        def _(m):
            product(m, key[...], grads[m])

        if last:
            squares = refs[n_in + 2 + cuts]
            for m in range(3):
                full = w[m].astype(F32)
                squares[m : m + 1, :] = jnp.sum(full * full, axis=0, keepdims=True)
        product(2, hidden[...], target[...])
        for m in range(3):
            for copy in out_copies(m):
                copy.wait()
        if last:
            own_copy().wait()

    outs = [sds((3, rows, width), F32)] + [sds((3, rows // cuts, width), BF16)] * cuts
    out_specs = [anywhere()] * len(outs)
    if last:
        outs += [sds((3, rows, width), BF16), sds((8, columns), F32)]
        out_specs += [anywhere(), whole(outs[-1])]
    operands = (*keys, *values, *rates, *pieces, *after)
    bf16_rows = pltpu.VMEM((2 * tokens, columns), BF16)
    return call(
        body, "gradients", positions, (1,), operands, [anywhere()] * len(operands), outs, out_specs,
        [
            pltpu.VMEM((3, rows, columns), BF16), bf16_rows, bf16_rows, pltpu.VMEM((2 * tokens, lanes), BF16),
            pltpu.VMEM((2, 2 * tokens, columns), BF16), bf16_rows, bf16_rows,
            pltpu.VMEM((3, rows, columns), F32), pltpu.VMEM((3, rows, width), BF16),
            pltpu.SemaphoreType.DMA((len(pieces), z_size)), pltpu.SemaphoreType.DMA((3, chunks)), pltpu.SemaphoreType.DMA((4, cuts + 1)),
        ],
        estimate=pl.CostEstimate(flops=6 * 2 * 2 * tokens * rows * columns, bytes_accessed=14 * 2**20, transcendentals=2 * tokens * columns),
    )


def added(positions, keep, received, after, dtype=BF16, microseconds=1, cuts=1):
    rows = keep.shape[1]
    n = len(received)

    def body(pos, *refs):
        sources, out = refs[: n + 1], refs[n + 1 + len(after)]
        buffers, summed, sems = refs[-n - 3 : -2], refs[-2], refs[-1]
        loads = [[pltpu.make_async_copy(a.at[m], b.at[m], sems.at[m, i]) for i, (a, b) in enumerate(zip(sources, buffers))] for m in range(3)]
        stores = [pltpu.make_async_copy(summed.at[m], out.at[m], sems.at[m, n + 1]) for m in range(3)]
        for copy in loads[0] + loads[1] + loads[2]:
            copy.start()
        for m in range(3):
            for copy in loads[m]:
                copy.wait()
            for c in range(cuts):
                at = pl.ds(c * (rows // cuts), rows // cuts)
                total = buffers[0][m, at, :] + buffers[1 + c][m].astype(F32)
                for ref in buffers[1 + cuts :]:
                    total = total + ref[m, at, :].astype(F32)
                summed[m, at, :] = total.astype(dtype)
            stores[m].start()
        for copy in stores:
            copy.wait()

    operands = (keep, *received, *after)
    shape = sds(keep.shape, dtype)
    return call(
        body, "added", positions, (1,), operands, [anywhere()] * len(operands), shape, anywhere(),
        [pltpu.VMEM(a.shape, a.dtype) for a in (keep, *received, shape)] + [pltpu.SemaphoreType.DMA((3, n + 2))],
        estimate=cost(microseconds),
    )


def total_gradient(positions, keep, received):
    def body(pos, keep_ref, *refs):
        grad, sums = refs[-2:]
        sums[...] = jnp.zeros_like(sums)
        for m in range(3):
            total = keep_ref[m]
            for ref in refs[:-2]:
                total = total + ref[m].astype(F32)
            grad[m] = total
            columns = jnp.sum(total * total, axis=0, keepdims=True)
            sums[m : m + 1, :] = jnp.broadcast_to(jnp.sum(columns, axis=1, keepdims=True), (1, sums.shape[1]))

    outs = [sds(keep.shape, F32), sds((8, 128), F32)]
    operands = (keep, *received)
    return call(body, "total_gradient", positions, (1,), operands, [whole(a) for a in operands], outs, [whole(o) for o in outs])


def renewed_block(positions, grad, own_w, squares, sums, sums_in):
    width = grad.shape[2]

    def body(pos, g_ref, w_ref, sq_ref, sums_ref, sums_in_ref, out):
        mine = pl.ds(pl.multiple_of(pos[2] * width, 128), width)
        for m in range(3):
            total_g = sums_ref[m : m + 1, :1] + sums_in_ref[m : m + 1, :1]
            total_w = jnp.sum(sq_ref[m : m + 1, :], axis=1, keepdims=True)
            scale = STEP_SIZE * jnp.sqrt(total_w + EPSILON) / jnp.sqrt(total_g + EPSILON)
            moved = w_ref[m].astype(F32) - scale * g_ref[m]
            col_moved = jnp.sum(moved * moved, axis=0, keepdims=True)
            out[m] = (moved * jnp.sqrt((sq_ref[m : m + 1, mine] + EPSILON) / (col_moved + EPSILON))).astype(BF16)

    operands = (grad, own_w, squares, sums, sums_in)
    shape = sds(grad.shape, BF16)
    return call(body, "renewed_block", positions, (1,), operands, [whole(a) for a in operands], shape, whole(shape))


def apply_renewed(positions, queries, queries_in, held, swapped, k, half, out, late, after):
    _, rows, width = held.shape
    columns = 2 * width
    heads, tokens, _ = queries.shape
    tile = tokens // 2 if tokens % 32 == 0 else tokens
    chunks = 2 * tokens // tile
    blocks = [b for _, b in late]
    n_in = 4 + len(blocks) + len(after) + (0 if out is None else 1)

    def body(pos, q0, q1, held_ref, swapped_ref, *refs):
        late_refs = refs[: len(blocks)]
        out_ref, send_ref, w, query, result, brought, sems_in, sems_q, sems_out, sems_late = refs[n_in - 4 :]
        x = pos[2]
        heads_of = (pos[0] * half + (pos[1] ^ k), pos[1] ^ k)
        weights = [
            pltpu.make_async_copy(ref, w.at[:, :, pl.ds(pl.multiple_of(xx * width, 128), width)], sems_in.at[n])
            for n, (ref, xx) in enumerate(((held_ref, x), (swapped_ref, 1 - x)))
        ]
        loads, stores = [], []
        for c in range(chunks):
            source, first = divmod(c * tile, tokens)
            here, there = pl.ds(c * tile, tile), pl.ds(first, tile)
            loads.append(pltpu.make_async_copy((q0, q1)[source].at[heads_of[source], there], query.at[here], sems_q.at[c]))
            to = send_ref.at[there] if source else out_ref.at[heads_of[0], there]
            stores.append(pltpu.make_async_copy(result.at[here], to, sems_out.at[c]))
        late_in = [pltpu.make_async_copy(ref, brought.at[n], sems_late.at[n, 0]) for n, ref in enumerate(late_refs)]
        late_out = [
            pltpu.make_async_copy(brought.at[n], out_ref.at[(1 - pos[0]) * half + (pos[1] ^ late[n][0])], sems_late.at[n, 1])
            for n in range(len(blocks))
        ]
        for copy in weights + loads + late_in:
            copy.start()
        for copy in weights:
            copy.wait()

        for copy in loads:
            copy.wait()

        def front(c):
            q = query[c * tile : (c + 1) * tile, :]
            return jnp.dot(q, w[0], preferred_element_type=F32), jnp.dot(q, w[1], preferred_element_type=F32)

        following = front(0)
        for c in range(chunks):
            gate, up = following
            if c + 1 < chunks:
                following = front(c + 1)
            hidden = (gate * (0.5 * jnp.tanh(0.5 * gate) + 0.5) * up).astype(BF16)
            result[c * tile : (c + 1) * tile, :] = jnp.dot(hidden, w[2], preferred_element_type=F32).astype(BF16)
            stores[c].start()
            if c == 0:
                for n in range(len(blocks)):
                    late_in[n].wait()
                    late_out[n].start()
        for copy in stores + late_out:
            copy.wait()

    operands = [queries, queries_in, held, swapped, *blocks, *after]
    aliases = {}
    if out is not None:
        aliases = {1 + len(operands): 0}
        operands.append(out)
    return call(
        body, "apply_renewed", positions, (1,), operands, [anywhere()] * len(operands),
        [sds(queries.shape, BF16), sds((tokens, columns), BF16)], [anywhere()] * 2,
        [
            pltpu.VMEM((3, rows, columns), BF16), pltpu.VMEM((2 * tokens, columns), BF16), pltpu.VMEM((2 * tokens, columns), BF16),
            pltpu.VMEM((max(len(blocks), 1), tokens, columns), BF16),
            pltpu.SemaphoreType.DMA((2,)), pltpu.SemaphoreType.DMA((chunks,)), pltpu.SemaphoreType.DMA((chunks,)),
            pltpu.SemaphoreType.DMA((max(len(blocks), 1), 2)),
        ],
        aliases,
        pl.CostEstimate(flops=3 * 2 * 2 * tokens * rows * columns, bytes_accessed=7 * 2**20, transcendentals=2 * tokens * columns),
    )


def place(positions, out, late, half):
    n = len(late)
    tokens, columns = late[0][1].shape
    cuts = 4 if tokens % 64 == 0 else 1
    tile = tokens // cuts

    def body(pos, *refs):
        out_ref, held, sems_in, sems_out = refs[-4:]
        pairs = []
        for i, (k, _) in enumerate(late):
            head = (1 - pos[0]) * half + (pos[1] ^ k)
            for c in range(cuts):
                at = pl.ds(c * tile, tile)
                pairs.append((
                    pltpu.make_async_copy(refs[i].at[at], held.at[i, at], sems_in.at[i, c]),
                    pltpu.make_async_copy(held.at[i, at], out_ref.at[head, at], sems_out.at[i, c]),
                ))
        for first, _ in pairs:
            first.start()
        for first, second in pairs:
            first.wait()
            second.start()
        for _, second in pairs:
            second.wait()

    return call(
        body, "place", positions, (1,), (*(b for _, b in late), out), [anywhere()] * (n + 1),
        sds(out.shape, BF16), anywhere(),
        [pltpu.VMEM((n, tokens, columns), BF16), pltpu.SemaphoreType.DMA((n, cuts)), pltpu.SemaphoreType.DMA((n, cuts))],
        {1 + n: 0}, cost(1),
    )


def on_device_fast(queries, keys, values, lr_codes, fast_gate, fast_up, fast_down):
    heads, tokens, _ = queries.shape
    half = heads // 2
    core, seq = lax.axis_index("sub"), lax.axis_index("seq")
    positions = jnp.stack([core, seq // 2, seq % 2, lax.axis_index("groups")]).astype(jnp.int32)
    flip = [(0, 1), (1, 0)]

    def over_sub(a):
        return lax.ppermute(a, "sub", flip)

    def over_groups(a):
        return lax.ppermute(a, "groups", flip)

    def over_x(a):
        return lax.ppermute(a, "seq", [(i, i ^ 1) for i in range(8)])

    def over_z(a, j):
        return lax.ppermute(a, "seq", [(i, i ^ (2 * j)) for i in range(8)])

    weights = (fast_gate, fast_up, fast_down)
    rows_in = tuple(over_sub(w) for w in weights)
    all_keys, all_values = (keys, over_sub(keys)), (values, over_sub(values))
    codes = (lr_codes, over_sub(lr_codes))

    def head_gradients(k, pieces, after):
        keep, send, *rest = gradients(positions, all_keys, all_values, rates, pieces, k, half, after, 1)
        return keep, over_x(send), *rest

    def turn(pieces, k, after, handed=None):
        arrived = (pieces[0], *(over_z(a, j) for j, a in enumerate(pieces[1:], 1)))
        return next_pieces(positions, arrived, rows, k, after, handed)

    everything, *pieces = first_pieces(positions, weights, rows_in, 3, ())
    rows = (everything, over_x(everything))
    held, *pieces = turn(pieces, 2, ())
    swapped = over_x(held)
    pieces3 = (held, swapped, over_groups(held), over_groups(swapped))
    rates = token_rates(positions, codes, half, (held,))
    queries_in = over_sub(other_half(positions, queries, half, (held,)))
    held, *pieces = turn(pieces, 1, (*pieces3, *rates))
    pieces2 = (held, over_groups(held))
    keep3, *sends = gradients(positions, all_keys, all_values, rates, pieces3, 3, half, (held,), 4)
    held, *pieces = turn(pieces, 0, (keep3, pieces2[1]))
    pieces1 = (held, over_groups(held))
    keep2, send2 = gradients(positions, all_keys, all_values, rates, pieces2, 2, half, (held,), 1)
    in3 = [over_x(a) for a in sends]
    sum3 = added(positions, keep3, in3, (keep2,), cuts=4)
    from1 = over_z(sum3, 1)
    (held,) = turn(pieces, None, (sum3, pieces1[1]))
    pieces0 = (held, over_groups(held))
    keep1, send1 = gradients(positions, all_keys, all_values, rates, pieces1, 1, half, (held,), 1)
    in2 = over_x(send2)
    sum2 = added(positions, keep2, (in2, from1), (keep1,))
    from2 = over_z(sum2, 2)
    keep0, in0, own_w, squares = head_gradients(0, pieces0, (sum2,))
    in1 = over_x(send1)
    sum1 = added(positions, keep1, (in1,), (keep0,))
    from1 = over_z(sum1, 1)
    partial = added(positions, keep0, (from2,), (sum1,), F32, 8)
    grad, sums = total_gradient(positions, partial, (in0, from1))
    renewed = renewed_block(positions, grad, own_w, squares, sums, over_x(sums))

    swapped = over_x(renewed)
    from1, from2 = over_z(renewed, 1), over_z(renewed, 2)
    from3 = over_z(from2, 1)
    matrices = {0: (renewed, swapped), 2: (from2, over_x(from2)), 3: (from3, over_x(from3))}

    def head_output(k, out, late, after):
        out, sent = apply_renewed(positions, queries, queries_in, *matrices[k], k, half, out, late, after)
        return out, (k, over_sub(sent))

    out, late0 = head_output(0, None, (), (from1, from2))
    swapped_late, _ = handed_on(positions, swapped, (from3, out))
    matrices[1] = (from1, over_z(swapped_late, 1))
    out, late2 = head_output(2, out, (), (swapped_late,))
    out, late1 = head_output(1, out, (late0,), matrices[3])
    out, late3 = head_output(3, out, (late2,), ())
    out = place(positions, out, (late1,), half)
    return place(positions, out, (late3,), half)


def solution(mesh):
    seq, sub, groups = mesh.shape["seq"], mesh.shape["sub"], mesh.shape["groups"]

    def on_device(queries, *rest):
        rows, columns = rest[3].shape[1:]
        fits = (groups, seq, sub, queries.shape[0]) == (2, 8, 2, 8) and rows % 32 == 0 and columns == seq * sub * rows and columns % 256 == 0
        return (on_device_fast if fits else on_device_generic)(queries, *rest)

    return jax.shard_map(
        on_device,
        mesh=mesh,
        in_specs=(
            P("head", ("groups", "seq", "sub"), None),
            P("head", ("groups", "seq", "sub"), None),
            P("head", ("groups", "seq", "sub"), None),
            P("head", ("groups", "seq", "sub")),
            P("head", ("seq", "sub"), None),
            P("head", ("seq", "sub"), None),
            P("head", ("seq", "sub"), None),
        ),
        out_specs=P("head", ("groups", "seq", "sub"), None),
        check_vma=False,
    )
```
